128 devices in a mesh: dp: 32 (over y, x, z_hi), mp: 4 (over z_lo, core).
Axes of the slice: x: 4, y: 4, z: 4 (z_hi: 2, z_lo: 2; z = z_hi * 2 + z_lo), core: 2. Of those that a mesh axis runs over, the one named last changes fastest.
Arguments:
- layer_in: bfloat16 [32, 512, 1024], P('dp', 'mp'), may hold values from -6 to 6
- memory: bfloat16 [32, 512, 1024], P('dp', 'mp'), may hold values from -6 to 6
- squeezed_mem: bfloat16 [32, 512, 1024], P('dp', 'mp'), may hold values from -6 to 6
- memory_fill: int32 [32], P('dp'), may hold values from 16 to 512, as said below
- squeezed_fill: int32 [32], P('dp'), may hold values from 0 to 512, as said below
- grad_out: bfloat16 [32, 512, 1024], P('dp', 'mp'), may hold values from -6 to 6
- attn_gain: float32 [1024], replicated, may hold values from 0.5 to 1.5
- w_query: bfloat16 [1024, 1024], replicated, may hold values from -0.1875 to 0.1875
- w_keyval: bfloat16 [1024, 2048], replicated, may hold values from -0.1875 to 0.1875
- w_output: bfloat16 [1024, 1024], replicated, may hold values from -0.75 to 0.75
- slopes: float32 [8], replicated, may hold values from 0.0005 to 0.05
- ffn_gain: float32 [1024], replicated, may hold values from 0.5 to 1.5
- w_up: bfloat16 [1024, 4096], P(None, 'mp'), may hold values from -0.1875 to 0.1875
- up_bias: float32 [4096], P('mp'), may hold values from -3 to 3
- w_down: bfloat16 [4096, 1024], P('mp'), may hold values from -0.09375 to 0.09375
- w_squeeze: bfloat16 [3072, 1024], replicated, may hold values from -0.109375 to 0.109375
Outputs:
- layer_out: bfloat16 [32, 512, 1024], P('dp', 'mp')
- new_squeezed: bfloat16 [32, 172, 1024], P('dp', 'mp')
- grad_in: float32 [32, 512, 1024], P('dp', 'mp')
- grad_attn_gain: float32 [1024], replicated
- grad_query: float32 [1024, 1024], P('mp')
- grad_keyval: float32 [1024, 2048], P('mp')
- grad_output: float32 [1024, 1024], P('mp')
- grad_slopes: float32 [8], replicated
- grad_ffn_gain: float32 [1024], replicated
- grad_up: float32 [1024, 4096], P(None, 'mp')
- grad_up_bias: float32 [4096], P('mp')
- grad_down: float32 [4096, 1024], P('mp')
- grad_squeeze: float32 [3072, 1024], P('mp')
The draws below stay inside these ranges and needn't reach their ends.
Inputs may be any that keep to these rules, and one draw needn't show every extreme that they name: A stream's valid memory slots are its last memory_fill ones. In every draw some stream has all 512 valid. A stream's valid compressed slots are its last squeezed_fill ones; it has any only where its memory_fill is 512. In every draw some stream has all 512 valid.
All inputs are finite; a program needn't handle non-finite values.
Results may differ from the reference program's by a relative error of at most 0.028.
Values may be sent and summed in bfloat16 or wider, within the bound.
A program may use at most 192 MiB of HBM per device.

```python
import math
import jax
import jax.numpy as jnp
from jax import lax

D = 1024
H = 8
DH = 128
FF = 4096
S = 512
M = 512
C = 512
STREAMS = 32
CN = 172


def draw_fills(key):
    keys = jax.random.split(key, 4)
    order = jnp.arange(STREAMS)
    chosen = jax.random.randint(keys[0], (), 0, STREAMS)
    is_long = (jax.random.randint(keys[1], (STREAMS,), 0, 4) == 0) | (order == chosen)
    short_fill = jax.random.randint(keys[2], (STREAMS,), M // 32, M // 2 + 1)
    mem_fill = jnp.where(is_long, M, short_fill).astype(jnp.int32)
    some_fill = jax.random.randint(keys[3], (STREAMS,), 1, C + 1)
    sq_fill = jnp.where(is_long, jnp.where(order == chosen, C, some_fill), 0).astype(jnp.int32)
    return (mem_fill, sq_fill)


def draw_memory_fill(key, part):
    shared = draw_fills(key)
    return shared[0]


def draw_squeezed_fill(key, part):
    shared = draw_fills(key)
    return shared[1]


def block_scale(own_key, shape, pieces, low, high):
    loudness, own = 1.0, jax.random.fold_in(own_key, 6)
    for dim, parts in pieces:
        heights = jnp.exp(jax.random.uniform(jax.random.fold_in(own, dim), (parts,), jnp.float32, low / len(pieces), high / len(pieces)))
        loudness = loudness * jnp.repeat(heights, shape[dim] // parts).reshape([-1 if axis == dim else 1 for axis in range(len(shape))])
    return loudness


def bell_draw(stream_key, shape, scale, limit, pieces=(), held_as=jnp.bfloat16):
    values = jax.random.normal(stream_key, shape, jnp.float32) * scale
    if len(pieces) > 0:
        values = block_scale(stream_key, shape, pieces, -0.22, 0.18) * values
    return jnp.clip(values, min=-limit, max=limit).astype(held_as)


def setup_inputs(seed: int = 0) -> dict:
    key_of = jax.random.split(jax.random.key(seed), 17)
    layer_in = bell_draw(key_of[0], (STREAMS, S, D), 1.0, 6.0, ((0, 32), (1, 4)))
    memory = bell_draw(key_of[1], (STREAMS, M, D), 1.0, 6.0, ((0, 32), (1, 4)))
    squeezed_mem = bell_draw(key_of[2], (STREAMS, C, D), 1.0, 6.0, ((0, 32), (1, 4)))
    memory_fill = draw_memory_fill(jax.random.fold_in(key_of[16], 71), 0)
    squeezed_fill = draw_squeezed_fill(jax.random.fold_in(key_of[16], 71), 0)
    grad_out = bell_draw(key_of[5], (STREAMS, S, D), 1.0, 6.0, ((0, 32), (1, 4)))
    attn_gain = jnp.clip(1.0 + 0.1 * jax.random.normal(key_of[6], (D,), jnp.float32), 0.5, 1.5)
    w_query = bell_draw(key_of[7], (D, D), D ** -0.5, 0.1875)
    w_keyval = bell_draw(key_of[8], (D, 2 * D), D ** -0.5, 0.1875)
    w_output = bell_draw(key_of[9], (D, D), (D // 16) ** -0.5, 0.75)
    slopes = jnp.clip(jnp.exp(jax.random.uniform(key_of[10], (H,), jnp.float32, math.log(0.0005), math.log(0.05))), 0.0005, 0.05)
    ffn_gain = jnp.clip(1.0 + 0.1 * jax.random.normal(key_of[11], (D,), jnp.float32), 0.5, 1.5)
    w_up = bell_draw(key_of[12], (D, FF), D ** -0.5, 0.1875, ((1, 4),))
    up_bias = bell_draw(key_of[13], (FF,), 0.5, 3.0, ((0, 4),), jnp.float32)
    w_down = bell_draw(key_of[14], (FF, D), FF ** -0.5, 0.09375, ((0, 4),))
    w_squeeze = bell_draw(key_of[15], (3 * D, D), (3 * D) ** -0.5, 0.109375)
    return dict(layer_in=layer_in, memory=memory, squeezed_mem=squeezed_mem, memory_fill=memory_fill, squeezed_fill=squeezed_fill, grad_out=grad_out, attn_gain=attn_gain, w_query=w_query, w_keyval=w_keyval, w_output=w_output, slopes=slopes, ffn_gain=ffn_gain, w_up=w_up, up_bias=up_bias, w_down=w_down, w_squeeze=w_squeeze)


@jax.custom_vjp
def low(v):
    return lax.optimization_barrier(v.astype(jnp.bfloat16)).astype(jnp.float32)

@jax.custom_vjp
def low_back(v):
    return v

def low_keep(v):
    return (low(v), None)

def low_pass(kept, grad):
    return (grad,)

def back_keep(v):
    return (v, None)

def back_low(kept, grad):
    return (low(grad),)
low.defvjp(low_keep, low_pass)
low_back.defvjp(back_keep, back_low)
EPS = 1e-05
NEG = -1e+30
HIGH = lax.Precision.HIGHEST

def matmul(left, right):
    return jnp.dot(left, right, precision=HIGH)

def layer_norm(rows, gain):
    centre = rows - lax.optimization_barrier(jnp.mean(rows, axis=-1, keepdims=True))
    spread = lax.optimization_barrier(jnp.mean(centre * centre, axis=-1, keepdims=True))
    return centre * lax.rsqrt(spread + EPS) * gain

def masked_softmax(scores, valid):
    scores = jnp.where(valid, scores, NEG)
    top = lax.optimization_barrier(jnp.max(scores, axis=-1, keepdims=True))
    weights = jnp.exp(scores - top)
    return weights / lax.optimization_barrier(jnp.sum(weights, axis=-1, keepdims=True))

def attend(query, keyval, bias, valid):
    rows = query.shape[0]
    count = keyval.shape[0]
    heads_q = query.reshape(rows, H, DH)
    keys = keyval[:, :D].reshape(count, H, DH)
    values = keyval[:, D:].reshape(count, H, DH)
    raw = jnp.einsum('ihd,jhd->hij', heads_q, keys, precision=HIGH) * DH ** (-0.5) + bias
    probs = low(masked_softmax(low_back(raw), valid))
    mixed = jnp.einsum('hij,jhd->ihd', probs, values, precision=HIGH).reshape(rows, D)
    return low_back(mixed)

def stream(params, frozen, seg_rows, fixed_rows, mem, old, mfill, sfill):
    g_attn, wq, wkv, wo, slopes, g_ffn, w_up, b_up, w_down, w_sq = params
    fg_attn, fwq, fwkv = frozen
    context = jnp.concatenate([old, mem, seg_rows], 0)
    normed = low(layer_norm(context, g_attn))
    query = low(low_back(matmul(normed[C + M:], wq)))
    keyval = low(low_back(matmul(normed, wkv)))
    rows = jnp.arange(S)[:, None]
    cols = jnp.arange(C + M + S)[None, :]
    distance = (C + M + rows - cols).astype(jnp.float32)
    valid = (cols < C) & (cols >= C - sfill) | (cols >= C) & (cols < C + M) & (cols >= C + M - mfill) | (cols >= C + M) & (cols <= C + M + rows)
    bias = -slopes[:, None, None] * distance[None]
    mixed = low(attend(query, keyval, bias, valid))
    branch = low_back(matmul(mixed, wo))
    mid = seg_rows + branch
    normed_mid = low(layer_norm(mid, g_ffn))
    pre = low_back(matmul(normed_mid, w_up) + b_up)
    hidden = low(jax.nn.gelu(pre))
    out_rows = mid + low_back(matmul(hidden, w_down))
    fquery = low(matmul(low(layer_norm(fixed_rows, fg_attn)), fwq))
    fkeyval = low(matmul(low(layer_norm(mem, fg_attn)), fwkv))
    padded = jnp.concatenate([mem, jnp.zeros((3 * CN - M, D), jnp.float32)], 0)
    windows = padded.reshape(CN, 3 * D)
    squeezed = low_back(matmul(windows, w_sq))
    sq_keyval = low(low_back(matmul(low(layer_norm(squeezed, fg_attn)), fwkv)))
    mem_valid = jnp.broadcast_to(jnp.arange(M)[None, :] >= M - mfill, (S, M))
    slot = jnp.arange(CN)[None, :]
    sq_valid = jnp.broadcast_to((3 * slot < M) & (3 * slot + 2 >= M - mfill), (S, CN))
    first = attend(fquery, fkeyval, 0.0, mem_valid)
    second = attend(fquery, sq_keyval, 0.0, sq_valid)
    diff = first - second
    loss = jnp.sum(diff * diff) / (S * D)
    return (out_rows, squeezed, loss)

def reference(layer_in, memory, squeezed_mem, memory_fill, squeezed_fill, grad_out, attn_gain, w_query, w_keyval, w_output, slopes, ffn_gain, w_up, up_bias, w_down, w_squeeze):
    group = math.gcd(STREAMS, 8)
    blocks = STREAMS // group

    def shaped(array):
        return array.astype(jnp.float32).reshape((blocks, group) + array.shape[1:])
    inputs = shaped(layer_in)
    mems = shaped(memory)
    olds = shaped(squeezed_mem)
    mfills = memory_fill.reshape(blocks, group)
    sfills = squeezed_fill.reshape(blocks, group)
    params = tuple((item.astype(jnp.float32) for item in (attn_gain, w_query, w_keyval, w_output, slopes, ffn_gain, w_up, up_bias, w_down, w_squeeze)))
    frozen = params[:3]

    def forward(seg_inputs, weights):

        def one_group(item):
            seg_rows, fixed_rows, mem, old, mfill, sfill = item
            return jax.vmap(stream, in_axes=(None, None, 0, 0, 0, 0, 0, 0))(weights, frozen, seg_rows, fixed_rows, mem, old, mfill, sfill)
        return lax.map(jax.checkpoint(one_group), (seg_inputs, inputs, mems, olds, mfills, sfills))
    outs, pullback = jax.vjp(forward, inputs, params)
    out_rows, squeezed, losses = outs
    cotangent = (shaped(grad_out), jnp.zeros_like(squeezed), jnp.ones_like(losses))
    grad_inputs, grads = pullback(cotangent)
    return (out_rows.reshape(STREAMS, S, D).astype(jnp.bfloat16), squeezed.reshape(STREAMS, CN, D).astype(jnp.bfloat16), grad_inputs.reshape(STREAMS, S, D), grads[0], grads[1], grads[2], grads[3], grads[4], grads[5], grads[6], grads[7], grads[8], grads[9])
```

```python
import functools

import jax
import jax.numpy as jnp
from jax import lax
from jax.experimental import pallas as pl
from jax.experimental.pallas import tpu as pltpu
from jax.sharding import PartitionSpec as P

D = 1024
H = 8
DH = 128
S = 512
M = 512
C = 512
CN = 172
CP = 192
EPS = 1e-05
NEG = -1e30
MESH = pl.DeviceIdType.MESH
BF = jnp.bfloat16
F32 = jnp.float32
VMEM = pl.BlockSpec(memory_space=pltpu.VMEM)


def dp_places():
    dp = lax.axis_index("dp")
    y, x, z = dp // 8, (dp // 2) % 4, dp % 2
    xa, xb = x + 1 - 2 * (x % 2), 3 - x
    ya, yb = y + 1 - 2 * (y % 2), 3 - y
    cube = [
        ((x + x // 2) % 2, y * 8 + xa * 2 + z),
        ((y + y // 2) % 2, ya * 8 + x * 2 + z),
        (x // 2, y * 8 + xb * 2 + z),
        (y // 2, yb * 8 + x * 2 + z),
    ]
    return cube, y * 8 + x * 2 + (1 - z)


def mp_places():
    mp = lax.axis_index("mp")
    zl, core = mp // 2, mp % 2
    return mp, zl, core, zl * 2 + (1 - core), (1 - zl) * 2 + core


def to_mp(src, dst, ssem, rsem, k, peer):
    return pltpu.make_async_remote_copy(
        src_ref=src, dst_ref=dst, send_sem=ssem.at[k], recv_sem=rsem.at[k],
        device_id=(lax.axis_index("dp"), peer), device_id_type=MESH,
    )


def to_dp(src, dst, ssem, rsem, k, peer):
    return pltpu.make_async_remote_copy(
        src_ref=src, dst_ref=dst, send_sem=ssem.at[k], recv_sem=rsem.at[k],
        device_id=(peer, lax.axis_index("mp")), device_id_type=MESH,
    )


def barrier(dps, mps):
    sem = pltpu.get_barrier_semaphore()
    for peer in dps:
        pl.semaphore_signal(sem, inc=1, device_id=(peer, lax.axis_index("mp")), device_id_type=MESH)
    for peer in mps:
        pl.semaphore_signal(sem, inc=1, device_id=(lax.axis_index("dp"), peer), device_id_type=MESH)
    pl.semaphore_wait(sem, len(dps) + len(mps))


def call(body, outs, args, sems, scratch, cid, aliases={}):
    return pl.pallas_call(
        body,
        out_shape=outs,
        in_specs=[VMEM] * len(args),
        out_specs=jax.tree.map(lambda _: VMEM, outs),
        scratch_shapes=list(scratch) + [pltpu.SemaphoreType.DMA((sems,)), pltpu.SemaphoreType.DMA((sems,))],
        input_output_aliases=aliases,
        compiler_params=pltpu.CompilerParams(
            collective_id=cid, has_side_effects=True, vmem_limit_bytes=52 << 20
        ),
    )(*args)


def rows_loop(total, step, body):
    def run(i, carry):
        body(pl.multiple_of(i * step, step))
        return carry

    lax.fori_loop(0, total // step, run, 0)


def gather_body(x_ref, o_ref, ssem, rsem):
    mp, zl, core, part, far = mp_places()
    barrier([], [part, far])
    a = to_mp(x_ref, o_ref.at[mp], ssem, rsem, 0, far)
    a.start()
    b = to_mp(x_ref, o_ref.at[mp], ssem, rsem, 1, part)
    b.start()
    o_ref[mp] = x_ref[...]
    a.wait_recv()
    c = to_mp(o_ref.at[far], o_ref.at[far], ssem, rsem, 2, part)
    c.start()
    b.wait()
    a.wait_send()
    c.wait()


def gather_mp(x, cid):
    return call(gather_body, jax.ShapeDtypeStruct((4,) + x.shape, x.dtype), (x,), 3, [], cid)


def sums_body(gnm, down, gnm_sum, down_sum, out, got, out2, got2, ssem, rsem):
    mp, zl, core, part, far = mp_places()
    barrier([], [part, far])
    for z in range(2):
        out[0, z] = gnm[2 * z + 1 - core].astype(BF)
    a = to_mp(out.at[0], got.at[0], ssem, rsem, 0, part)
    a.start()
    for z in range(2):
        out[1, z] = down[2 * z + 1 - core].astype(BF)
    b = to_mp(out.at[1], got.at[1], ssem, rsem, 1, part)
    b.start()
    a.wait()
    for z in range(2):
        out2[z] = (gnm[2 * z + core] + got[0, z].astype(F32)).astype(BF)
    a = to_mp(out2.at[pl.ds(0, 2)], got2.at[pl.ds(0, 2)], ssem, rsem, 2, far)
    a.start()
    b.wait()
    out2[2] = (down[(1 - zl) * 2 + core] + got[1, 1 - zl].astype(F32)).astype(BF)
    b = to_mp(out2.at[2], got2.at[2], ssem, rsem, 3, far)
    b.start()
    mine = down[zl * 2 + core] + got[1, zl].astype(F32)
    a.wait()
    for z in range(2):
        gnm_sum[z] = out2[z].astype(F32) + got2[z].astype(F32)
    b.wait()
    down_sum[...] = mine + got2[2].astype(F32)


def sums_mp(gnm, down, cid):
    buf = pltpu.VMEM((2, 2, 128, D), BF)
    buf2 = pltpu.VMEM((3, 128, D), BF)
    return call(
        sums_body,
        (jax.ShapeDtypeStruct((2, 128, D), F32), jax.ShapeDtypeStruct((128, D), F32)),
        (gnm.reshape(4, 128, D), down.reshape(4, 128, D)), 4, [buf, buf, buf2, buf2], cid,
    )


def pair_body(x_ref, o_ref, ssem, rsem):
    mp, zl, core, part, far = mp_places()
    barrier([], [part])
    copies = []
    for z in range(2):
        copies.append(to_mp(x_ref.at[z], o_ref.at[z, core], ssem, rsem, z, part))
        copies[-1].start()
    for z in range(2):
        o_ref[z, core] = x_ref[z]
    for c in copies:
        c.wait()


def pair_gather(x, cid):
    return call(pair_body, jax.ShapeDtypeStruct((2, 2) + x.shape[1:], x.dtype), (x,), 2, [], cid)


def tail_body(seg, sq, seg_sum, sq_sum, out, got, out2, got2, sout, sgot, sout2, sgot2, ssem, rsem):
    mp, zl, core, part, far = mp_places()
    barrier([], [part, far])
    sout[...] = sq[1 - core].astype(BF)
    a = to_mp(sout, sgot, ssem, rsem, 0, part)
    a.start()
    for z in range(2):
        out[z] = seg[2 * z + 1 - core].astype(BF)
    b = to_mp(out, got, ssem, rsem, 1, part)
    b.start()
    a.wait()
    sout2[...] = (sq[core] + sgot[...].astype(F32)).astype(BF)
    a = to_mp(sout2, sgot2, ssem, rsem, 2, far)
    a.start()
    b.wait()
    out2[...] = (seg[(1 - zl) * 2 + core] + got[1 - zl].astype(F32)).astype(BF)
    b = to_mp(out2, got2, ssem, rsem, 3, far)
    b.start()
    mine = seg[zl * 2 + core] + got[zl].astype(F32)
    a.wait()
    sq_sum[core] = (sout2[...].astype(F32) + sgot2[...].astype(F32)).astype(BF)
    a = to_mp(sq_sum.at[core], sq_sum.at[core], ssem, rsem, 4, part)
    a.start()
    b.wait()
    seg_sum[...] = mine + got2[...].astype(F32)
    a.wait()


def tail_mp(seg, sq, cid):
    buf, one = pltpu.VMEM((2, 128, D), BF), pltpu.VMEM((128, D), BF)
    half = pltpu.VMEM((96, D), BF)
    return call(
        tail_body,
        (jax.ShapeDtypeStruct((128, D), F32), jax.ShapeDtypeStruct((2, 96, D), BF)),
        (seg.reshape(4, 128, D), sq.reshape(2, 96, D)), 5, [buf, buf, one, one, half, half, half, half], cid,
    )


ROWS = 3072
CHUNKS = ((0, 1024), (1024, 1024), (2048, 768), (2816, 256))
STRIPS = 6


def add_into(dst, dst_at, src, src_at, rows):
    step = 64 if rows % 64 == 0 else 16

    def body(i, carry):
        to = dst_at(pl.multiple_of(i * step, 16), step)
        at = src_at(pl.multiple_of(i * step, 16), step)
        dst[to] = (dst[to].astype(F32) + src[at].astype(F32)).astype(BF)
        return carry

    lax.fori_loop(0, rows // step, body, 0)


def reduce_body(x_ref, t_ref, s_ref, o_ref, ot_ref, os_ref, recv, trecv, tpack, tgot, srecv, free, ssem, rsem):
    cube, zp = dp_places()
    mp, zl, core, part, far = mp_places()
    diag = 3 - mp
    others = (part, far, diag)
    barrier([peer for _, peer in cube] + [zp], others)
    o_ref[...] = x_ref[...]
    ot_ref[...] = t_ref[...]
    os_ref[...] = s_ref[...]
    count = [0]

    def sem():
        count[0] += 1
        return count[0] - 1

    pending = []

    def go(cp):
        cp.start()
        pending.append(cp)
        return cp

    places = [(r0, n, [r0] * 4, [[] for _ in range(4)]) for r0, n in CHUNKS]
    tcur, told = [0] * 4, [[] for _ in range(4)]
    small_steps = [peer for _, peer in cube] + [zp]

    for s in range(10):
        waits = []
        if s == 4:
            for cp in pending:
                cp.wait_send()
            pending.clear()
            for _, peer in cube:
                pl.semaphore_signal(free, inc=1, device_id=(peer, mp), device_id_type=MESH)
        if s == 5:
            pl.semaphore_wait(free, 4)
        if s < 7:
            k = sem()
            rows = pl.ds(0, 16) if s < 5 else pl.ds(0, 8)
            if s < 5:
                cp = go(to_dp(os_ref.at[rows], srecv.at[s, rows], ssem, rsem, k, small_steps[s]))
            else:
                cp = go(to_mp(os_ref.at[rows], srecv.at[s, rows], ssem, rsem, k, (part, far)[s - 5]))
            waits.append(("small", cp, s, rows))
        if s < 4:
            half = 256 >> (s + 1)
            for j in range(STRIPS):
                q = j % 4
                bit, peer = cube[(q + s) % 4]
                cols = pl.ds(128 * j, 128)
                keep = pl.multiple_of(tcur[q] + bit * half, 16)
                give = pl.multiple_of(tcur[q] + (1 - bit) * half, 16)
                at = 256 - (256 >> s)
                cp = go(to_dp(ot_ref.at[:, pl.ds(give, half), cols], trecv.at[:, pl.ds(at, half), cols], ssem, rsem, sem(), peer))
                waits.append(("strip", cp, j, keep, at, half))
            for q in range(4):
                bit, peer = cube[(q + s) % 4]
                told[q].append(tcur[q])
                tcur[q] = pl.multiple_of(tcur[q] + bit * half, 16)
        elif s == 4:
            for j in range(STRIPS):
                cols = pl.ds(128 * j, 128)
                cp = go(to_dp(ot_ref.at[:, pl.ds(tcur[j % 4], 16), cols], trecv.at[:, pl.ds(240, 16), cols], ssem, rsem, sem(), zp))
                waits.append(("strip", cp, j, tcur[j % 4], 240, 16))
        elif s == 5:
            for j in range(STRIPS):
                cols = pl.ds(128 * j, 128)
                tpack[:, j] = ot_ref[:, pl.ds(tcur[j % 4], 16), cols]
            for peer in others:
                cp = go(to_mp(tpack.at[peer], tgot.at[mp], ssem, rsem, sem(), peer))
                waits.append(("swap", cp))
        else:
            k = 9 - s
            half = 256 >> (k + 1)
            for j in range(STRIPS):
                q = j % 4
                bit, peer = cube[(q + k) % 4]
                cols = pl.ds(128 * j, 128)
                here = ot_ref.at[:, pl.ds(tcur[q], half), cols]
                waits.append(("got", go(to_dp(here, here, ssem, rsem, sem(), peer))))
            for q in range(4):
                tcur[q] = told[q][k]
        for r0, n, cur, old in places:
            if s == 9:
                continue
            for q in range(4):
                cols = pl.ds(256 * q, 256)
                if s < 4:
                    bit, peer = cube[(q + s) % 4]
                    half = n >> (s + 1)
                    keep = pl.multiple_of(cur[q] + bit * half, 16)
                    give = pl.multiple_of(cur[q] + (1 - bit) * half, 16)
                    at = r0 + n - (n >> s)
                    cp = go(to_dp(o_ref.at[pl.ds(give, half), cols], recv.at[pl.ds(at, half), cols], ssem, rsem, sem(), peer))
                    waits.append(("quarter", cp, keep, at, half, cols))
                    old[q].append(cur[q])
                    cur[q] = keep
                elif s == 4:
                    size = n >> 4
                    at = r0 + n - size
                    cp = go(to_dp(o_ref.at[pl.ds(cur[q], size), cols], recv.at[pl.ds(at, size), cols], ssem, rsem, sem(), zp))
                    waits.append(("quarter", cp, cur[q], at, size, cols))
                else:
                    k = 8 - s
                    bit, peer = cube[(q + k) % 4]
                    here = o_ref.at[pl.ds(cur[q], n >> (k + 1)), cols]
                    waits.append(("got", go(to_dp(here, here, ssem, rsem, sem(), peer))))
                    cur[q] = old[q][k]
        for kind, cp, *rest in waits:
            if s == 4 or kind in ("small", "swap"):
                cp.wait_send()
                pending[:] = [other for other in pending if other is not cp]
            cp.wait_recv()
            if kind == "small":
                step, rows = rest
                os_ref[rows, :] = os_ref[rows, :] + srecv[step, rows, :]
            elif kind == "strip":
                j, keep, at, half = rest
                cols = pl.ds(128 * j, 128)
                add_into(
                    ot_ref, lambda r, m: (slice(None), pl.ds(keep + r, m), cols),
                    trecv, lambda r, m: (slice(None), pl.ds(at + r, m), cols), half,
                )
            elif kind == "quarter":
                keep, at, half, cols = rest
                add_into(
                    o_ref, lambda r, m: (pl.ds(keep + r, m), cols),
                    recv, lambda r, m: (pl.ds(at + r, m), cols), half,
                )
        if s == 5:
            tgot[mp] = tpack[mp]
            for j in range(STRIPS):
                cols = pl.ds(128 * j, 128)
                ot_ref[:, pl.ds(tcur[j % 4], 16), cols] = tgot[:, j]
    for cp in pending:
        cp.wait_send()


def reduce_dp(x, t, s, cid):
    return call(
        reduce_body,
        tuple(jax.ShapeDtypeStruct(a.shape, a.dtype) for a in (x, t, s)),
        (x, t, s), 7 + 5 * STRIPS + 3 + 4 * STRIPS + 9 * 4 * len(CHUNKS),
        [
            pltpu.VMEM(x.shape, BF), pltpu.VMEM(t.shape, BF), pltpu.VMEM((4, STRIPS, 16, 128), BF),
            pltpu.VMEM((4, STRIPS, 16, 128), BF), pltpu.VMEM((7, 16, D), F32), pltpu.SemaphoreType.REGULAR,
        ],
        cid,
    )


def normalize(rows):
    centre = rows - jnp.mean(rows, axis=-1, keepdims=True)
    inv = lax.rsqrt(jnp.mean(centre * centre, axis=-1, keepdims=True) + EPS)
    return centre * inv, inv


def norm_back(grad, gain, unit, inv):
    g = grad * gain
    return inv * (g - jnp.mean(g, axis=-1, keepdims=True) - unit * jnp.mean(g * unit, axis=-1, keepdims=True))


def mm(a, b, dims="nn"):
    left = 1 if dims[0] == "n" else 0
    right = 0 if dims[1] == "n" else 1
    return lax.dot_general(a, b, (((left,), (right,)), ((), ())), preferred_element_type=F32)


def softmax(scores):
    weights = jnp.exp(scores - jnp.max(scores, axis=-1, keepdims=True))
    return weights / jnp.sum(weights, axis=-1, keepdims=True)


def per_device(
    layer_in, memory, squeezed_mem, memory_fill, squeezed_fill, grad_out, attn_gain, w_query, w_keyval,
    w_output, slopes, ffn_gain, w_up, up_bias, w_down, w_squeeze,
):
    mp, zl, core, part, far = mp_places()
    raw = jnp.concatenate([layer_in[0], memory[0], squeezed_mem[0], grad_out[0]], axis=0)
    whole = gather_mp(raw, 0).reshape(4, 4, 128, D)
    seg, mem, old, gout = (whole[:, a].reshape(512, D) for a in range(4))
    wq = lax.dynamic_slice_in_dim(w_query, mp * 256, 256, 1)
    wkv = jnp.concatenate(
        [lax.dynamic_slice_in_dim(w_keyval, mp * 256, 256, 1), lax.dynamic_slice_in_dim(w_keyval, D + mp * 256, 256, 1)], axis=1
    )
    wo = lax.dynamic_slice_in_dim(w_output, mp * 256, 256, 0)
    slope = lax.dynamic_slice_in_dim(slopes, mp * 2, 2, 0)
    unit, _ = normalize(jnp.concatenate([old, mem, seg], axis=0).astype(F32))
    normed = (unit * attn_gain).astype(BF)
    seg_normed = normed[C + M:]
    query = mm(seg_normed, wq).astype(BF)
    keyval = mm(normed, wkv).astype(BF)
    windows = jnp.concatenate([mem, jnp.zeros((3 * CP - M, D), BF)], axis=0).reshape(CP, 3 * D)
    squeezed = mm(windows, w_squeeze)
    sq_unit, sq_inv = normalize(squeezed)
    sq_kv = mm((sq_unit * attn_gain).astype(BF), wkv).astype(BF)

    rows = jnp.arange(S)[:, None]
    cols = jnp.arange(C + M + S)[None, :]
    distance = (C + M + rows - cols).astype(F32)
    mem_limit = M - memory_fill[0]
    old_limit = C - squeezed_fill[0]
    valid = (
        (cols < C) & (cols >= old_limit)
        | (cols >= C) & (cols < C + M) & (cols >= C + mem_limit)
        | (cols >= C + M) & (cols <= C + M + rows)
    )
    mem_valid = (jnp.arange(M) >= mem_limit)[None, :]
    slots = jnp.arange(CP)[None, :]
    sq_valid = (3 * slots < M) & (3 * slots + 2 >= mem_limit)
    scale = DH ** (-0.5)
    kept, mixed_own = [], []
    gsq_k, gsq_v = [], []
    for h in range(2):
        at = slice(h * DH, (h + 1) * DH)
        vat = slice(256 + h * DH, 256 + (h + 1) * DH)
        q, k, v = query[:, at], keyval[:, at], keyval[:, vat]
        probs = softmax(jnp.where(valid, mm(q, k, "nt") * scale - slope[h] * distance, NEG))
        mixed_own.append(mm(probs.astype(BF), v).astype(BF))
        kept.append(probs)
        km, vm = keyval[C : C + M, at], keyval[C : C + M, vat]
        first = mm(softmax(jnp.where(mem_valid, mm(q, km, "nt") * scale, NEG)).astype(BF), vm)
        ks, vs = sq_kv[:, at], sq_kv[:, vat]
        sprobs = softmax(jnp.where(sq_valid, mm(q, ks, "nt") * scale, NEG))
        second = mm(sprobs.astype(BF), vs)
        gsecond = ((first - second) * (-2.0 / (S * D))).astype(BF)
        gp = mm(gsecond, vs, "nt")
        gsq_v.append(mm(sprobs.astype(BF), gsecond, "tn"))
        gs = (sprobs * (gp - jnp.sum(sprobs * gp, axis=-1, keepdims=True))).astype(BF)
        gsq_k.append(mm(gs, q, "tn") * scale)
    mixed_own = jnp.concatenate(mixed_own, axis=1)
    mixed = gather_mp(mixed_own, 1).transpose(1, 0, 2).reshape(S, D)
    gsq = jnp.concatenate(gsq_k + gsq_v, axis=1).astype(BF)
    dsq = mm(gsq, wkv, "nt")
    dsq = norm_back(dsq, attn_gain, sq_unit, sq_inv)

    mid = seg.astype(F32) + mm(mixed, w_output)
    mid_unit, mid_inv = normalize(mid)
    normed_mid = (mid_unit * ffn_gain).astype(BF)
    pre = mm(normed_mid, w_up) + up_bias
    hidden, gelu_back = jax.vjp(jax.nn.gelu, pre)
    hidden = hidden.astype(BF)
    down = mm(hidden, w_down)
    grad_down = mm(hidden, gout, "tn")
    ghid = mm(gout, w_down, "nt")
    gpre = gelu_back(ghid)[0].astype(BF)
    grad_up_bias = jnp.sum(gpre.astype(F32), axis=0)
    grad_up = mm(normed_mid, gpre, "tn")
    gnm, down_sum = sums_mp(mm(gpre, w_up, "nt"), down, 2)

    own_mid = lax.dynamic_slice_in_dim(mid, mp * 128, 128, 0)
    layer_out = (own_mid + down_sum).astype(BF)

    def parity(a):
        return lax.dynamic_index_in_dim(a.reshape(2, 2, 128, a.shape[-1]), core, 1, keepdims=False)

    unit2, inv2 = parity(mid_unit), parity(mid_inv)
    gmid = parity(gout).astype(F32) + norm_back(gnm, ffn_gain, unit2, inv2)
    own_gnm = lax.dynamic_index_in_dim(gnm, zl, 0, keepdims=False)
    own_unit = lax.dynamic_index_in_dim(unit2, zl, 0, keepdims=False)
    grad_ffn_gain = jnp.sum(own_gnm * own_unit, axis=0)
    own_gmid = lax.dynamic_index_in_dim(gmid, zl, 0, keepdims=False)
    gbranch = pair_gather(gmid.astype(BF), 3).reshape(S, D)
    grad_output = mm(mixed_own, gbranch, "tn")
    gmix = mm(gbranch, wo, "nt").astype(BF)
    gk, gv, gq, gslope = [], [], [], []
    for h in range(2):
        at = slice(h * DH, (h + 1) * DH)
        vat = slice(256 + h * DH, 256 + (h + 1) * DH)
        probs, g = kept[h], gmix[:, at]
        gp = mm(g, keyval[:, vat], "nt")
        gv.append(mm(probs.astype(BF), g, "tn"))
        gs = (probs * (gp - jnp.sum(probs * gp, axis=-1, keepdims=True))).astype(BF)
        gslope.append(-jnp.sum(gs.astype(F32) * distance))
        gq.append((mm(gs, keyval[:, at]) * scale).astype(BF))
        gk.append(mm(gs, query[:, at], "tn") * scale)
    gkv = jnp.concatenate(gk + gv, axis=1).astype(BF)
    gq = jnp.concatenate(gq, axis=1)
    grad_kv = mm(normed, gkv, "tn")
    grad_q = mm(seg_normed, gq, "tn")
    grad_attn_gain = (jnp.sum(grad_kv * wkv.astype(F32), axis=1) + jnp.sum(grad_q * wq.astype(F32), axis=1)) / attn_gain
    seg_terms = mm(gkv[C + M:], wkv, "nt") + mm(gq, wq, "nt")
    seg_sum, dsq_sum = tail_mp(seg_terms, dsq, 4)
    own_seg = layer_in[0].astype(F32)
    seg_unit, seg_inv = normalize(own_seg)
    grad_in = own_gmid + norm_back(seg_sum, attn_gain, seg_unit, seg_inv)
    own_windows = lax.dynamic_slice_in_dim(windows, mp * 768, 768, 1)
    grad_squeeze = mm(own_windows, dsq_sum.reshape(CP, D), "tn")

    x = jnp.concatenate([g.astype(BF) for g in (grad_down, grad_up, grad_squeeze, grad_output)], axis=0)
    t = jnp.concatenate([grad_kv, grad_q], axis=1).astype(BF).reshape(4, 256, 768)
    slope_row = lax.dynamic_update_slice(jnp.zeros((D,), F32), jnp.stack(gslope), (mp * 2,))
    s = jnp.concatenate(
        [jnp.stack([grad_attn_gain, grad_ffn_gain, slope_row]), jnp.zeros((5, D), F32), grad_up_bias[None], jnp.zeros((7, D), F32)], axis=0
    )
    x, t, s = reduce_dp(x, t, s, 5)
    x = x.astype(F32)
    t = t.astype(F32).transpose(1, 0, 2)
    new_squeezed = lax.dynamic_slice_in_dim(squeezed, mp * 43, 43, 0).astype(BF)
    return (
        layer_out[None],
        new_squeezed[None],
        grad_in[None],
        s[0],
        t[:, :, 512:].reshape(256, D),
        jnp.concatenate([t[:, :, :256].reshape(256, D), t[:, :, 256:512].reshape(256, D)], axis=1),
        x[2816:],
        s[2, :8],
        s[1],
        x[1024:2048],
        s[8],
        x[:1024],
        x[2048:2816],
    )


def solution(mesh):
    rows = P("dp", "mp", None)
    in_specs = (
        rows, rows, rows, P("dp"), P("dp"), rows, P(), P(), P(), P(), P(), P(), P(None, "mp"), P("mp"), P("mp", None), P(),
    )
    out_specs = (
        rows, rows, rows, P(), P("mp", None), P("mp", None), P("mp", None), P(), P(), P(None, "mp"), P("mp"), P("mp", None), P("mp", None),
    )
    return jax.shard_map(per_device, mesh=mesh, in_specs=in_specs, out_specs=out_specs, check_vma=False)
```

```python
import functools

import jax
import jax.numpy as jnp
from jax import lax
from jax.experimental import pallas as pl
from jax.experimental.pallas import tpu as pltpu
from jax.sharding import PartitionSpec as P

D = 1024
H = 8
DH = 128
S = 512
M = 512
C = 512
CN = 172
CP = 192
EPS = 1e-05
NEG = -1e30
SCALE = DH ** (-0.5)
RECON = -2.0 / (S * D)
MESH = pl.DeviceIdType.MESH
BF = jnp.bfloat16
F32 = jnp.float32
VMEM = pl.BlockSpec(memory_space=pltpu.VMEM)
SMEM = pl.BlockSpec(memory_space=pltpu.SMEM)
ANY = pl.BlockSpec(memory_space=pl.ANY)
STRIPS = 6
SEG, MEM, OLD, GOUT = 0, 1, 2, 3
BASE = {OLD: 0, MEM: 512, SEG: 1024}
COPIES = 420


def dp_places():
    dp = lax.axis_index("dp")
    y, x, z = dp // 8, (dp // 2) % 4, dp % 2
    xa, xb = x + 1 - 2 * (x % 2), 3 - x
    ya, yb = y + 1 - 2 * (y % 2), 3 - y
    cube = [
        ((x + x // 2) % 2, y * 8 + xa * 2 + z),
        ((y + y // 2) % 2, ya * 8 + x * 2 + z),
        (x // 2, y * 8 + xb * 2 + z),
        (y // 2, yb * 8 + x * 2 + z),
    ]
    return cube, y * 8 + x * 2 + (1 - z)


def mp_places():
    mp = lax.axis_index("mp")
    zl, core = mp // 2, mp % 2
    return mp, zl, core, zl * 2 + (1 - core), (1 - zl) * 2 + core


class Links:
    def __init__(self, ssem, rsem):
        self.ssem, self.rsem, self.count = ssem, rsem, 0

    def start(self, src, dst, place):
        k = self.count
        self.count += 1
        cp = pltpu.make_async_remote_copy(
            src_ref=src, dst_ref=dst, send_sem=self.ssem.at[k], recv_sem=self.rsem.at[k],
            device_id=place, device_id_type=MESH,
        )
        cp.start()
        return cp

    def mp(self, src, dst, peer):
        return self.start(src, dst, (lax.axis_index("dp"), peer))

    def dp(self, src, dst, peer):
        return self.start(src, dst, (peer, lax.axis_index("mp")))


def loop(total, step, body, init=None):
    def run(i, carry):
        return body(pl.multiple_of(i * step, step), carry)

    return lax.fori_loop(0, total // step, run, init)


def each(total, step, body):
    def run(r, carry):
        body(r)
        return carry

    loop(total, step, run, 0)


def add_into(dst, dst_at, src, src_at, rows):
    step = 64 if rows % 64 == 0 else 16

    def body(r):
        to, at = dst_at(r, step), src_at(r, step)
        dst[to] = (dst[to].astype(F32) + src[at].astype(F32)).astype(BF)

    each(rows, step, body)


class Quarters:
    def __init__(self, links, ref, n, recv, base, free):
        self.links, self.ref, self.n, self.recv, self.base, self.free = links, ref, n, recv, base, free
        self.cube, self.zp = dp_places()
        self.cur, self.old = [0] * 4, [[] for _ in range(4)]
        self.flying, self.sent, self.stage = [None] * 4, [], 0

    def launch(self, q, s):
        cols = pl.ds(256 * q, 256)
        n, cur = self.n, self.cur
        if s < 4:
            bit, peer = self.cube[(q + s) % 4]
            half = n >> (s + 1)
            give = pl.multiple_of(cur[q] + (1 - bit) * half, 16)
            self.old[q].append(cur[q])
            cur[q] = pl.multiple_of(cur[q] + bit * half, 16)
            cp = self.links.dp(
                self.ref.at[pl.ds(give, half), cols], self.recv.at[pl.ds(self.base + n - (n >> s), half), cols], peer
            )
        elif s == 4:
            size = n >> 4
            cp = self.links.dp(
                self.ref.at[pl.ds(cur[q], size), cols], self.recv.at[pl.ds(self.base + n - size, size), cols], self.zp
            )
        else:
            k = 8 - s
            bit, peer = self.cube[(q + k) % 4]
            here = self.ref.at[pl.ds(cur[q], n >> (k + 1)), cols]
            cp = self.links.dp(here, here, peer)
            cur[q] = self.old[q][k]
        self.flying[q] = cp

    def begin(self):
        for q in range(4):
            self.launch(q, 0)

    def advance(self):
        s, n = self.stage, self.n
        if s > 8:
            return
        if s == 4:
            pl.semaphore_wait(self.free, 4)
        for q in range(4):
            cp, cols = self.flying[q], pl.ds(256 * q, 256)
            if s == 4:
                cp.wait_send()
            else:
                self.sent.append(cp)
            cp.wait_recv()
            if s <= 4:
                rows = n >> min(s + 1, 4)
                at = self.base + n - (n >> s)
                here = self.cur[q]
                add_into(
                    self.ref, lambda r, m: (pl.ds(here + r, m), cols),
                    self.recv, lambda r, m: (pl.ds(at + r, m), cols), rows,
                )
            if s < 8:
                self.launch(q, s + 1)
        if s == 3:
            for cp in self.sent:
                cp.wait_send()
            self.sent = []
            for _, peer in self.cube:
                pl.semaphore_signal(self.free, inc=1, device_id=(peer, lax.axis_index("mp")), device_id_type=MESH)
        self.stage += 1

    def finish(self):
        for cp in self.sent:
            cp.wait_send()


class Strips:
    def __init__(self, links, ref, recv, pack, got, free):
        self.links, self.ref, self.recv, self.pack, self.got, self.free = links, ref, recv, pack, got, free
        self.cube, self.zp = dp_places()
        self.cur, self.old = [0] * 4, [[] for _ in range(4)]
        self.flying, self.sent, self.stage = [], [], 0

    def launch(self, s):
        ref, cur = self.ref, self.cur
        self.flying = []
        for j in range(STRIPS):
            q, cols = j % 4, pl.ds(128 * j, 128)
            if s < 4:
                bit, peer = self.cube[(q + s) % 4]
                half = 256 >> (s + 1)
                give = pl.multiple_of(cur[q] + (1 - bit) * half, 16)
                cp = self.links.dp(
                    ref.at[:, pl.ds(give, half), cols], self.recv.at[:, pl.ds(256 - (256 >> s), half), cols], peer
                )
            elif s == 4:
                cp = self.links.dp(ref.at[:, pl.ds(cur[q], 16), cols], self.recv.at[:, pl.ds(240, 16), cols], self.zp)
            else:
                k = 9 - s
                bit, peer = self.cube[(q + k) % 4]
                here = ref.at[:, pl.ds(cur[q], 256 >> (k + 1)), cols]
                cp = self.links.dp(here, here, peer)
            self.flying.append(cp)
        for q in range(4):
            if s < 4:
                bit, _ = self.cube[(q + s) % 4]
                self.old[q].append(cur[q])
                cur[q] = pl.multiple_of(cur[q] + bit * (256 >> (s + 1)), 16)
            elif s > 4:
                cur[q] = self.old[q][9 - s]

    def begin(self):
        self.launch(0)

    def advance(self):
        s = self.stage
        if s > 9:
            return
        mp, zl, core, part, far = mp_places()
        if s == 5:
            for cp in self.flying:
                cp.wait()
            self.got[mp] = self.pack[mp]
            for j in range(STRIPS):
                self.ref[:, pl.ds(self.cur[j % 4], 16), pl.ds(128 * j, 128)] = self.got[:, j]
            pl.semaphore_wait(self.free, 4)
            self.launch(6)
        else:
            for j, cp in enumerate(self.flying):
                cols = pl.ds(128 * j, 128)
                if s == 4:
                    cp.wait_send()
                else:
                    self.sent.append(cp)
                cp.wait_recv()
                if s <= 4:
                    rows, at, here = 256 >> min(s + 1, 4), 256 - (256 >> s), self.cur[j % 4]
                    add_into(
                        self.ref, lambda r, m: (slice(None), pl.ds(here + r, m), cols),
                        self.recv, lambda r, m: (slice(None), pl.ds(at + r, m), cols), rows,
                    )
            if s == 3:
                for cp in self.sent:
                    cp.wait_send()
                self.sent = []
                for _, peer in self.cube:
                    pl.semaphore_signal(self.free, inc=1, device_id=(peer, mp), device_id_type=MESH)
            if s == 4:
                for j in range(STRIPS):
                    self.pack[:, j] = self.ref[:, pl.ds(self.cur[j % 4], 16), pl.ds(128 * j, 128)]
                self.flying = [self.links.mp(self.pack.at[peer], self.got.at[mp], peer) for peer in (part, far, 3 - mp)]
            elif s < 9:
                self.launch(s + 1)
        self.stage += 1

    def finish(self):
        for cp in self.sent:
            cp.wait_send()


class Smalls:
    def __init__(self, links, ref, recv):
        self.links, self.ref, self.recv, self.stage = links, ref, recv, 0
        cube, zp = dp_places()
        self.peers = [peer for _, peer in cube] + [zp]

    def begin(self):
        s = self.stage
        mp, zl, core, part, far = mp_places()
        self.rows = pl.ds(0, 16 if s < 5 else 8)
        src, dst = self.ref.at[self.rows], self.recv.at[s, self.rows]
        if s < 5:
            self.cp = self.links.dp(src, dst, self.peers[s])
        else:
            self.cp = self.links.mp(src, dst, (part, far)[s - 5])

    def advance(self):
        if self.stage > 6:
            return
        self.cp.wait()
        self.ref[self.rows, :] = self.ref[self.rows, :] + self.recv[self.stage, self.rows, :]
        self.stage += 1
        if self.stage <= 6:
            self.begin()

    def finish(self):
        pass


def dg(a, b, left=1, right=0):
    return lax.dot_general(a, b, (((left,), (right,)), ((), ())), preferred_element_type=F32)


def normalize(rows):
    centre = rows - jnp.mean(rows, axis=-1, keepdims=True)
    inv = lax.rsqrt(jnp.mean(centre * centre, axis=-1, keepdims=True) + EPS)
    return centre * inv, inv


def norm_back(grad, gain, unit, inv):
    g = grad * gain
    return inv * (g - jnp.mean(g, axis=-1, keepdims=True) - unit * jnp.mean(g * unit, axis=-1, keepdims=True))


def iota(shape, dim):
    return lax.broadcasted_iota(jnp.int32, shape, dim)


def fold(x, op):
    out = x[:8]
    for i in range(1, x.shape[0] // 8):
        out = op(out, x[8 * i : 8 * i + 8])
    return out


def layer_body(
    seg_in, mem_in, old_in, gout_in, wq_in, wkv_in, wo_in, wup_in, wdn_in, wsq_in,
    mfill, sfill, slopes, again, fgain, ubias,
    lout, sqz_out, gin, x_down, x_up, x_sq, x_out, t_ref, s_ref,
    raw, normed, wkvq, wo, wup, wdn, wsq, kv, query, expo, tmp, tmp2, stat, acc, mixt, mixg, mid, nm, hid, gpre,
    out, got, keep, out2, got2, gb, gmix, gkv, gq, win, sqz, skv, esq, gsq, rec, sbuf, sgot, sqsum, trecv, tpack, tgot, srecv,
    lsem, free, ssem, rsem,
):
    links = Links(ssem, rsem)
    mp, zl, core, part, far = mp_places()
    diag = 3 - mp
    cube, zp = dp_places()
    dp = lax.axis_index("dp")
    mine = pl.ds(pl.multiple_of(mp * 256, 256), 256)

    ins = {SEG: seg_in, MEM: mem_in, OLD: old_in, GOUT: gout_in}
    own_loads = {}
    nlocal = [0]

    def load(src, dst):
        cp = pltpu.make_async_copy(src, dst, lsem.at[nlocal[0]])
        nlocal[0] += 1
        cp.start()
        return cp

    for a in (SEG, MEM, OLD, GOUT):
        own_loads[a] = load(ins[a], raw.at[a, mp])
    w_loads = [
        load(wkv_in.at[:, mine], wkvq.at[:, pl.ds(0, 256)]),
        load(wkv_in.at[:, pl.ds(pl.multiple_of(D + mp * 256, 256), 256)], wkvq.at[:, pl.ds(256, 256)]),
        load(wq_in.at[:, mine], wkvq.at[:, pl.ds(512, 256)]),
    ]
    sq_load = load(wsq_in, wsq)
    late_loads = [load(wo_in, wo), load(wup_in, wup), load(wdn_in, wdn)]

    sem = pltpu.get_barrier_semaphore()
    for peer in [peer for _, peer in cube] + [zp]:
        pl.semaphore_signal(sem, inc=1, device_id=(peer, mp), device_id_type=MESH)
    for peer in (part, far, diag):
        pl.semaphore_signal(sem, inc=1, device_id=(dp, peer), device_id_type=MESH)
    pl.semaphore_wait(sem, 8)

    done = []

    far_cp, part_cp, fwd_cp = {}, {}, {}

    def send_far(a):
        far_cp[a] = links.mp(ins[a], raw.at[a, mp], far)

    send_far(SEG)
    send_far(MEM)
    for a in (SEG, MEM, OLD, GOUT):
        part_cp[a] = links.mp(ins[a], raw.at[a, mp], part)

    def norm_rows(a, owner):
        unit, _ = normalize(raw[a, owner].astype(F32))
        normed[pl.ds(pl.multiple_of(BASE[a] + owner * 128, 128), 128), :] = (unit * again[...]).astype(BF)

    def arrive(a, following=None):
        far_cp[a].wait_recv()
        fwd_cp[a] = links.mp(raw.at[a, far], raw.at[a, far], part)
        done.extend([far_cp[a], fwd_cp[a]])
        if following is not None:
            send_far(following)

    def project(a):
        rows = pl.ds(BASE[a], 512)
        kv[rows, :] = dg(normed[rows, :], wkvq[:, 0:512]).astype(BF)
        if a == SEG:
            query[...] = dg(normed[rows, :], wkvq[:, 512:768]).astype(BF)

    mem_limit = M - mfill[0]
    old_limit = C - sfill[0]

    def slope_of(h):
        return slopes[mp * 2 + h]

    def heads(h):
        return pl.ds(h * DH, DH)

    def column(r, rows):
        return iota((rows, 1), 0) + r

    def exponentials(src, dst, dst0, rows, colmask, causal=False):
        step = 64

        def one(r, top):
            s = src[pl.ds(r, step), :] * SCALE + colmask(r, step)
            if causal:
                s = jnp.where(iota((step, 512), 0) + r <= iota((step, 512), 1), s, NEG)
            src[pl.ds(r, step), :] = s
            return jnp.maximum(top, fold(s, jnp.maximum))

        top = loop(rows, step, one, jnp.full((8, 512), NEG, F32))
        top = jnp.max(top, axis=0, keepdims=True)

        def two(r, total):
            e = jnp.exp(src[pl.ds(r, step), :] - top).astype(BF)
            dst[pl.ds(dst0 + r, step), :] = e
            return total + fold(e.astype(F32), jnp.add)

        total = loop(rows, step, two, jnp.zeros((8, 512), F32))
        return top, jnp.sum(total, axis=0, keepdims=True)

    def attend(h, a):
        base = BASE[a]
        rows = pl.ds(base, 512)
        g = base // 512
        tmp[...] = dg(kv[rows, heads(h)], query[:, heads(h)], 1, 1)
        slope = slope_of(h)

        def colmask(r, step):
            j = column(r, step)
            bias = slope * (j + (base - 1536)).astype(F32)
            if a == MEM:
                bias = jnp.where(j >= mem_limit, bias, NEG)
            if a == OLD:
                bias = jnp.where(j >= old_limit, bias, NEG)
            return bias

        top, total = exponentials(tmp, expo.at[h], base, 512, colmask, a == SEG)
        stat[h * 6 + g : h * 6 + g + 1, :] = top
        stat[h * 6 + 3 + g : h * 6 + 4 + g, :] = total
        acc[h * 3 + g] = dg(kv[rows, pl.ds(256 + h * DH, DH)], expo[h, rows, :], 0, 0)

    def first_of(h):
        rows = pl.ds(BASE[MEM], 512)
        tmp[...] = dg(kv[rows, heads(h)], query[:, heads(h)], 1, 1)
        _, total = exponentials(
            tmp, gkv, 0, 512, lambda r, step: jnp.where(column(r, step) >= mem_limit, 0.0, NEG)
        )
        rec[heads(h), :] = dg(kv[rows, pl.ds(256 + h * DH, DH)], gkv[0:512, :], 0, 0) / total

    for a in (SEG, MEM, OLD):
        own_loads[a].wait()
        norm_rows(a, mp)
    own_loads[GOUT].wait()
    for a in (SEG, MEM, OLD):
        part_cp[a].wait_recv()
        norm_rows(a, part)
    arrive(SEG, OLD)
    norm_rows(SEG, far)
    for cp in w_loads:
        cp.wait()
    fwd_cp[SEG].wait_recv()
    norm_rows(SEG, diag)
    project(SEG)
    attend(0, SEG)
    arrive(MEM, GOUT)
    norm_rows(MEM, far)
    attend(1, SEG)
    fwd_cp[MEM].wait_recv()
    norm_rows(MEM, diag)
    project(MEM)
    for h in range(2):
        attend(h, MEM)

    sq_load.wait()

    def squeeze():
        rows = raw[MEM].reshape(512, D)
        for tap in range(3):
            pick = (iota((CP, 512), 1) == 3 * iota((CP, 512), 0) + tap).astype(BF)
            win[:, tap * D : (tap + 1) * D] = dg(pick, rows).astype(BF)
        for half in range(2):
            cols = pl.ds(half * 512, 512)
            sqz[:, cols] = dg(win[...], wsq[:, cols])

    squeeze()
    for peer in [peer for _, peer in cube] + [zp]:
        pl.semaphore_signal(free.at[0], inc=1, device_id=(peer, mp), device_id_type=MESH)
    arrive(OLD)
    norm_rows(OLD, far)
    sqz_out[...] = sqz[...].astype(BF)
    unit, _ = normalize(sqz[...])
    skv[...] = dg((unit * again[...]).astype(BF), wkvq[:, 0:512]).astype(BF)
    fwd_cp[OLD].wait_recv()
    norm_rows(OLD, diag)
    project(OLD)
    for h in range(2):
        attend(h, OLD)

    for h in range(2):
        tops = [stat[h * 6 + g : h * 6 + g + 1, :] for g in range(3)]
        sums = [stat[h * 6 + 3 + g : h * 6 + 4 + g, :] for g in range(3)]
        top = jnp.maximum(jnp.maximum(tops[0], tops[1]), tops[2])
        scales = [jnp.exp(t - top) for t in tops]
        total = scales[0] * sums[0] + scales[1] * sums[1] + scales[2] * sums[2]
        mixed = jnp.zeros((DH, 512), F32)
        for g in range(3):
            inv = scales[g] / total
            stat[12 + h * 3 + g : 13 + h * 3 + g, :] = inv
            mixed = mixed + acc[h * 3 + g] * inv
        mixt[heads(h), :] = mixed
        mixg[mp, :, heads(h)] = mixed.T.astype(BF)
    mix_far = links.mp(mixg.at[mp], mixg.at[mp], far)
    mix_part = links.mp(mixg.at[mp], mixg.at[mp], part)
    done.extend([mix_far, mix_part])

    for h in range(2):
        first_of(h)
    arrive(GOUT)

    def second_of(h):
        keys, values = skv[:, heads(h)], skv[:, pl.ds(256 + h * DH, DH)]
        tmp[0:CP, :] = dg(keys, query[:, heads(h)], 1, 1)

        def colmask(r, step):
            slot = column(r, step)
            return jnp.where((3 * slot < M) & (3 * slot + 2 >= mem_limit), 0.0, NEG)

        _, total = exponentials(tmp, esq, 0, CP, colmask)
        inv = 1.0 / total
        second = dg(values, esq[...], 0, 0) * inv
        grad = (rec[heads(h), :] - second) * RECON
        inner = inv * jnp.sum(grad * second, axis=0, keepdims=True)
        scaled = (grad * inv).astype(BF)
        gsq[:, pl.ds(256 + h * DH, DH)] = dg(esq[...], scaled, 1, 1).astype(BF)
        gp = dg(values, scaled)
        gs = (esq[...].astype(F32) * (gp - inner)).astype(BF)
        gsq[:, heads(h)] = (dg(gs, query[:, heads(h)]) * SCALE).astype(BF)

    for h in range(2):
        second_of(h)

    def seg_rows():
        return raw[SEG].reshape(512, D).astype(F32)

    def mix_into(owners, first=False):
        for half in range(2):
            cols = pl.ds(half * 512, 512)
            base = raw[SEG, :, :, cols].reshape(512, 512).astype(F32) if first else mid[:, cols]
            for owner in owners:
                base = base + dg(mixg[owner], wo[pl.ds(pl.multiple_of(owner * 256, 256), 256), cols])
            mid[:, cols] = base

    for cp in late_loads:
        cp.wait()
    mix_part.wait_recv()
    mix_into((mp, part), True)
    mix_far.wait_recv()
    mix_fwd = links.mp(mixg.at[far], mixg.at[far], part)
    done.append(mix_fwd)
    unit, inv = normalize(sqz[...])
    sqz[...] = norm_back(dg(gsq[...], wkvq[:, 0:512], 1, 1), again[...], unit, inv)
    sbuf[0] = sqz[pl.ds(pl.multiple_of((1 - core) * 96, 16), 96), :].astype(BF)
    sq_part = links.mp(sbuf.at[0], sgot.at[0], part)
    done.append(sq_part)
    mix_into((far,))
    mix_fwd.wait_recv()
    mix_into((diag,))

    def norm_mid(r):
        unit, _ = normalize(mid[pl.ds(r, 128), :])
        nm[pl.ds(r, 128), :] = (unit * fgain[...]).astype(BF)

    each(512, 128, norm_mid)
    for a in (SEG, MEM, OLD, GOUT):
        done.append(part_cp[a])
    part_cp[GOUT].wait_recv()
    fwd_cp[GOUT].wait_recv()

    def gout_rows():
        return raw[GOUT].reshape(512, D)

    for half in range(2):
        cols = pl.ds(half * 512, 512)
        tmp[...] = dg(nm[...], wup[:, cols])
        tmp2[...] = dg(gout_rows(), wdn[cols, :], 1, 1)

        def gelu(r, total):
            rows = pl.ds(r, 32)
            v = tmp[rows, :] + ubias[:, cols]
            square = v * v
            th = jnp.tanh(0.7978845608028654 * v * (1.0 + 0.044715 * square))
            hid[rows, cols] = (0.5 * v * (1.0 + th)).astype(BF)
            slope = 0.5 * (1.0 + th) + (0.5 * 0.7978845608028654) * v * (1.0 - th * th) * (1.0 + 3 * 0.044715 * square)
            g = (slope * tmp2[rows, :]).astype(BF)
            gpre[rows, cols] = g
            return total + fold(g.astype(F32), jnp.add)

        total = loop(512, 32, gelu, jnp.zeros((8, 512), F32))
        s_ref[8:9, cols] = jnp.sum(total, axis=0, keepdims=True)

    def block(z, other):
        return pl.ds(pl.multiple_of((2 * z + ((1 - core) if other else core)) * 128, 128), 128)

    gnm_part, gnm_far, down_part = [], [], []
    for z in range(2):
        out[0, z] = dg(gpre[block(z, True), :], wup[...], 1, 1).astype(BF)
        gnm_part.append(links.mp(out.at[0, z], got.at[0, z], part))
    for z in range(2):
        keep[0, z] = dg(gpre[block(z, False), :], wup[...], 1, 1)
    for z in range(2):
        gnm_part[z].wait_recv()
        out2[z] = (keep[0, z] + got[0, z].astype(F32)).astype(BF)
        gnm_far.append(links.mp(out2.at[z], got2.at[z], far))
    sq_part.wait_recv()
    sbuf[1] = (sqz[pl.ds(pl.multiple_of(core * 96, 16), 96), :] + sgot[0].astype(F32)).astype(BF)
    sq_far = links.mp(sbuf.at[1], sgot.at[1], far)
    for z in range(2):
        out[1, z] = dg(hid[block(z, True), :], wdn[...]).astype(BF)
        down_part.append(links.mp(out.at[1, z], got.at[1, z], part))
    for half in range(2):
        rows = pl.ds(half * 512, 512)
        for quarter in range(2):
            cols = pl.ds(quarter * 512, 512)
            x_down[rows, cols] = dg(hid[:, rows], raw[GOUT, :, :, cols].reshape(512, 512), 0, 0).astype(BF)
    pl.semaphore_wait(free.at[0], 5)
    sums_down = Quarters(links, x_down, 1024, wsq, 0, free.at[1])
    sums_up = Quarters(links, x_up, 1024, wsq, 1024, free.at[2])
    sums_sq = Quarters(links, x_sq, 768, wsq, 2048, free.at[3])
    sums_down.begin()
    for z in range(2):
        keep[1, z] = dg(hid[block(z, False), :], wdn[...])
    for z in range(2):
        down_part[z].wait_recv()
    out2[2] = (keep[1, 1 - zl] + got[1, 1 - zl].astype(F32)).astype(BF)
    down_far = links.mp(out2.at[2], got2.at[2], far)
    for half in range(2):
        rows = pl.ds(half * 512, 512)
        for quarter in range(2):
            cols = pl.ds(quarter * 512, 512)
            x_up[rows, cols] = dg(nm[:, rows], gpre[:, cols], 0, 0).astype(BF)
    sums_up.begin()
    sq_far.wait()
    sqsum[core] = (sbuf[1].astype(F32) + sgot[1].astype(F32)).astype(BF)
    sq_back = links.mp(sqsum.at[core], sqsum.at[core], part)

    gb_cp = []
    gain_total = jnp.zeros((1, D), F32)
    for z in range(2):
        gnm_far[z].wait()
        rows = block(z, False)
        unit, inv = normalize(mid[rows, :])
        g = out2[z].astype(F32) + got2[z].astype(F32)
        gain_total = gain_total + jnp.sum(g * unit, axis=0, keepdims=True) * jnp.where(zl == z, 1.0, 0.0)
        gmid = raw[GOUT, 2 * z + core].astype(F32) + norm_back(g, fgain[...], unit, inv)
        keep[0, z] = gmid
        gb[z, core] = gmid.astype(BF)
        gb_cp.append(links.mp(gb.at[z, core], gb.at[z, core], part))
    s_ref[1:2, :] = gain_total
    sq_back.wait()
    for half in range(2):
        cols = pl.ds(half * 512, 512)
        x_sq[:, cols] = dg(win[:, pl.ds(pl.multiple_of(mp * 768, 256), 768)], sqsum[:, :, cols].reshape(CP, 512), 0, 0).astype(BF)
    sums_sq.begin()
    for cp in gb_cp:
        cp.wait()

    gmix[...] = dg(wo[mine, :], gb[...].reshape(512, D), 1, 1)
    for half in range(2):
        cols = pl.ds(half * 512, 512)
        x_out[:, cols] = dg(mixg[mp], gb[:, :, :, cols].reshape(512, 512), 0, 0).astype(BF)
    sums_out = Quarters(links, x_out, 256, wsq, 2816, free.at[4])
    sums_out.begin()
    slope_row = jnp.zeros((1, D), F32)
    for h in range(2):
        grad = gmix[heads(h), :]
        inner = jnp.sum(grad * mixt[heads(h), :], axis=0, keepdims=True)
        slope_acc = jnp.zeros((8, 512), F32)
        gqt = jnp.zeros((DH, 512), F32)
        for a in (OLD, MEM, SEG):
            base = BASE[a]
            rows = pl.ds(base, 512)
            inv = stat[12 + h * 3 + base // 512 : 13 + h * 3 + base // 512, :]
            scaled = (grad * inv).astype(BF)
            shift = inv * inner
            tmp[...] = dg(kv[rows, pl.ds(256 + h * DH, DH)], scaled)
            gkv[rows, pl.ds(256 + h * DH, DH)] = dg(expo[h, rows, :], scaled, 1, 1).astype(BF)

            def score_grads(r, total):
                at = pl.ds(base + r, 64)
                gs = (expo[h, at, :].astype(F32) * (tmp[pl.ds(r, 64), :] - shift)).astype(BF)
                expo[h, at, :] = gs
                dist = (iota((64, 512), 1) - iota((64, 512), 0) + (1024 - base - r)).astype(F32)
                return total + fold(gs.astype(F32) * dist, jnp.add)

            slope_acc = loop(512, 64, score_grads, slope_acc)
            gkv[rows, heads(h)] = (dg(expo[h, rows, :], query[:, heads(h)]) * SCALE).astype(BF)
            gqt = gqt + dg(kv[rows, heads(h)], expo[h, rows, :], 0, 0)
        gq[:, heads(h)] = (gqt * SCALE).T.astype(BF)
        value = -jnp.sum(jnp.sum(slope_acc, axis=0, keepdims=True), axis=1, keepdims=True)
        slope_row = slope_row + jnp.where(iota((1, D), 1) == mp * 2 + h, value, 0.0)
        sums_down.advance()
        sums_up.advance()
    s_ref[2:3, :] = slope_row
    s_ref[3:8, :] = jnp.zeros((5, D), F32)
    s_ref[9:16, :] = jnp.zeros((7, D), F32)

    for b in range(4):
        feats = pl.ds(b * 256, 256)
        big = dg(normed[:, feats], gkv[...], 0, 0)
        small = dg(normed[1024:1536, feats], gq[...], 0, 0)
        t_ref[b, :, 0:512] = big.astype(BF)
        t_ref[b, :, 512:768] = small.astype(BF)
        terms = small[:, 0:128] * wkvq[feats, 512:640].astype(F32) + small[:, 128:256] * wkvq[feats, 640:768].astype(F32)
        for j in range(4):
            terms = terms + big[:, j * 128 : (j + 1) * 128] * wkvq[feats, j * 128 : (j + 1) * 128].astype(F32)
        s_ref[0:1, feats] = jnp.sum(terms.T, axis=0, keepdims=True) / again[:, feats]
    sums_t = Strips(links, t_ref, trecv, tpack, tgot, free.at[5])
    sums_t.begin()
    sums_s = Smalls(links, s_ref, srecv)
    sums_s.begin()

    def seg_terms(z, other):
        rows = block(z, other)
        at = pl.ds(pl.multiple_of(BASE[SEG] + (2 * z + ((1 - core) if other else core)) * 128, 128), 128)
        return dg(gkv[at, :], wkvq[:, 0:512], 1, 1) + dg(gq[rows, :], wkvq[:, 512:768], 1, 1)

    for cp in gnm_part:
        cp.wait_send()
    for cp in down_part:
        cp.wait_send()
    seg_part = []
    for z in range(2):
        out[0, z] = seg_terms(z, True).astype(BF)
        seg_part.append(links.mp(out.at[0, z], got.at[0, z], part))
    down_far.wait()
    lout[...] = (
        mid[pl.ds(pl.multiple_of(mp * 128, 128), 128), :]
        + keep[1, zl] + got[1, zl].astype(F32) + got2[2].astype(F32)
    ).astype(BF)
    for z in range(2):
        keep[1, z] = seg_terms(z, False)
    for cp in seg_part:
        cp.wait_recv()
    out2[3] = (keep[1, 1 - zl] + got[0, 1 - zl].astype(F32)).astype(BF)
    seg_far = links.mp(out2.at[3], got2.at[3], far)
    done.extend(seg_part)

    for sums in (sums_sq, sums_down, sums_up, sums_out, sums_t, sums_s):
        sums.advance()
    seg_far.wait()
    unit, inv = normalize(raw[SEG, mp].astype(F32))
    total = keep[1, zl] + got[0, zl].astype(F32) + got2[3].astype(F32)
    gin[...] = keep[0, zl] + norm_back(total, again[...], unit, inv)
    everything = (sums_sq, sums_down, sums_up, sums_out, sums_t, sums_s)
    for _ in range(10):
        for sums in everything:
            sums.advance()
    for sums in everything:
        sums.finish()
    for cp in done:
        cp.wait_send()


def layer(args):
    def out_shape(shape, dtype):
        return jax.ShapeDtypeStruct(shape, dtype)

    outs = (
        out_shape((128, D), BF), out_shape((CP, D), BF), out_shape((128, D), F32), out_shape((1024, D), BF),
        out_shape((1024, D), BF), out_shape((768, D), BF), out_shape((256, D), BF), out_shape((4, 256, 768), BF),
        out_shape((16, D), F32),
    )
    v = pltpu.VMEM
    scratch = [
        v((4, 4, 128, D), BF), v((1536, D), BF), v((D, 768), BF), v((D, D), BF), v((D, D), BF), v((D, D), BF),
        v((3072, D), BF), v((1536, 512), BF), v((512, 256), BF), v((2, 1536, 512), BF), v((512, 512), F32),
        v((512, 512), F32), v((24, 512), F32), v((6, DH, 512), F32), v((256, 512), F32), v((4, 512, 256), BF),
        v((512, D), F32), v((512, D), BF), v((512, D), BF), v((512, D), BF),
        v((2, 2, 128, D), BF), v((2, 2, 128, D), BF), v((2, 2, 128, D), F32), v((4, 128, D), BF), v((4, 128, D), BF),
        v((2, 2, 128, D), BF), v((256, 512), F32), v((1536, 512), BF), v((512, 256), BF),
        v((CP, 3 * D), BF), v((CP, D), F32), v((CP, 512), BF), v((CP, 512), BF), v((CP, 512), BF), v((256, 512), F32),
        v((2, 96, D), BF), v((2, 96, D), BF), v((2, 96, D), BF),
        v((4, 256, 768), BF), v((4, STRIPS, 16, 128), BF), v((4, STRIPS, 16, 128), BF), v((7, 16, D), F32),
        pltpu.SemaphoreType.DMA((16,)), pltpu.SemaphoreType.REGULAR((8,)),
        pltpu.SemaphoreType.DMA((COPIES,)), pltpu.SemaphoreType.DMA((COPIES,)),
    ]
    return pl.pallas_call(
        layer_body,
        out_shape=outs,
        in_specs=[ANY] * 10 + [SMEM] * 3 + [VMEM] * 3,
        out_specs=tuple(VMEM for _ in outs),
        scratch_shapes=scratch,
        compiler_params=pltpu.CompilerParams(collective_id=0, has_side_effects=True, vmem_limit_bytes=62 << 20),
    )(*args)


def per_device(
    layer_in, memory, squeezed_mem, memory_fill, squeezed_fill, grad_out, attn_gain, w_query, w_keyval,
    w_output, slopes, ffn_gain, w_up, up_bias, w_down, w_squeeze,
):
    mp = lax.axis_index("mp")
    lout, sqz, gin, down, up, sq, gout, t, s = layer((
        layer_in[0], memory[0], squeezed_mem[0], grad_out[0], w_query, w_keyval, w_output, w_up, w_down, w_squeeze,
        memory_fill, squeezed_fill, slopes, attn_gain[None], ffn_gain[None], up_bias[None],
    ))
    t = t.astype(F32).transpose(1, 0, 2)
    return (
        lout[None],
        lax.dynamic_slice_in_dim(sqz, mp * 43, 43, 0)[None],
        gin[None],
        s[0],
        t[:, :, 512:].reshape(256, D),
        jnp.concatenate([t[:, :, :256].reshape(256, D), t[:, :, 256:512].reshape(256, D)], axis=1),
        gout.astype(F32),
        s[2, :8],
        s[1],
        up.astype(F32),
        s[8],
        down.astype(F32),
        sq.astype(F32),
    )


def solution(mesh):
    rows = P("dp", "mp", None)
    in_specs = (
        rows, rows, rows, P("dp"), P("dp"), rows, P(), P(), P(), P(), P(), P(), P(None, "mp"), P("mp"), P("mp", None), P(),
    )
    out_specs = (
        rows, rows, rows, P(), P("mp", None), P("mp", None), P("mp", None), P(), P(), P(None, "mp"), P("mp"), P("mp", None), P("mp", None),
    )
    return jax.shard_map(per_device, mesh=mesh, in_specs=in_specs, out_specs=out_specs, check_vma=False)
```

```python
import functools

import jax
import jax.numpy as jnp
from jax import lax
from jax.experimental import pallas as pl
from jax.experimental.pallas import tpu as pltpu
from jax.sharding import PartitionSpec as P

D = 1024
H = 8
DH = 128
S = 512
M = 512
C = 512
CN = 172
CP = 192
EPS = 1e-05
NEG = -1e30
SCALE = DH ** (-0.5)
RECON = -2.0 / (S * D)
MESH = pl.DeviceIdType.MESH
BF = jnp.bfloat16
F32 = jnp.float32
VMEM = pl.BlockSpec(memory_space=pltpu.VMEM)
SMEM = pl.BlockSpec(memory_space=pltpu.SMEM)
ANY = pl.BlockSpec(memory_space=pl.ANY)
STRIPS = 6
SEG, MEM, OLD, GOUT = 0, 1, 2, 3
BASE = {OLD: 0, MEM: 512, SEG: 1024}
SENDS = 72
RECVS = 160


def dp_places():
    dp = lax.axis_index("dp")
    y, x, z = dp // 8, (dp // 2) % 4, dp % 2
    xa, xb = x + 1 - 2 * (x % 2), 3 - x
    ya, yb = y + 1 - 2 * (y % 2), 3 - y
    cube = [
        ((x + x // 2) % 2, y * 8 + xa * 2 + z),
        ((y + y // 2) % 2, ya * 8 + x * 2 + z),
        (x // 2, y * 8 + xb * 2 + z),
        (y // 2, yb * 8 + x * 2 + z),
    ]
    return cube, y * 8 + x * 2 + (1 - z)


def mp_places():
    mp = lax.axis_index("mp")
    zl, core = mp // 2, mp % 2
    return mp, zl, core, zl * 2 + (1 - core), (1 - zl) * 2 + core


class Flight:
    def __init__(self, links, cp, send, recv):
        self.links, self.cp, self.send, self.recv = links, cp, send, recv

    def wait_send(self):
        self.cp.wait_send()
        self.links.spare.append(self.send)

    def wait_recv(self):
        self.cp.wait_recv()

    def wait(self):
        self.wait_send()
        self.wait_recv()


class Links:
    def __init__(self, ssem, rsem):
        self.ssem, self.rsem, self.spare, self.sends, self.recvs = ssem, rsem, [], 0, 0

    def start(self, src, dst, place, like=None):
        if self.spare:
            k = self.spare.pop(0)
        else:
            k, self.sends = self.sends, self.sends + 1
        if like is not None:
            r = like.recv
        else:
            r, self.recvs = self.recvs, self.recvs + 1
        cp = pltpu.make_async_remote_copy(
            src_ref=src, dst_ref=dst, send_sem=self.ssem.at[k], recv_sem=self.rsem.at[r],
            device_id=place, device_id_type=MESH,
        )
        cp.start()
        return Flight(self, cp, k, r)

    def mp(self, src, dst, peer):
        return self.start(src, dst, (lax.axis_index("dp"), peer))

    def dp(self, src, dst, peer, like=None):
        return self.start(src, dst, (peer, lax.axis_index("mp")), like)


def loop(total, step, body, init=None):
    def run(i, carry):
        return body(pl.multiple_of(i * step, step), carry)

    return lax.fori_loop(0, total // step, run, init)


def each(total, step, body):
    def run(r, carry):
        body(r)
        return carry

    loop(total, step, run, 0)


def add_into(dst, dst_at, src, src_at, rows):
    step = 64 if rows % 64 == 0 else 16

    def body(r):
        to, at = dst_at(r, step), src_at(r, step)
        dst[to] = dst[to] + src[at]

    each(rows, step, body)


class Quarters:
    last = 8

    def __init__(self, links, ref, n, recv, base, free, order=(0, 1, 2, 3)):
        self.links, self.ref, self.n, self.recv, self.base, self.free = links, ref, n, recv, base, free
        self.order = order
        self.cube, self.zp = dp_places()
        self.cur, self.old = [0] * 4, [[] for _ in range(4)]
        self.flying, self.sent, self.stage, self.out = [None] * 4, [], 0, [[] for _ in range(4)]

    def launch(self, q, s):
        cols = pl.ds(256 * q, 256)
        n, cur = self.n, self.cur
        if s < 4:
            bit, peer = self.cube[(self.order[q] + s) % 4]
            half = n >> (s + 1)
            give = pl.multiple_of(cur[q] + (1 - bit) * half, 16)
            self.old[q].append(cur[q])
            cur[q] = pl.multiple_of(cur[q] + bit * half, 16)
            cp = self.links.dp(
                self.ref.at[pl.ds(give, half), cols], self.recv.at[pl.ds(self.base + n - (n >> s), half), cols], peer
            )
        elif s == 4:
            size = n >> 4
            cp = self.links.dp(
                self.ref.at[pl.ds(cur[q], size), cols], self.recv.at[pl.ds(self.base + n - size, size), cols], self.zp
            )
        else:
            k = 8 - s
            bit, peer = self.cube[(self.order[q] + k) % 4]
            here = self.ref.at[pl.ds(cur[q], n >> (k + 1)), cols]
            cp = self.links.dp(here, here, peer, self.out[q][k])
            cur[q] = self.old[q][k]
        self.out[q].append(cp)
        self.flying[q] = cp

    def begin(self):
        for q in range(4):
            self.launch(q, 0)

    def advance(self):
        s, n = self.stage, self.n
        if s > 8:
            return
        if s == 4:
            pl.semaphore_wait(self.free, 4)
        earlier, self.sent = self.sent, []
        for q in range(4):
            cp, cols = self.flying[q], pl.ds(256 * q, 256)
            if s == 4:
                cp.wait_send()
            else:
                self.sent.append(cp)
            cp.wait_recv()
            if s <= 4:
                rows = n >> min(s + 1, 4)
                at = self.base + n - (n >> s)
                here = self.cur[q]
                add_into(
                    self.ref, lambda r, m: (pl.ds(here + r, m), cols),
                    self.recv, lambda r, m: (pl.ds(at + r, m), cols), rows,
                )
            if s < 8:
                self.launch(q, s + 1)
        for cp in earlier:
            cp.wait_send()
        if s == 3:
            for cp in self.sent:
                cp.wait_send()
            self.sent = []
            for _, peer in self.cube:
                pl.semaphore_signal(self.free, inc=1, device_id=(peer, lax.axis_index("mp")), device_id_type=MESH)
        self.stage += 1

    def finish(self):
        for cp in self.sent:
            cp.wait_send()


class Strips:
    last = 9

    def __init__(self, links, ref, recv, pack, got, free):
        self.links, self.ref, self.recv, self.pack, self.got, self.free = links, ref, recv, pack, got, free
        self.cube, self.zp = dp_places()
        self.cur, self.old = [0] * 4, [[] for _ in range(4)]
        self.flying, self.sent, self.stage, self.out = [], [], 0, []

    def launch(self, s):
        ref, cur = self.ref, self.cur
        self.flying = []
        for j in range(STRIPS):
            q, cols = j % 4, pl.ds(128 * j, 128)
            if s < 4:
                bit, peer = self.cube[(q + s) % 4]
                half = 256 >> (s + 1)
                give = pl.multiple_of(cur[q] + (1 - bit) * half, 16)
                cp = self.links.dp(
                    ref.at[:, pl.ds(give, half), cols], self.recv.at[:, pl.ds(256 - (256 >> s), half), cols], peer
                )
            elif s == 4:
                cp = self.links.dp(ref.at[:, pl.ds(cur[q], 16), cols], self.recv.at[:, pl.ds(240, 16), cols], self.zp)
            else:
                k = 9 - s
                bit, peer = self.cube[(q + k) % 4]
                here = ref.at[:, pl.ds(cur[q], 256 >> (k + 1)), cols]
                cp = self.links.dp(here, here, peer, self.out[k][j])
            self.flying.append(cp)
        self.out.append(self.flying)
        for q in range(4):
            if s < 4:
                bit, _ = self.cube[(q + s) % 4]
                self.old[q].append(cur[q])
                cur[q] = pl.multiple_of(cur[q] + bit * (256 >> (s + 1)), 16)
            elif s > 4:
                cur[q] = self.old[q][9 - s]

    def begin(self):
        self.launch(0)

    def advance(self):
        s = self.stage
        if s > 9:
            return
        mp, zl, core, part, far = mp_places()
        earlier, self.sent = self.sent, []
        if s == 5:
            for cp in self.flying:
                cp.wait()
            self.got[mp] = self.pack[mp]
            for j in range(STRIPS):
                self.ref[:, pl.ds(self.cur[j % 4], 16), pl.ds(128 * j, 128)] = self.got[:, j]
            pl.semaphore_wait(self.free, 4)
            self.launch(6)
        else:
            for j, cp in enumerate(self.flying):
                cols = pl.ds(128 * j, 128)
                if s == 4:
                    cp.wait_send()
                else:
                    self.sent.append(cp)
                cp.wait_recv()
                if s <= 4:
                    rows, at, here = 256 >> min(s + 1, 4), 256 - (256 >> s), self.cur[j % 4]
                    add_into(
                        self.ref, lambda r, m: (slice(None), pl.ds(here + r, m), cols),
                        self.recv, lambda r, m: (slice(None), pl.ds(at + r, m), cols), rows,
                    )
            if s == 3:
                for cp in self.sent:
                    cp.wait_send()
                self.sent = []
                for _, peer in self.cube:
                    pl.semaphore_signal(self.free, inc=1, device_id=(peer, mp), device_id_type=MESH)
            if s == 4:
                for j in range(STRIPS):
                    self.pack[:, j] = self.ref[:, pl.ds(self.cur[j % 4], 16), pl.ds(128 * j, 128)]
                self.flying = [self.links.mp(self.pack.at[peer], self.got.at[mp], peer) for peer in (part, far, 3 - mp)]
            elif s < 9:
                self.launch(s + 1)
        for cp in earlier:
            cp.wait_send()
        self.stage += 1

    def finish(self):
        for cp in self.sent:
            cp.wait_send()


class Smalls:
    last = 6

    def __init__(self, links, ref, recv):
        self.links, self.ref, self.recv, self.stage = links, ref, recv, 0
        cube, zp = dp_places()
        self.peers = [peer for _, peer in cube] + [zp]

    def begin(self):
        s = self.stage
        mp, zl, core, part, far = mp_places()
        self.rows = pl.ds(0, 16 if s < 5 else 8)
        src, dst = self.ref.at[self.rows], self.recv.at[s, self.rows]
        if s < 5:
            self.cp = self.links.dp(src, dst, self.peers[s])
        else:
            self.cp = self.links.mp(src, dst, (part, far)[s - 5])

    def advance(self):
        if self.stage > 6:
            return
        self.cp.wait()
        self.ref[self.rows, :] = self.ref[self.rows, :] + self.recv[self.stage, self.rows, :]
        self.stage += 1
        if self.stage <= 6:
            self.begin()

    def finish(self):
        pass


def dg(a, b, left=1, right=0):
    return lax.dot_general(a, b, (((left,), (right,)), ((), ())), preferred_element_type=F32)


def normalize(rows):
    centre = rows - jnp.mean(rows, axis=-1, keepdims=True)
    inv = lax.rsqrt(jnp.mean(centre * centre, axis=-1, keepdims=True) + EPS)
    return centre * inv, inv


def norm_back(grad, gain, unit, inv):
    g = grad * gain
    return inv * (g - jnp.mean(g, axis=-1, keepdims=True) - unit * jnp.mean(g * unit, axis=-1, keepdims=True))


def iota(shape, dim):
    return lax.broadcasted_iota(jnp.int32, shape, dim)


def fold(x, op):
    out = x[:8]
    for i in range(1, x.shape[0] // 8):
        out = op(out, x[8 * i : 8 * i + 8])
    return out


def layer_body(
    seg_in, mem_in, old_in, gout_in, wq_in, wkv_in, wo_in, wup_in, wdn_in, wsq_in,
    mfill, sfill, slopes, again, fgain, ubias,
    lout, sqz_out, gin, down_out, up_out, sq_out, out_out, t_out, s_ref,
    raw, normed, wkvq, wo, wup, wdn, wsq, kv, query, expo, tmp, tmp2, stat, acc, mixt, mixg, mid, nm, hid, gpre,
    out, got, keep, out2, got2, gb, gmix, gkv, gq, win, sqz, skv, esq, gsq, rec, sbuf, sgot, sqsum, trecv, tpack, tgot, srecv,
    x_down, x_up, x_sq, x_out, t_ref, lsem, free, ssem, rsem,
):
    links = Links(ssem, rsem)
    mp, zl, core, part, far = mp_places()
    diag = 3 - mp
    cube, zp = dp_places()
    dp = lax.axis_index("dp")
    mine = pl.ds(pl.multiple_of(mp * 256, 256), 256)

    ins = {SEG: seg_in, MEM: mem_in, OLD: old_in, GOUT: gout_in}
    own_loads = {}
    nlocal = [0]

    def load(src, dst):
        cp = pltpu.make_async_copy(src, dst, lsem.at[nlocal[0]])
        nlocal[0] += 1
        cp.start()
        return cp

    for a in (SEG, MEM, OLD, GOUT):
        own_loads[a] = load(ins[a], raw.at[a, mp])
    w_loads = [
        load(wkv_in.at[:, mine], wkvq.at[:, pl.ds(0, 256)]),
        load(wkv_in.at[:, pl.ds(pl.multiple_of(D + mp * 256, 256), 256)], wkvq.at[:, pl.ds(256, 256)]),
        load(wq_in.at[:, mine], wkvq.at[:, pl.ds(512, 256)]),
    ]

    sem = pltpu.get_barrier_semaphore()
    for peer in [peer for _, peer in cube] + [zp]:
        pl.semaphore_signal(sem, inc=1, device_id=(peer, mp), device_id_type=MESH)
    for peer in (part, far, diag):
        pl.semaphore_signal(sem, inc=1, device_id=(dp, peer), device_id_type=MESH)
    pl.semaphore_wait(sem, 8)

    done = []

    far_cp, part_cp, fwd_cp = {}, {}, {}

    queue = [(a, i) for a in (SEG, MEM, OLD, GOUT) for i in range(2)]

    def send_far():
        a, i = queue[len(far_cp)]
        rows = pl.ds(64 * i, 64)
        far_cp[a, i] = links.mp(ins[a].at[rows], raw.at[a, mp, rows], far)

    def pump():
        far_cp[queue[len(far_cp) - 2]].wait_send()
        send_far()

    send_far()
    send_far()
    for a in (SEG, MEM, OLD, GOUT):
        part_cp[a] = links.mp(ins[a], raw.at[a, mp], part)
    sq_load = load(wsq_in, wsq)
    late_loads = [load(wo_in, wo), load(wup_in, wup), load(wdn_in, wdn)]

    def norm_rows(a, owner):
        unit, _ = normalize(raw[a, owner].astype(F32))
        normed[pl.ds(pl.multiple_of(BASE[a] + owner * 128, 128), 128), :] = (unit * again[...]).astype(BF)

    def arrive(a):
        far_cp[a, 0].wait_recv()
        far_cp[a, 1].wait_recv()
        fwd_cp[a] = links.mp(raw.at[a, far], raw.at[a, far], part)
        done.append(fwd_cp[a])

    def project(a):
        rows = pl.ds(BASE[a], 512)
        kv[rows, :] = dg(normed[rows, :], wkvq[:, 0:512]).astype(BF)
        if a == SEG:
            query[...] = dg(normed[rows, :], wkvq[:, 512:768]).astype(BF)

    mem_limit = M - mfill[0]
    old_limit = C - sfill[0]

    def slope_of(h):
        return slopes[mp * 2 + h]

    def heads(h):
        return pl.ds(h * DH, DH)

    def column(r, rows):
        return iota((rows, 1), 0) + r

    def exponentials(src, dst, dst0, rows, colmask, causal=False):
        step = 64

        def one(r, top):
            s = src[pl.ds(r, step), :] * SCALE + colmask(r, step)
            if causal:
                s = jnp.where(iota((step, 512), 0) + r <= iota((step, 512), 1), s, NEG)
            src[pl.ds(r, step), :] = s
            return jnp.maximum(top, fold(s, jnp.maximum))

        top = loop(rows, step, one, jnp.full((8, 512), NEG, F32))
        top = jnp.max(top, axis=0, keepdims=True)

        def two(r, total):
            e = jnp.exp(src[pl.ds(r, step), :] - top).astype(BF)
            dst[pl.ds(dst0 + r, step), :] = e
            return total + fold(e.astype(F32), jnp.add)

        total = loop(rows, step, two, jnp.zeros((8, 512), F32))
        return top, jnp.sum(total, axis=0, keepdims=True)

    def attend(h, a):
        base = BASE[a]
        rows = pl.ds(base, 512)
        g = base // 512
        tmp[...] = dg(kv[rows, heads(h)], query[:, heads(h)], 1, 1)
        slope = slope_of(h)

        def colmask(r, step):
            j = column(r, step)
            bias = slope * (j + (base - 1536)).astype(F32)
            if a == MEM:
                bias = jnp.where(j >= mem_limit, bias, NEG)
            if a == OLD:
                bias = jnp.where(j >= old_limit, bias, NEG)
            return bias

        top, total = exponentials(tmp, expo.at[h], base, 512, colmask, a == SEG)
        stat[h * 6 + g : h * 6 + g + 1, :] = top
        stat[h * 6 + 3 + g : h * 6 + 4 + g, :] = total
        acc[h * 3 + g] = dg(kv[rows, pl.ds(256 + h * DH, DH)], expo[h, rows, :], 0, 0)

    def first_of(h):
        rows = pl.ds(BASE[MEM], 512)
        tmp[...] = dg(kv[rows, heads(h)], query[:, heads(h)], 1, 1)
        _, total = exponentials(
            tmp, gkv, 0, 512, lambda r, step: jnp.where(column(r, step) >= mem_limit, 0.0, NEG)
        )
        rec[heads(h), :] = dg(kv[rows, pl.ds(256 + h * DH, DH)], gkv[0:512, :], 0, 0) / total

    for a in (SEG, MEM, OLD):
        own_loads[a].wait()
        norm_rows(a, mp)
    own_loads[GOUT].wait()
    for a in (SEG, MEM, OLD):
        part_cp[a].wait_recv()
        norm_rows(a, part)
    pump()
    for cp in w_loads:
        cp.wait()
    pump()
    arrive(SEG)
    norm_rows(SEG, far)
    fwd_cp[SEG].wait_recv()
    norm_rows(SEG, diag)
    pump()
    project(SEG)
    pump()
    arrive(MEM)
    norm_rows(MEM, far)
    attend(0, SEG)
    fwd_cp[MEM].wait_recv()
    norm_rows(MEM, diag)
    pump()
    project(MEM)
    attend(1, SEG)
    pump()
    arrive(OLD)
    norm_rows(OLD, far)
    attend(0, MEM)
    fwd_cp[OLD].wait_recv()
    norm_rows(OLD, diag)
    project(OLD)
    attend(1, MEM)
    for h in range(2):
        attend(h, OLD)
    far_cp[GOUT, 0].wait_send()
    done.append(far_cp[GOUT, 1])

    for h in range(2):
        tops = [stat[h * 6 + g : h * 6 + g + 1, :] for g in range(3)]
        sums = [stat[h * 6 + 3 + g : h * 6 + 4 + g, :] for g in range(3)]
        top = jnp.maximum(jnp.maximum(tops[0], tops[1]), tops[2])
        scales = [jnp.exp(t - top) for t in tops]
        total = scales[0] * sums[0] + scales[1] * sums[1] + scales[2] * sums[2]
        mixed = jnp.zeros((DH, 512), F32)
        for g in range(3):
            inv = scales[g] / total
            stat[12 + h * 3 + g : 13 + h * 3 + g, :] = inv
            mixed = mixed + acc[h * 3 + g] * inv
        mixt[heads(h), :] = mixed
        mixg[mp, :, heads(h)] = mixed.T.astype(BF)
    mix_far, mix_part, mix_fwd = [], [], []

    def half_rows(z):
        return pl.ds(z * 256, 256)

    for z in range(2):
        here = mixg.at[mp, half_rows(z)]
        mix_far.append(links.mp(here, here, far))
        mix_part.append(links.mp(here, here, part))
    done.extend(mix_far + mix_part)

    sq_load.wait()

    def squeeze():
        rows = raw[MEM].reshape(512, D)
        for tap in range(3):
            pick = (iota((CP, 512), 1) == 3 * iota((CP, 512), 0) + tap).astype(BF)
            win[:, tap * D : (tap + 1) * D] = dg(pick, rows).astype(BF)
        for half in range(2):
            cols = pl.ds(half * 512, 512)
            sqz[:, cols] = dg(win[...], wsq[:, cols])

    squeeze()
    for peer in [peer for _, peer in cube] + [zp]:
        pl.semaphore_signal(free.at[0], inc=1, device_id=(peer, mp), device_id_type=MESH)
    arrive(GOUT)

    def seg_rows():
        return raw[SEG].reshape(512, D).astype(F32)

    def mix_into(z, owners, first=False):
        rows = half_rows(z)
        for half in range(2):
            cols = pl.ds(half * 512, 512)
            base = raw[SEG, 2 * z : 2 * z + 2, :, cols].reshape(256, 512).astype(F32) if first else mid[rows, cols]
            for owner in owners:
                base = base + dg(mixg[owner, rows, :], wo[pl.ds(pl.multiple_of(owner * 256, 256), 256), cols])
            mid[rows, cols] = base

    for cp in late_loads:
        cp.wait()
    for a in (SEG, MEM, OLD, GOUT):
        done.append(part_cp[a])
    part_cp[GOUT].wait_recv()
    fwd_cp[GOUT].wait_recv()

    def norm_mid(r):
        unit, _ = normalize(mid[pl.ds(r, 128), :])
        nm[pl.ds(r, 128), :] = (unit * fgain[...]).astype(BF)

    def forward_mix(z):
        mix_far[z].wait_recv()
        here = mixg.at[far, half_rows(z)]
        mix_fwd.append(links.mp(here, here, part))
        done.append(mix_fwd[z])

    for z in range(2):
        mix_part[z].wait_recv()
        mix_into(z, (mp, part), True)
    forward_mix(0)
    mix_into(0, (far,))
    bias_total = [jnp.zeros((8, 512), F32), jnp.zeros((8, 512), F32)]
    for z in range(2):
        if z == 1:
            forward_mix(1)
            mix_into(1, (far,))
        mix_fwd[z].wait_recv()
        mix_into(z, (diag,))
        rows = half_rows(z)
        norm_mid(z * 256)
        norm_mid(z * 256 + 128)
        for half in range(2):
            cols = pl.ds(half * 512, 512)
            tmp[half_rows(half), :] = dg(nm[rows, :], wup[:, cols])
            tmp2[half_rows(half), :] = dg(raw[GOUT, 2 * z : 2 * z + 2].reshape(256, D), wdn[cols, :], 1, 1)
        for half in range(2):
            cols = pl.ds(half * 512, 512)

            def gelu(r, total):
                at = pl.ds(r + half * 256, 32)
                to = pl.ds(r + z * 256, 32)
                v = tmp[at, :] + ubias[:, cols]
                square = v * v
                th = jnp.tanh(0.7978845608028654 * v * (1.0 + 0.044715 * square))
                hid[to, cols] = (0.5 * v * (1.0 + th)).astype(BF)
                slope = 0.5 * (1.0 + th) + (0.5 * 0.7978845608028654) * v * (1.0 - th * th) * (1.0 + 3 * 0.044715 * square)
                g = (slope * tmp2[at, :]).astype(BF)
                gpre[to, cols] = g
                return total + fold(g.astype(F32), jnp.add)

            bias_total[half] = loop(256, 32, gelu, bias_total[half])
    for half in range(2):
        s_ref[8:9, pl.ds(half * 512, 512)] = jnp.sum(bias_total[half], axis=0, keepdims=True)

    def block(z, other):
        return pl.ds(pl.multiple_of((2 * z + ((1 - core) if other else core)) * 128, 128), 128)

    pl.semaphore_wait(free.at[0], 5)
    sums_down = Quarters(links, x_down, 1024, wsq, 0, free.at[1])
    sums_up = Quarters(links, x_up, 1024, wsq, 1024, free.at[2])
    sums_sq = Quarters(links, x_sq, 768, wsq, 2048, free.at[3])
    for half in range(2):
        rows = pl.ds(half * 512, 512)
        for quarter in range(2):
            cols = pl.ds(quarter * 512, 512)
            x_down[rows, cols] = dg(hid[:, rows], raw[GOUT, :, :, cols].reshape(512, 512), 0, 0).astype(BF)
    sums_down.begin()
    gnm_part, gnm_far, down_part = [], [], []
    for z in range(2):
        out[0, z] = dg(gpre[block(z, True), :], wup[...], 1, 1).astype(BF)
        gnm_part.append(links.mp(out.at[0, z], got.at[0, z], part))
    for half in range(2):
        rows = pl.ds(half * 512, 512)
        for quarter in range(2):
            cols = pl.ds(quarter * 512, 512)
            x_up[rows, cols] = dg(nm[:, rows], gpre[:, cols], 0, 0).astype(BF)
    sums_up.begin()
    for z in range(2):
        keep[0, z] = dg(gpre[block(z, False), :], wup[...], 1, 1)
        gnm_part[z].wait_recv()
        out2[z] = (keep[0, z] + got[0, z].astype(F32)).astype(BF)
        gnm_far.append(links.mp(out2.at[z], got2.at[z], far))

    pick = (iota((48, CP), 1) == iota((48, CP), 0) + mp * 43).astype(BF)
    sqz_out[...] = dg(pick, sqz[...].astype(BF))[0:43].astype(BF)
    unit, _ = normalize(sqz[...])
    skv[...] = dg((unit * again[...]).astype(BF), wkvq[:, 0:512]).astype(BF)
    first_of(0)
    sums_down.advance()
    first_of(1)

    def second_of(h):
        keys, values = skv[:, heads(h)], skv[:, pl.ds(256 + h * DH, DH)]
        tmp[0:CP, :] = dg(keys, query[:, heads(h)], 1, 1)

        def colmask(r, step):
            slot = column(r, step)
            return jnp.where((3 * slot < M) & (3 * slot + 2 >= mem_limit), 0.0, NEG)

        _, total = exponentials(tmp, esq, 0, CP, colmask)
        inv = 1.0 / total
        second = dg(values, esq[...], 0, 0) * inv
        grad = (rec[heads(h), :] - second) * RECON
        inner = inv * jnp.sum(grad * second, axis=0, keepdims=True)
        scaled = (grad * inv).astype(BF)
        gsq[:, pl.ds(256 + h * DH, DH)] = dg(esq[...], scaled, 1, 1).astype(BF)
        gp = dg(values, scaled)
        gs = (esq[...].astype(F32) * (gp - inner)).astype(BF)
        gsq[:, heads(h)] = (dg(gs, query[:, heads(h)]) * SCALE).astype(BF)

    for h in range(2):
        second_of(h)
    unit, inv = normalize(sqz[...])
    sqz[...] = norm_back(dg(gsq[...], wkvq[:, 0:512], 1, 1), again[...], unit, inv)
    sbuf[0] = sqz[pl.ds(pl.multiple_of((1 - core) * 96, 16), 96), :].astype(BF)
    sq_part = links.mp(sbuf.at[0], sgot.at[0], part)
    done.append(sq_part)
    for z in range(2):
        out[1, z] = dg(hid[block(z, True), :], wdn[...]).astype(BF)
        down_part.append(links.mp(out.at[1, z], got.at[1, z], part))
    sums_down.advance()
    sums_up.advance()
    sq_part.wait_recv()
    sbuf[1] = (sqz[pl.ds(pl.multiple_of(core * 96, 16), 96), :] + sgot[0].astype(F32)).astype(BF)
    for z in range(2):
        keep[1, z] = dg(hid[block(z, False), :], wdn[...])
    sums_down.advance()

    gb_cp = []
    gain_total = jnp.zeros((1, D), F32)
    for z in range(2):
        gnm_far[z].wait()
        rows = block(z, False)
        unit, inv = normalize(mid[rows, :])
        g = out2[z].astype(F32) + got2[z].astype(F32)
        gain_total = gain_total + jnp.sum(g * unit, axis=0, keepdims=True) * jnp.where(zl == z, 1.0, 0.0)
        gmid = raw[GOUT, 2 * z + core].astype(F32) + norm_back(g, fgain[...], unit, inv)
        keep[0, z] = gmid
        gb[z, core] = gmid.astype(BF)
        gb_cp.append(links.mp(gb.at[z, core], gb.at[z, core], part))
    s_ref[1:2, :] = gain_total
    sq_far = links.mp(sbuf.at[1], sgot.at[1], far)
    sums_down.advance()
    sums_up.advance()
    for z in range(2):
        down_part[z].wait_recv()
    out2[2] = (keep[1, 1 - zl] + got[1, 1 - zl].astype(F32)).astype(BF)
    for cp in gb_cp:
        cp.wait()

    gmix[...] = dg(wo[mine, :], gb[...].reshape(512, D), 1, 1)
    for half in range(2):
        cols = pl.ds(half * 512, 512)
        x_out[:, cols] = dg(mixg[mp], gb[:, :, :, cols].reshape(512, 512), 0, 0).astype(BF)
    sums_out = Quarters(links, x_out, 256, wsq, 2816, free.at[4], (2, 3, 2, 3))
    sums_out.begin()
    slope_row = jnp.zeros((1, D), F32)
    for h in range(2):
        grad = gmix[heads(h), :]
        inner = jnp.sum(grad * mixt[heads(h), :], axis=0, keepdims=True)
        slope_acc = jnp.zeros((8, 512), F32)
        gqt = jnp.zeros((DH, 512), F32)
        for a in (OLD, MEM, SEG):
            base = BASE[a]
            rows = pl.ds(base, 512)
            inv = stat[12 + h * 3 + base // 512 : 13 + h * 3 + base // 512, :]
            scaled = (grad * inv).astype(BF)
            shift = inv * inner
            tmp[...] = dg(kv[rows, pl.ds(256 + h * DH, DH)], scaled)
            gkv[rows, pl.ds(256 + h * DH, DH)] = dg(expo[h, rows, :], scaled, 1, 1).astype(BF)

            def score_grads(r, total):
                at = pl.ds(base + r, 64)
                gs = (expo[h, at, :].astype(F32) * (tmp[pl.ds(r, 64), :] - shift)).astype(BF)
                expo[h, at, :] = gs
                dist = (iota((64, 512), 1) - iota((64, 512), 0) + (1024 - base - r)).astype(F32)
                return total + fold(gs.astype(F32) * dist, jnp.add)

            slope_acc = loop(512, 64, score_grads, slope_acc)
            gkv[rows, heads(h)] = (dg(expo[h, rows, :], query[:, heads(h)]) * SCALE).astype(BF)
            gqt = gqt + dg(kv[rows, heads(h)], expo[h, rows, :], 0, 0)
        gq[:, heads(h)] = (gqt * SCALE).T.astype(BF)
        value = -jnp.sum(jnp.sum(slope_acc, axis=0, keepdims=True), axis=1, keepdims=True)
        slope_row = slope_row + jnp.where(iota((1, D), 1) == mp * 2 + h, value, 0.0)
        sums_down.advance()
        sums_up.advance()
        if h == 0:
            sq_far.wait()
            sqsum[core] = (sbuf[1].astype(F32) + sgot[1].astype(F32)).astype(BF)
            sq_back = links.mp(sqsum.at[core], sqsum.at[core], part)
            down_far = links.mp(out2.at[2], got2.at[2], far)
        else:
            sq_back.wait()
            for half in range(2):
                cols = pl.ds(half * 512, 512)
                x_sq[:, cols] = dg(win[:, pl.ds(pl.multiple_of(mp * 768, 256), 768)], sqsum[:, :, cols].reshape(CP, 512), 0, 0).astype(BF)
            sums_sq.begin()
    s_ref[2:3, :] = slope_row
    s_ref[3:8, :] = jnp.zeros((5, D), F32)
    s_ref[9:16, :] = jnp.zeros((7, D), F32)

    for b in range(4):
        feats = pl.ds(b * 256, 256)
        big = dg(normed[:, feats], gkv[...], 0, 0)
        small = dg(normed[1024:1536, feats], gq[...], 0, 0)
        t_ref[b, :, 0:512] = big.astype(BF)
        t_ref[b, :, 512:768] = small.astype(BF)
        terms = small[:, 0:128] * wkvq[feats, 512:640].astype(F32) + small[:, 128:256] * wkvq[feats, 640:768].astype(F32)
        for j in range(4):
            terms = terms + big[:, j * 128 : (j + 1) * 128] * wkvq[feats, j * 128 : (j + 1) * 128].astype(F32)
        s_ref[0:1, feats] = jnp.sum(terms.T, axis=0, keepdims=True) / again[:, feats]
    sums_t = Strips(links, t_ref, trecv, tpack, tgot, free.at[5])
    sums_t.begin()
    sums_s = Smalls(links, s_ref, srecv)
    sums_s.begin()
    sums_down.advance()
    sums_up.advance()

    def seg_terms(z, other):
        rows = block(z, other)
        at = pl.ds(pl.multiple_of(BASE[SEG] + (2 * z + ((1 - core) if other else core)) * 128, 128), 128)
        return dg(gkv[at, :], wkvq[:, 0:512], 1, 1) + dg(gq[rows, :], wkvq[:, 512:768], 1, 1)

    for cp in gnm_part:
        cp.wait_send()
    for cp in down_part:
        cp.wait_send()
    seg_part = []
    for z in range(2):
        out[0, z] = seg_terms(z, True).astype(BF)
        seg_part.append(links.mp(out.at[0, z], got.at[0, z], part))
    down_far.wait()
    lout[...] = (
        mid[pl.ds(pl.multiple_of(mp * 128, 128), 128), :]
        + keep[1, zl] + got[1, zl].astype(F32) + got2[2].astype(F32)
    ).astype(BF)
    for z in range(2):
        keep[1, z] = seg_terms(z, False)
    for cp in seg_part:
        cp.wait_recv()
    out2[3] = (keep[1, 1 - zl] + got[0, 1 - zl].astype(F32)).astype(BF)
    seg_far = links.mp(out2.at[3], got2.at[3], far)
    done.extend(seg_part)

    for sums in (sums_down, sums_up, sums_sq, sums_out, sums_t, sums_s):
        sums.advance()
    seg_far.wait()
    unit, inv = normalize(raw[SEG, mp].astype(F32))
    total = keep[1, zl] + got[0, zl].astype(F32) + got2[3].astype(F32)
    gin[...] = keep[0, zl] + norm_back(total, again[...], unit, inv)
    everything = {sums_down: (x_down, down_out), sums_up: (x_up, up_out), sums_t: (t_ref, t_out), sums_out: (x_out, out_out), sums_sq: (x_sq, sq_out), sums_s: None}
    leaving = []
    for _ in range(11):
        for sums, where in everything.items():
            last = sums.stage == sums.last
            sums.advance()
            if last and where is not None:
                leaving.append(load(*where))
    for sums in everything:
        sums.finish()
    for cp in leaving:
        cp.wait()
    for cp in done:
        cp.wait_send()


def layer(args):
    def out_shape(shape, dtype):
        return jax.ShapeDtypeStruct(shape, dtype)

    outs = (
        out_shape((128, D), BF), out_shape((43, D), BF), out_shape((128, D), F32), out_shape((1024, D), BF),
        out_shape((1024, D), BF), out_shape((768, D), BF), out_shape((256, D), BF), out_shape((4, 256, 768), BF),
        out_shape((16, D), F32),
    )
    v = pltpu.VMEM
    scratch = [
        v((4, 4, 128, D), BF), v((1536, D), BF), v((D, 768), BF), v((D, D), BF), v((D, D), BF), v((D, D), BF),
        v((3072, D), BF), v((1536, 512), BF), v((512, 256), BF), v((2, 1536, 512), BF), v((512, 512), F32),
        v((512, 512), F32), v((24, 512), F32), v((6, DH, 512), F32), v((256, 512), F32), v((4, 512, 256), BF),
        v((512, D), F32), v((512, D), BF), v((512, D), BF), v((512, D), BF),
        v((2, 2, 128, D), BF), v((2, 2, 128, D), BF), v((2, 2, 128, D), F32), v((4, 128, D), BF), v((4, 128, D), BF),
        v((2, 2, 128, D), BF), v((256, 512), F32), v((1536, 512), BF), v((512, 256), BF),
        v((CP, 3 * D), BF), v((CP, D), F32), v((CP, 512), BF), v((CP, 512), BF), v((CP, 512), BF), v((256, 512), F32),
        v((2, 96, D), BF), v((2, 96, D), BF), v((2, 96, D), BF),
        v((4, 256, 768), BF), v((4, STRIPS, 16, 128), BF), v((4, STRIPS, 16, 128), BF), v((7, 16, D), F32),
        v((D, D), BF), v((D, D), BF), v((768, D), BF), v((256, D), BF), v((4, 256, 768), BF),
        pltpu.SemaphoreType.DMA((17,)), pltpu.SemaphoreType.REGULAR((6,)),
        pltpu.SemaphoreType.DMA((SENDS,)), pltpu.SemaphoreType.DMA((RECVS,)),
    ]
    return pl.pallas_call(
        layer_body,
        out_shape=outs,
        in_specs=[ANY] * 10 + [SMEM] * 3 + [VMEM] * 3,
        out_specs=(VMEM, VMEM, VMEM, ANY, ANY, ANY, ANY, ANY, VMEM),
        scratch_shapes=scratch,
        compiler_params=pltpu.CompilerParams(collective_id=0, has_side_effects=True, vmem_limit_bytes=62 << 20),
    )(*args)


def widen_body(lout, sqz, gin, down, up, sq, outp, t, s, *refs):
    (o_lout, o_sqz, o_gin, o_again, o_q, o_kv, o_out, o_slopes, o_fgain, o_up, o_ubias, o_down, o_sq) = refs[:13]
    lin, wide, sem_in, sem_out = refs[13:]
    pieces = []
    for src, dst, n in ((down, o_down, 4), (up, o_up, 4), (sq, o_sq, 3), (outp, o_out, 1)):
        for i in range(n):
            pieces.append((src.at[pl.ds(256 * i, 256)], dst.at[pl.ds(256 * i, 256)]))
    loads = []
    for i, (src, _) in enumerate(pieces):
        loads.append(pltpu.make_async_copy(src, lin.at[i], sem_in.at[i]))
    for cp in loads:
        cp.start()
    for b in range(4):
        for part in range(2):
            o_kv[:, pl.ds(part * D + b * 256, 256)] = t[b, :, part * 256 : part * 256 + 256].astype(F32)
        o_q[:, pl.ds(b * 256, 256)] = t[b, :, 512:768].astype(F32)
    o_lout[...] = lout[...]
    o_gin[...] = gin[...]
    o_sqz[...] = sqz[...]
    o_again[...] = s[0:1, :]
    o_fgain[...] = s[1:2, :]
    o_slopes[...] = s[2:3, 0:8]
    o_ubias[...] = s[8:9, :]
    stores = []
    for i, (_, dst) in enumerate(pieces):
        loads[i].wait()
        wide[i] = lin[i].astype(F32)
        stores.append(pltpu.make_async_copy(wide.at[i], dst, sem_out.at[i]))
        stores[-1].start()
    for cp in stores:
        cp.wait()


def widen(args):
    def out_shape(shape, dtype):
        return jax.ShapeDtypeStruct(shape, dtype)

    outs = (
        out_shape((128, D), BF), out_shape((43, D), BF), out_shape((128, D), F32), out_shape((1, D), F32),
        out_shape((256, D), F32), out_shape((256, 2 * D), F32), out_shape((256, D), F32), out_shape((1, 8), F32),
        out_shape((1, D), F32), out_shape((D, D), F32), out_shape((1, D), F32), out_shape((D, D), F32),
        out_shape((768, D), F32),
    )
    hbm = (6, 9, 11, 12)
    return pl.pallas_call(
        widen_body,
        out_shape=outs,
        in_specs=[VMEM, VMEM, VMEM, ANY, ANY, ANY, ANY, VMEM, VMEM],
        out_specs=tuple(ANY if i in hbm else VMEM for i in range(13)),
        scratch_shapes=[
            pltpu.VMEM((12, 256, D), BF), pltpu.VMEM((12, 256, D), F32),
            pltpu.SemaphoreType.DMA((12,)), pltpu.SemaphoreType.DMA((12,)),
        ],
        compiler_params=pltpu.CompilerParams(vmem_limit_bytes=62 << 20),
    )(*args)


def per_device(
    layer_in, memory, squeezed_mem, memory_fill, squeezed_fill, grad_out, attn_gain, w_query, w_keyval,
    w_output, slopes, ffn_gain, w_up, up_bias, w_down, w_squeeze,
):
    done = layer((
        layer_in[0], memory[0], squeezed_mem[0], grad_out[0], w_query, w_keyval, w_output, w_up, w_down, w_squeeze,
        memory_fill, squeezed_fill, slopes, attn_gain[None], ffn_gain[None], up_bias[None],
    ))
    lout, sqz, gin, again, q, kv, out, slope, fgain, up, ubias, down, sq = widen(done)
    return (
        lout[None], sqz[None], gin[None], again[0], q, kv, out, slope[0], fgain[0], up, ubias[0], down, sq,
    )


def solution(mesh):
    rows = P("dp", "mp", None)
    in_specs = (
        rows, rows, rows, P("dp"), P("dp"), rows, P(), P(), P(), P(), P(), P(), P(None, "mp"), P("mp"), P("mp", None), P(),
    )
    out_specs = (
        rows, rows, rows, P(), P("mp", None), P("mp", None), P("mp", None), P(), P(), P(None, "mp"), P("mp"), P("mp", None), P("mp", None),
    )
    return jax.shard_map(per_device, mesh=mesh, in_specs=in_specs, out_specs=out_specs, check_vma=False)
```

```python
import functools

import jax
import jax.numpy as jnp
from jax import lax
from jax.experimental import pallas as pl
from jax.experimental.pallas import tpu as pltpu
from jax.sharding import PartitionSpec as P

D = 1024
H = 8
DH = 128
S = 512
M = 512
C = 512
CN = 172
CP = 192
EPS = 1e-05
NEG = -1e30
SCALE = DH ** (-0.5)
RECON = -2.0 / (S * D)
MESH = pl.DeviceIdType.MESH
BF = jnp.bfloat16
F32 = jnp.float32
VMEM = pl.BlockSpec(memory_space=pltpu.VMEM)
SMEM = pl.BlockSpec(memory_space=pltpu.SMEM)
ANY = pl.BlockSpec(memory_space=pl.ANY)
STRIPS = 6
SEG, MEM, OLD, GOUT = 0, 1, 2, 3
BASE = {OLD: 0, MEM: 512, SEG: 1024}
ORDER = (
    "send.s", "psend.m", "psend.s", "own.o", "psend.o", "own.s", "par.o", "send.o", "par.m", "own.m", "par.s",
    "psend.g", "pjo.s", "arr.s", "pjo.o", "pjo.m", "dia.s", "send.m", "far.s", "pjf.s", "arr.o", "at.s.0", "at.s.1",
    "far.o", "dia.o", "pjf.o", "at.o.1", "arr.m", "send.g", "far.m", "at.o.0", "dia.m", "pjf.m", "at.m.1", "at.m.0",
    "combine", "f0", "arr.g", "mf1", "squeeze", "gh0", "mix0a", "fw0", "gh1", "mix0b", "mix1a", "fw1", "ffn0",
    "mix1b", "ffn1", "gnmo", "up", "gnmw", "gS0", "f1", "down", "gS1", "r1", "s1", "s0", "U0", "dsq", "dno", "lnb0",
    "sqS", "lnb1", "D0", "U1", "xout", "att0.0", "sqT", "att0.1", "att0", "att1.0", "xsq", "att1.1", "D1", "att1",
    "t.0", "t.1", "U2", "t.2", "D2", "t", "dnw", "sego", "S0", "D3", "Q0", "dnS", "segw", "T0", "O0", "Q1", "U3",
    "S1", "D4", "O1", "T1", "Q2", "D5", "S2", "Q3", "U4", "O2", "T2", "D6", "Q4", "T3", "O3", "U5", "Q5", "D7", "U6",
    "T4", "Q6", "T5", "segS", "O4", "T6", "S3", "lout", "O5", "Q7", "U7", "O6", "T7", "S4", "T8", "gin", "O7", "U8",
    "S5", "Q8", "D8", "O8", "S6", "T9",
)
SENDS = 86
RECVS = 173


def dp_places():
    dp = lax.axis_index("dp")
    y, x, z = dp // 8, (dp // 2) % 4, dp % 2
    xa, xb = x + 1 - 2 * (x % 2), 3 - x
    ya, yb = y + 1 - 2 * (y % 2), 3 - y
    cube = [
        ((x + x // 2) % 2, y * 8 + xa * 2 + z),
        ((y + y // 2) % 2, ya * 8 + x * 2 + z),
        (x // 2, y * 8 + xb * 2 + z),
        (y // 2, yb * 8 + x * 2 + z),
    ]
    return cube, y * 8 + x * 2 + (1 - z)


def mp_places():
    mp = lax.axis_index("mp")
    zl, core = mp // 2, mp % 2
    return mp, zl, core, zl * 2 + (1 - core), (1 - zl) * 2 + core


class Flight:
    def __init__(self, links, cp, send, recv):
        self.links, self.cp, self.send, self.recv = links, cp, send, recv

    def wait_send(self):
        self.cp.wait_send()
        self.links.spare.append(self.send)

    def wait_recv(self):
        self.cp.wait_recv()

    def wait(self):
        self.wait_send()
        self.wait_recv()


class Links:
    def __init__(self, ssem, rsem):
        self.ssem, self.rsem, self.spare, self.sends, self.recvs = ssem, rsem, [], 0, 0

    def start(self, src, dst, place, like=None):
        if self.spare:
            k = self.spare.pop(0)
        else:
            k, self.sends = self.sends, self.sends + 1
        if like is not None:
            r = like.recv
        else:
            r, self.recvs = self.recvs, self.recvs + 1
        cp = pltpu.make_async_remote_copy(
            src_ref=src, dst_ref=dst, send_sem=self.ssem.at[k], recv_sem=self.rsem.at[r],
            device_id=place, device_id_type=MESH,
        )
        cp.start()
        return Flight(self, cp, k, r)

    def mp(self, src, dst, peer):
        return self.start(src, dst, (lax.axis_index("dp"), peer))

    def dp(self, src, dst, peer, like=None):
        return self.start(src, dst, (peer, lax.axis_index("mp")), like)


def loop(total, step, body, init=None):
    def run(i, carry):
        return body(pl.multiple_of(i * step, step), carry)

    return lax.fori_loop(0, total // step, run, init)


def each(total, step, body):
    def run(r, carry):
        body(r)
        return carry

    loop(total, step, run, 0)


def add_into(dst, dst_at, src, src_at, rows):
    step = 128 if rows % 128 == 0 else 64 if rows % 64 == 0 else 16

    def body(r):
        to, at = dst_at(r, step), src_at(r, step)
        dst[to] = dst[to] + src[at]

    each(rows, step, body)


def quarters(row0, rows, orders):
    return [(row0, rows, 256 * q, 256, order) for q, order in enumerate(orders)]


CUBE_FIRST = ((0, 1, 2, 3, 4), (1, 2, 3, 0, 4), (2, 3, 0, 1, 4), (3, 0, 1, 2, 4))
Z_FIRST = ((4, 0, 1, 2, 3), (4, 1, 2, 3, 0), (4, 2, 3, 0, 1), (4, 3, 0, 1, 2))


class Pieces:
    last = 8

    def __init__(self, links, ref, recv, base, free, pieces):
        self.links, self.ref, self.recv, self.base, self.free, self.pieces = links, ref, recv, base, free, pieces
        cube, zp = dp_places()
        self.dims = cube + [(lax.axis_index("dp") % 2, zp)]
        self.cur, self.old = [p[0] for p in pieces], [[] for _ in pieces]
        self.flying, self.sent, self.stage, self.out = [None] * len(pieces), [], 0, [[] for _ in pieces]

    def launch(self, i, s):
        row0, n, col0, width, order = self.pieces[i]
        cols, cur = pl.ds(col0, width), self.cur
        at = self.base + row0 + n - (n >> s)
        if s < 4:
            bit, peer = self.dims[order[s]]
            half = n >> (s + 1)
            give = pl.multiple_of(cur[i] + (1 - bit) * half, 16)
            self.old[i].append(cur[i])
            cur[i] = pl.multiple_of(cur[i] + bit * half, 16)
            cp = self.links.dp(self.ref.at[pl.ds(give, half), cols], self.recv.at[pl.ds(at, half), cols], peer)
        elif s == 4:
            size = n >> 4
            cp = self.links.dp(
                self.ref.at[pl.ds(cur[i], size), cols], self.recv.at[pl.ds(at, size), cols], self.dims[order[4]][1]
            )
        else:
            k = 8 - s
            here = self.ref.at[pl.ds(cur[i], n >> (k + 1)), cols]
            cp = self.links.dp(here, here, self.dims[order[k]][1], self.out[i][k])
            cur[i] = self.old[i][k]
        self.out[i].append(cp)
        self.flying[i] = cp

    def begin(self):
        for i in range(len(self.pieces)):
            self.launch(i, 0)

    def advance(self):
        s = self.stage
        if s == 4:
            pl.semaphore_wait(self.free, 5)
        earlier, self.sent = self.sent, []
        for i, (row0, n, col0, width, _) in enumerate(self.pieces):
            cp, cols = self.flying[i], pl.ds(col0, width)
            if s == 4:
                cp.wait_send()
            else:
                self.sent.append(cp)
            cp.wait_recv()
            if s <= 4:
                at, here = self.base + row0 + n - (n >> s), self.cur[i]
                add_into(
                    self.ref, lambda r, m: (pl.ds(here + r, m), cols),
                    self.recv, lambda r, m: (pl.ds(at + r, m), cols), n >> min(s + 1, 4),
                )
            if s < 8:
                self.launch(i, s + 1)
        for cp in earlier:
            cp.wait_send()
        if s == 3:
            for cp in self.sent:
                cp.wait_send()
            self.sent = []
            for _, peer in self.dims:
                pl.semaphore_signal(self.free, inc=1, device_id=(peer, lax.axis_index("mp")), device_id_type=MESH)
        self.stage += 1

    def finish(self):
        for cp in self.sent:
            cp.wait_send()


DOWN_PIECES = quarters(0, 1024, CUBE_FIRST)
UP_PIECES = quarters(0, 1024, CUBE_FIRST)
SQ_PIECES = quarters(0, 256, CUBE_FIRST) + quarters(256, 512, Z_FIRST)


class Strips:
    last = 9

    def __init__(self, links, ref, recv, pack, got, free):
        self.links, self.ref, self.recv, self.pack, self.got, self.free = links, ref, recv, pack, got, free
        self.cube, self.zp = dp_places()
        self.cur, self.old = [0] * 4, [[] for _ in range(4)]
        self.flying, self.sent, self.stage, self.out = [], [], 0, []

    def launch(self, s):
        ref, cur = self.ref, self.cur
        self.flying = []
        for j in range(STRIPS):
            q, cols = j % 4, pl.ds(128 * j, 128)
            if s < 4:
                bit, peer = self.cube[(q + s) % 4]
                half = 256 >> (s + 1)
                give = pl.multiple_of(cur[q] + (1 - bit) * half, 16)
                cp = self.links.dp(
                    ref.at[:, pl.ds(give, half), cols], self.recv.at[:, pl.ds(256 - (256 >> s), half), cols], peer
                )
            elif s == 4:
                cp = self.links.dp(ref.at[:, pl.ds(cur[q], 16), cols], self.recv.at[:, pl.ds(240, 16), cols], self.zp)
            else:
                k = 9 - s
                bit, peer = self.cube[(q + k) % 4]
                here = ref.at[:, pl.ds(cur[q], 256 >> (k + 1)), cols]
                cp = self.links.dp(here, here, peer, self.out[k][j])
            self.flying.append(cp)
        self.out.append(self.flying)
        for q in range(4):
            if s < 4:
                bit, _ = self.cube[(q + s) % 4]
                self.old[q].append(cur[q])
                cur[q] = pl.multiple_of(cur[q] + bit * (256 >> (s + 1)), 16)
            elif s > 4:
                cur[q] = self.old[q][9 - s]

    def begin(self):
        self.launch(0)

    def advance(self):
        s = self.stage
        if s > 9:
            return
        mp, zl, core, part, far = mp_places()
        earlier, self.sent = self.sent, []
        if s == 5:
            for cp in self.flying:
                cp.wait()
            self.got[mp] = self.pack[mp]
            for j in range(STRIPS):
                self.ref[:, pl.ds(self.cur[j % 4], 16), pl.ds(128 * j, 128)] = self.got[:, j]
            pl.semaphore_wait(self.free, 4)
            self.launch(6)
        else:
            for j, cp in enumerate(self.flying):
                cols = pl.ds(128 * j, 128)
                if s == 4:
                    cp.wait_send()
                else:
                    self.sent.append(cp)
                cp.wait_recv()
                if s <= 4:
                    rows, at, here = 256 >> min(s + 1, 4), 256 - (256 >> s), self.cur[j % 4]
                    add_into(
                        self.ref, lambda r, m: (slice(None), pl.ds(here + r, m), cols),
                        self.recv, lambda r, m: (slice(None), pl.ds(at + r, m), cols), rows,
                    )
            if s == 3:
                for cp in self.sent:
                    cp.wait_send()
                self.sent = []
                for _, peer in self.cube:
                    pl.semaphore_signal(self.free, inc=1, device_id=(peer, mp), device_id_type=MESH)
            if s == 4:
                for j in range(STRIPS):
                    self.pack[:, j] = self.ref[:, pl.ds(self.cur[j % 4], 16), pl.ds(128 * j, 128)]
                self.flying = [self.links.mp(self.pack.at[peer], self.got.at[mp], peer) for peer in (part, far, 3 - mp)]
            elif s < 9:
                self.launch(s + 1)
        for cp in earlier:
            cp.wait_send()
        self.stage += 1

    def finish(self):
        for cp in self.sent:
            cp.wait_send()


class Smalls:
    last = 6

    def __init__(self, links, ref, recv):
        self.links, self.ref, self.recv, self.stage = links, ref, recv, 0
        cube, zp = dp_places()
        self.peers = [peer for _, peer in cube] + [zp]

    def begin(self):
        s = self.stage
        mp, zl, core, part, far = mp_places()
        self.rows = pl.ds(0, 16 if s < 5 else 8)
        src, dst = self.ref.at[self.rows], self.recv.at[s, self.rows]
        if s < 5:
            self.cp = self.links.dp(src, dst, self.peers[s])
        else:
            self.cp = self.links.mp(src, dst, (part, far)[s - 5])

    def advance(self):
        if self.stage > 6:
            return
        self.cp.wait()
        self.ref[self.rows, :] = self.ref[self.rows, :] + self.recv[self.stage, self.rows, :]
        self.stage += 1
        if self.stage <= 6:
            self.begin()

    def finish(self):
        pass


def dg(a, b, left=1, right=0):
    return lax.dot_general(a, b, (((left,), (right,)), ((), ())), preferred_element_type=F32)


def normalize(rows):
    centre = rows - jnp.mean(rows, axis=-1, keepdims=True)
    inv = lax.rsqrt(jnp.mean(centre * centre, axis=-1, keepdims=True) + EPS)
    return centre * inv, inv


def norm_back(grad, gain, unit, inv):
    g = grad * gain
    return inv * (g - jnp.mean(g, axis=-1, keepdims=True) - unit * jnp.mean(g * unit, axis=-1, keepdims=True))


def iota(shape, dim):
    return lax.broadcasted_iota(jnp.int32, shape, dim)


def fold(x, op):
    out = x[:8]
    for i in range(1, x.shape[0] // 8):
        out = op(out, x[8 * i : 8 * i + 8])
    return out


def layer_body(
    seg_in, mem_in, old_in, gout_in, wq_in, wkv_in, wo_in, wup_in, wdn_in, wsq_in,
    mfill, sfill, slopes, again, fgain, ubias,
    lout_out, sqz_out, gin_out, down_out, up_out, sq_out, out_out, t_out, s_out,
    raw, normed, wkvq, wo, wup, wdn, wsq, kv, query, expo, tmp, tmp2, stat, acc, mixt, mixg, mid, nm, hid, gpre,
    out, got, keep, out2, got2, gb, gmix, gkv, gq, win, sqz, skv, esq, gsq, rec, sbuf, sgot, sqsum, trecv, tpack, tgot, srecv,
    x_down, x_up, x_sq, x_out, t_ref, s_ref, lout, gin, lsem, free, ssem, rsem,
):
    links = Links(ssem, rsem)
    mp, zl, core, part, far = mp_places()
    diag = 3 - mp
    cube, zp = dp_places()
    dp = lax.axis_index("dp")
    mine = pl.ds(pl.multiple_of(mp * 256, 256), 256)

    ins = {SEG: seg_in, MEM: mem_in, OLD: old_in, GOUT: gout_in}
    own_loads = {}
    nlocal = [0]

    def load(src, dst):
        cp = pltpu.make_async_copy(src, dst, lsem.at[nlocal[0]])
        nlocal[0] += 1
        cp.start()
        return cp

    for a in (SEG, MEM, OLD, GOUT):
        own_loads[a] = load(ins[a], raw.at[a, mp])
    w_loads = [
        load(wkv_in.at[:, mine], wkvq.at[:, pl.ds(0, 256)]),
        load(wkv_in.at[:, pl.ds(pl.multiple_of(D + mp * 256, 256), 256)], wkvq.at[:, pl.ds(256, 256)]),
        load(wq_in.at[:, mine], wkvq.at[:, pl.ds(512, 256)]),
    ]

    sem = pltpu.get_barrier_semaphore()
    for peer in [peer for _, peer in cube] + [zp]:
        pl.semaphore_signal(sem, inc=1, device_id=(peer, mp), device_id_type=MESH)
    for peer in (part, far, diag):
        pl.semaphore_signal(sem, inc=1, device_id=(dp, peer), device_id_type=MESH)
    pl.semaphore_wait(sem, 8)

    done = []

    far_cp, part_cp, fwd_cp = {}, {}, {}
    sq_load = load(wsq_in, wsq)
    late_loads = [load(wo_in, wo), load(wup_in, wup), load(wdn_in, wdn)]
    mem_limit = M - mfill[0]
    old_limit = C - sfill[0]

    def slope_of(h):
        return slopes[mp * 2 + h]

    def heads(h):
        return pl.ds(h * DH, DH)

    def column(r, rows):
        return iota((rows, 1), 0) + r

    def exponentials(src, dst, dst0, rows, colmask, causal=False):
        step = 64

        def one(r, top):
            s = src[pl.ds(r, step), :] * SCALE + colmask(r, step)
            if causal:
                s = jnp.where(iota((step, 512), 0) + r <= iota((step, 512), 1), s, NEG)
            src[pl.ds(r, step), :] = s
            return jnp.maximum(top, fold(s, jnp.maximum))

        top = loop(rows, step, one, jnp.full((8, 512), NEG, F32))
        top = jnp.max(top, axis=0, keepdims=True)

        def two(r, total):
            e = jnp.exp(src[pl.ds(r, step), :] - top).astype(BF)
            dst[pl.ds(dst0 + r, step), :] = e
            return total + fold(e.astype(F32), jnp.add)

        total = loop(rows, step, two, jnp.zeros((8, 512), F32))
        return top, jnp.sum(total, axis=0, keepdims=True)

    def attend(h, a):
        base = BASE[a]
        rows = pl.ds(base, 512)
        g = base // 512
        tmp[...] = dg(kv[rows, heads(h)], query[:, heads(h)], 1, 1)
        slope = slope_of(h)

        def colmask(r, step):
            j = column(r, step)
            bias = slope * (j + (base - 1536)).astype(F32)
            if a == MEM:
                bias = jnp.where(j >= mem_limit, bias, NEG)
            if a == OLD:
                bias = jnp.where(j >= old_limit, bias, NEG)
            return bias

        top, total = exponentials(tmp, expo.at[h], base, 512, colmask, a == SEG)
        stat[h * 6 + g : h * 6 + g + 1, :] = top
        stat[h * 6 + 3 + g : h * 6 + 4 + g, :] = total
        acc[h * 3 + g] = dg(kv[rows, pl.ds(256 + h * DH, DH)], expo[h, rows, :], 0, 0)

    def first_of(h):
        rows = pl.ds(BASE[MEM], 512)
        tmp[...] = dg(kv[rows, heads(h)], query[:, heads(h)], 1, 1)
        _, total = exponentials(
            tmp, gkv, 0, 512, lambda r, step: jnp.where(column(r, step) >= mem_limit, 0.0, NEG)
        )
        rec[heads(h), :] = dg(kv[rows, pl.ds(256 + h * DH, DH)], gkv[0:512, :], 0, 0) / total

    tasks, ran = {}, set()

    def task(name, *after):
        def keep_it(run):
            tasks[name] = (run, after)
            return run

        return keep_it

    sums = {
        "D": Pieces(links, x_down, wsq, 0, free.at[1], DOWN_PIECES),
        "U": Pieces(links, x_up, wsq, 1024, free.at[2], UP_PIECES),
        "Q": Pieces(links, x_sq, wsq, 2048, free.at[3], SQ_PIECES),
        "O": Pieces(links, x_out, wsq, 2816, free.at[4], quarters(0, 256, [CUBE_FIRST[q] for q in (2, 3, 2, 3)])),
        "T": Strips(links, t_ref, trecv, tpack, tgot, free.at[5]),
        "S": Smalls(links, s_ref, srecv),
    }
    results = {"D": (x_down, down_out), "U": (x_up, up_out), "Q": (x_sq, sq_out), "O": (x_out, out_out), "T": (t_ref, t_out), "S": (s_ref, s_out)}
    flights = {}
    leaving, roomy = [], []
    bias_rows = [jnp.zeros((8, 512), F32)] * 2
    totals = {"gain": jnp.zeros((1, D), F32), "slope": jnp.zeros((1, D), F32), "bias": bias_rows}

    def begin(name):
        if not roomy:
            pl.semaphore_wait(free.at[0], 5)
            roomy.append(True)
        sums[name].begin()

    def half_rows(z):
        return pl.ds(z * 256, 256)

    def block(z, other):
        return pl.ds(pl.multiple_of((2 * z + ((1 - core) if other else core)) * 128, 128), 128)

    waited = set()

    def once(name, copies):
        if name not in waited:
            waited.add(name)
            for cp in copies:
                cp.wait()

    def norm_rows(a, owner):
        unit, _ = normalize(raw[a, owner].astype(F32))
        normed[pl.ds(pl.multiple_of(BASE[a] + owner * 128, 128), 128), :] = (unit * again[...]).astype(BF)

    def send_rows(a, copies, peer):
        copies[a] = links.mp(ins[a], raw.at[a, mp], peer)
        done.append(copies[a])

    def norm_own(a):
        own_loads[a].wait()
        norm_rows(a, mp)

    def norm_part(a):
        part_cp[a].wait_recv()
        norm_rows(a, part)

    def arrive(a):
        far_cp[a].wait_recv()
        fwd_cp[a] = links.mp(raw.at[a, far], raw.at[a, far], part)
        done.append(fwd_cp[a])

    def norm_diag(a):
        fwd_cp[a].wait_recv()
        norm_rows(a, diag)

    def project(a, chip):
        once("wkvq", w_loads)
        own = pl.ds(pl.multiple_of(chip * 256, 256), 256)
        rows = pl.ds(pl.multiple_of(BASE[a] + chip * 256, 256), 256)
        kv[rows, :] = dg(normed[rows, :], wkvq[:, 0:512]).astype(BF)
        if a == SEG:
            query[own, :] = dg(normed[rows, :], wkvq[:, 512:768]).astype(BF)

    for c, a in (("s", SEG), ("m", MEM), ("o", OLD), ("g", GOUT)):
        task(f"send.{c}")(functools.partial(send_rows, a, far_cp, far))
        task(f"psend.{c}")(functools.partial(send_rows, a, part_cp, part))
        task(f"arr.{c}", f"send.{c}")(functools.partial(arrive, a))
        if a != GOUT:
            task(f"own.{c}")(functools.partial(norm_own, a))
            task(f"par.{c}", f"psend.{c}")(functools.partial(norm_part, a))
            task(f"far.{c}", f"arr.{c}")(functools.partial(norm_rows, a, far))
            task(f"dia.{c}", f"arr.{c}")(functools.partial(norm_diag, a))
            task(f"pjo.{c}", f"own.{c}", f"par.{c}")(functools.partial(project, a, zl))
            task(f"pjf.{c}", f"far.{c}", f"dia.{c}")(functools.partial(project, a, 1 - zl))
            for h in range(2):
                task(f"at.{c}.{h}", f"pjo.{c}", f"pjf.{c}", "pjo.s", "pjf.s")(functools.partial(attend, h, a))

    @task("combine", *(f"at.{c}.{h}" for c in "smo" for h in range(2)))
    def _():
        for h in range(2):
            tops = [stat[h * 6 + g : h * 6 + g + 1, :] for g in range(3)]
            sums = [stat[h * 6 + 3 + g : h * 6 + 4 + g, :] for g in range(3)]
            top = jnp.maximum(jnp.maximum(tops[0], tops[1]), tops[2])
            scales = [jnp.exp(t - top) for t in tops]
            total = scales[0] * sums[0] + scales[1] * sums[1] + scales[2] * sums[2]
            mixed = jnp.zeros((DH, 512), F32)
            for g in range(3):
                inv = scales[g] / total
                stat[12 + h * 3 + g : 13 + h * 3 + g, :] = inv
                mixed = mixed + acc[h * 3 + g] * inv
            mixt[heads(h), :] = mixed
            mixg[mp, :, heads(h)] = mixed.T.astype(BF)
        for z in range(2):
            here = mixg.at[mp, half_rows(z)]
            flights["mix_part", z] = links.mp(here, here, part)
            done.append(flights["mix_part", z])
        send_mix(0)

    def send_mix(z):
        here = mixg.at[mp, half_rows(z)]
        flights["mix_far", z] = links.mp(here, here, far)
        done.append(flights["mix_far", z])

    task("mf1", "combine")(functools.partial(send_mix, 1))

    @task("squeeze", "dia.m")
    def _():
        sq_load.wait()
        rows = raw[MEM].reshape(512, D)
        for tap in range(3):
            pick = (iota((CP, 512), 1) == 3 * iota((CP, 512), 0) + tap).astype(BF)
            win[:, tap * D : (tap + 1) * D] = dg(pick, rows).astype(BF)
        for half in range(2):
            cols = pl.ds(half * 512, 512)
            sqz[:, cols] = dg(win[...], wsq[:, cols])
        for peer in [peer for _, peer in cube] + [zp]:
            pl.semaphore_signal(free.at[0], inc=1, device_id=(peer, mp), device_id_type=MESH)

    @task("r1", "squeeze")
    def _():
        pick = (iota((48, CP), 1) == iota((48, CP), 0) + mp * 43).astype(BF)
        sqz_out[...] = dg(pick, sqz[...].astype(BF))[0:43].astype(BF)
        unit, _ = normalize(sqz[...])
        skv[...] = dg((unit * again[...]).astype(BF), wkvq[:, 0:512]).astype(BF)

    for h in range(2):
        task(f"f{h}", "pjo.m", "pjf.m", "pjo.s", "pjf.s")(functools.partial(first_of, h))

    def second_of(h):
        keys, values = skv[:, heads(h)], skv[:, pl.ds(256 + h * DH, DH)]
        tmp[0:CP, :] = dg(keys, query[:, heads(h)], 1, 1)

        def colmask(r, step):
            slot = column(r, step)
            return jnp.where((3 * slot < M) & (3 * slot + 2 >= mem_limit), 0.0, NEG)

        _, total = exponentials(tmp, esq, 0, CP, colmask)
        inv = 1.0 / total
        second = dg(values, esq[...], 0, 0) * inv
        grad = (rec[heads(h), :] - second) * RECON
        inner = inv * jnp.sum(grad * second, axis=0, keepdims=True)
        scaled = (grad * inv).astype(BF)
        gsq[:, pl.ds(256 + h * DH, DH)] = dg(esq[...], scaled, 1, 1).astype(BF)
        gp = dg(values, scaled)
        gs = (esq[...].astype(F32) * (gp - inner)).astype(BF)
        gsq[:, heads(h)] = (dg(gs, query[:, heads(h)]) * SCALE).astype(BF)

    for h in range(2):
        task(f"s{h}", "r1", f"f{h}", "pjo.s", "pjf.s")(functools.partial(second_of, h))

    @task("dsq", "s0", "s1")
    def _():
        unit, inv = normalize(sqz[...])
        sqz[...] = norm_back(dg(gsq[...], wkvq[:, 0:512], 1, 1), again[...], unit, inv)
        sbuf[0] = sqz[pl.ds(pl.multiple_of((1 - core) * 96, 16), 96), :].astype(BF)
        flights["sq_part"] = links.mp(sbuf.at[0], sgot.at[0], part)
        done.append(flights["sq_part"])

    @task("sqS", "dsq")
    def _():
        flights["sq_part"].wait_recv()
        sbuf[1] = (sqz[pl.ds(pl.multiple_of(core * 96, 16), 96), :] + sgot[0].astype(F32)).astype(BF)
        flights["sq_far"] = links.mp(sbuf.at[1], sgot.at[1], far)

    @task("sqT", "sqS")
    def _():
        flights["sq_far"].wait()
        sqsum[core] = (sbuf[1].astype(F32) + sgot[1].astype(F32)).astype(BF)
        flights["sq_back"] = links.mp(sqsum.at[core], sqsum.at[core], part)

    @task("xsq", "sqT")
    def _():
        flights["sq_back"].wait()
        for half in range(2):
            cols = pl.ds(half * 512, 512)
            x_sq[:, cols] = dg(win[:, pl.ds(pl.multiple_of(mp * 768, 256), 768)], sqsum[:, :, cols].reshape(CP, 512), 0, 0).astype(BF)
        begin("Q")

    def mix_into(z, owners, first=False):
        rows = half_rows(z)
        for half in range(2):
            cols = pl.ds(half * 512, 512)
            base = raw[SEG, 2 * z : 2 * z + 2, :, cols].reshape(256, 512).astype(F32) if first else mid[rows, cols]
            for owner in owners:
                base = base + dg(mixg[owner, rows, :], wo[pl.ds(pl.multiple_of(owner * 256, 256), 256), cols])
            mid[rows, cols] = base

    def mix_own(z):
        once("weights", late_loads)
        flights["mix_part", z].wait_recv()
        mix_into(z, (mp, part), True)

    def forward_mix(z):
        flights["mix_far", z].wait_recv()
        here = mixg.at[far, half_rows(z)]
        flights["mix_fwd", z] = links.mp(here, here, part)
        done.append(flights["mix_fwd", z])

    def grad_hidden(z):
        once("weights", late_loads)
        if z == 0:
            own_loads[GOUT].wait()
            part_cp[GOUT].wait_recv()
            fwd_cp[GOUT].wait_recv()
        for half in range(2):
            cols = pl.ds(half * 512, 512)
            keep[z, :, :, cols] = dg(raw[GOUT, 2 * z : 2 * z + 2].reshape(256, D), wdn[cols, :], 1, 1).reshape(2, 128, 512)

    def feed_forward(z):
        flights["mix_fwd", z].wait_recv()
        mix_into(z, (diag,))
        rows = half_rows(z)
        for i in range(2):
            at = pl.ds(z * 256 + i * 128, 128)
            unit, _ = normalize(mid[at, :])
            nm[at, :] = (unit * fgain[...]).astype(BF)
        for half in range(2):
            cols = pl.ds(half * 512, 512)
            tmp[half_rows(half), :] = dg(nm[rows, :], wup[:, cols])
        for half, i in ((0, 0), (0, 1), (1, 0), (1, 1)):
            cols = pl.ds(half * 512, 512)

            def gelu(r, total):
                to = pl.ds(r + z * 256 + i * 128, 64)
                v = tmp[pl.ds(r + half * 256 + i * 128, 64), :] + ubias[:, cols]
                square = v * v
                th = jnp.tanh(0.7978845608028654 * v * (1.0 + 0.044715 * square))
                hid[to, cols] = (0.5 * v * (1.0 + th)).astype(BF)
                slope = 0.5 * (1.0 + th) + (0.5 * 0.7978845608028654) * v * (1.0 - th * th) * (1.0 + 3 * 0.044715 * square)
                g = (slope * keep[z, i, pl.ds(r, 64), cols]).astype(BF)
                gpre[to, cols] = g
                return total + fold(g.astype(F32), jnp.add)

            totals["bias"][half] = loop(128, 64, gelu, totals["bias"][half])
        if z == 1:
            for half in range(2):
                s_ref[8:9, pl.ds(half * 512, 512)] = jnp.sum(totals["bias"][half], axis=0, keepdims=True)

    for z in range(2):
        task(f"mix{z}a", "combine", *(["mix0a"] if z else []))(functools.partial(mix_own, z))
        task(f"fw{z}", "combine", *(["fw0", "mf1"] if z else []))(functools.partial(forward_mix, z))
        task(f"gh{z}", "arr.g", "psend.g", *(["gh0"] if z else []))(functools.partial(grad_hidden, z))
        task(f"mix{z}b", f"mix{z}a", f"fw{z}")(functools.partial(mix_into, z, (far,)))
        task(f"ffn{z}", f"mix{z}b", f"gh{z}", *(["ffn0"] if z else []))(functools.partial(feed_forward, z))

    def tiles(dst, left, right):
        for half in range(2):
            rows = pl.ds(half * 512, 512)
            for quarter in range(2):
                cols = pl.ds(quarter * 512, 512)
                dst[rows, cols] = dg(left(rows), right(cols), 0, 0).astype(BF)

    @task("down", "ffn1", "squeeze")
    def _():
        tiles(x_down, lambda rows: hid[:, rows], lambda cols: raw[GOUT, :, :, cols].reshape(512, 512))
        begin("D")

    @task("up", "ffn1", "squeeze")
    def _():
        tiles(x_up, lambda rows: nm[:, rows], lambda cols: gpre[:, cols])
        begin("U")

    @task("gnmo", "ffn1")
    def _():
        for z in range(2):
            out[0, z] = dg(gpre[block(z, True), :], wup[...], 1, 1).astype(BF)
            flights["gnm_part", z] = links.mp(out.at[0, z], got.at[0, z], part)

    @task("gnmw", "gnmo")
    def _():
        for z in range(2):
            keep[0, z] = dg(gpre[block(z, False), :], wup[...], 1, 1)

    def gnm_sum(z):
        flights["gnm_part", z].wait_recv()
        out2[z] = (keep[0, z] + got[0, z].astype(F32)).astype(BF)
        flights["gnm_far", z] = links.mp(out2.at[z], got2.at[z], far)

    @task("dno", "ffn1")
    def _():
        for z in range(2):
            out[1, z] = dg(hid[block(z, True), :], wdn[...]).astype(BF)
            flights["down_part", z] = links.mp(out.at[1, z], got.at[1, z], part)
            done.append(flights["down_part", z])

    @task("dnw", "ffn1")
    def _():
        for z in range(2):
            keep[1, z] = dg(hid[block(z, False), :], wdn[...])

    @task("dnS", "dno", "dnw")
    def _():
        for z in range(2):
            flights["down_part", z].wait_recv()
        out2[2] = (keep[1, 1 - zl] + got[1, 1 - zl].astype(F32)).astype(BF)
        flights["down_far"] = links.mp(out2.at[2], got2.at[2], far)

    @task("lout", "dnS")
    def _():
        flights["down_far"].wait()
        lout[...] = (
            mid[pl.ds(pl.multiple_of(mp * 128, 128), 128), :]
            + keep[1, zl] + got[1, zl].astype(F32) + got2[2].astype(F32)
        ).astype(BF)
        leaving.append(load(lout, lout_out))

    def norm_mid_back(z):
        flights["gnm_far", z].wait()
        rows = block(z, False)
        unit, inv = normalize(mid[rows, :])
        g = out2[z].astype(F32) + got2[z].astype(F32)
        totals["gain"] = totals["gain"] + jnp.sum(g * unit, axis=0, keepdims=True) * jnp.where(zl == z, 1.0, 0.0)
        gmid = raw[GOUT, 2 * z + core].astype(F32) + norm_back(g, fgain[...], unit, inv)
        keep[0, z] = gmid
        gb[z, core] = gmid.astype(BF)
        flights["gb", z] = links.mp(gb.at[z, core], gb.at[z, core], part)
        if z == 1:
            s_ref[1:2, :] = totals["gain"]

    for z in range(2):
        task(f"gS{z}", "gnmw", *(["gS0"] if z else []))(functools.partial(gnm_sum, z))
        task(f"lnb{z}", f"gS{z}", *(["lnb0"] if z else []))(functools.partial(norm_mid_back, z))

    @task("xout", "lnb1", "squeeze")
    def _():
        for z in range(2):
            flights["gb", z].wait()
        gmix[...] = dg(wo[mine, :], gb[...].reshape(512, D), 1, 1)
        for half in range(2):
            cols = pl.ds(half * 512, 512)
            x_out[:, cols] = dg(mixg[mp], gb[:, :, :, cols].reshape(512, 512), 0, 0).astype(BF)
        begin("O")

    carried = {}

    def attend_back(h, a):
        base = BASE[a]
        rows = pl.ds(base, 512)
        grad = gmix[heads(h), :]
        if a == OLD:
            carried["inner"] = jnp.sum(grad * mixt[heads(h), :], axis=0, keepdims=True)
            carried["slope"] = jnp.zeros((8, 512), F32)
        inv = stat[12 + h * 3 + base // 512 : 13 + h * 3 + base // 512, :]
        scaled = (grad * inv).astype(BF)
        shift = inv * carried["inner"]
        tmp[...] = dg(kv[rows, pl.ds(256 + h * DH, DH)], scaled)
        gkv[rows, pl.ds(256 + h * DH, DH)] = dg(expo[h, rows, :], scaled, 1, 1).astype(BF)

        def score_grads(r, total):
            at = pl.ds(base + r, 64)
            gs = (expo[h, at, :].astype(F32) * (tmp[pl.ds(r, 64), :] - shift)).astype(BF)
            expo[h, at, :] = gs
            dist = (iota((64, 512), 1) - iota((64, 512), 0) + (1024 - base - r)).astype(F32)
            return total + fold(gs.astype(F32) * dist, jnp.add)

        carried["slope"] = loop(512, 64, score_grads, carried["slope"])
        gkv[rows, heads(h)] = (dg(expo[h, rows, :], query[:, heads(h)]) * SCALE).astype(BF)
        if a == SEG:
            gqt = dg(kv[:, heads(h)], expo[h], 0, 0)
            gq[:, heads(h)] = (gqt * SCALE).T.astype(BF)
            value = -jnp.sum(jnp.sum(carried["slope"], axis=0, keepdims=True), axis=1, keepdims=True)
            totals["slope"] = totals["slope"] + jnp.where(iota((1, D), 1) == mp * 2 + h, value, 0.0)

    before = ("xout", "f0", "f1")
    for h in range(2):
        for name, a in ((f"att{h}.0", OLD), (f"att{h}.1", MEM), (f"att{h}", SEG)):
            task(name, *before)(functools.partial(attend_back, h, a))
            before = (name,)

    def projections(b):
        feats = pl.ds(b * 256, 256)
        big = dg(normed[:, feats], gkv[...], 0, 0)
        small = dg(normed[1024:1536, feats], gq[...], 0, 0)
        t_ref[b, :, 0:512] = big.astype(BF)
        t_ref[b, :, 512:768] = small.astype(BF)
        terms = small[:, 0:128] * wkvq[feats, 512:640].astype(F32) + small[:, 128:256] * wkvq[feats, 640:768].astype(F32)
        for j in range(4):
            terms = terms + big[:, j * 128 : (j + 1) * 128] * wkvq[feats, j * 128 : (j + 1) * 128].astype(F32)
        s_ref[0:1, feats] = jnp.sum(terms.T, axis=0, keepdims=True) / again[:, feats]
        if b == 3:
            begin("T")
            s_ref[2:3, :] = totals["slope"]
            s_ref[3:8, :] = jnp.zeros((5, D), F32)
            s_ref[9:16, :] = jnp.zeros((7, D), F32)
            begin("S")

    for b in range(4):
        task(("t.0", "t.1", "t.2", "t")[b], "att1", *([("t.0", "t.1", "t.2")[b - 1]] if b else []))(functools.partial(projections, b))

    def seg_terms(z, other):
        rows = block(z, other)
        at = pl.ds(pl.multiple_of(BASE[SEG] + (2 * z + ((1 - core) if other else core)) * 128, 128), 128)
        return dg(gkv[at, :], wkvq[:, 0:512], 1, 1) + dg(gq[rows, :], wkvq[:, 512:768], 1, 1)

    @task("sego", "att1")
    def _():
        for z in range(2):
            flights["gnm_part", z].wait_send()
            out[0, z] = seg_terms(z, True).astype(BF)
            flights["seg_part", z] = links.mp(out.at[0, z], got.at[0, z], part)
            done.append(flights["seg_part", z])

    @task("segw", "att1")
    def _():
        for z in range(2):
            terms = seg_terms(z, False)
            for half in range(2):
                tmp2[(2 * z + half) * 128 : (2 * z + half + 1) * 128, :] = terms[:, half * 512 : (half + 1) * 512]

    @task("segS", "sego", "segw")
    def _():
        for z in range(2):
            flights["seg_part", z].wait_recv()
        for half in range(2):
            cols = pl.ds(half * 512, 512)
            at = pl.ds(pl.multiple_of((2 * (1 - zl) + half) * 128, 128), 128)
            out2[3, :, cols] = (tmp2[at, :] + got[0, 1 - zl, :, cols].astype(F32)).astype(BF)
        flights["seg_far"] = links.mp(out2.at[3], got2.at[3], far)

    @task("gin", "segS")
    def _():
        flights["seg_far"].wait()
        unit, inv = normalize(raw[SEG, mp].astype(F32))
        own = [tmp2[pl.ds(pl.multiple_of((2 * zl + half) * 128, 128), 128), :] for half in range(2)]
        total = jnp.concatenate(own, axis=1) + got[0, zl].astype(F32) + got2[3].astype(F32)
        gin[...] = keep[0, zl] + norm_back(total, again[...], unit, inv)
        leaving.append(load(gin, gin_out))

    for name in ORDER:
        if name in tasks:
            run, after = tasks[name]
            assert all(other in ran for other in after), name
            run()
        else:
            part_sum = sums[name[0]]
            assert part_sum.stage == int(name[1:]), name
            part_sum.advance()
            if part_sum.stage > part_sum.last:
                leaving.append(load(*results[name[0]]))
        ran.add(name)
    assert len(ran) == len(tasks) + sum(part_sum.last + 1 for part_sum in sums.values())
    for part_sum in sums.values():
        part_sum.finish()
    for cp in leaving:
        cp.wait()
    for cp in done:
        cp.wait_send()
    assert links.sends <= SENDS and links.recvs <= RECVS, (links.sends, links.recvs)


def layer(args):
    def out_shape(shape, dtype):
        return jax.ShapeDtypeStruct(shape, dtype)

    outs = (
        out_shape((128, D), BF), out_shape((43, D), BF), out_shape((128, D), F32), out_shape((1024, D), BF),
        out_shape((1024, D), BF), out_shape((768, D), BF), out_shape((256, D), BF), out_shape((4, 256, 768), BF),
        out_shape((16, D), F32),
    )
    v = pltpu.VMEM
    scratch = [
        v((4, 4, 128, D), BF), v((1536, D), BF), v((D, 768), BF), v((D, D), BF), v((D, D), BF), v((D, D), BF),
        v((3072, D), BF), v((1536, 512), BF), v((512, 256), BF), v((2, 1536, 512), BF), v((512, 512), F32),
        v((512, 512), F32), v((24, 512), F32), v((6, DH, 512), F32), v((256, 512), F32), v((4, 512, 256), BF),
        v((512, D), F32), v((512, D), BF), v((512, D), BF), v((512, D), BF),
        v((2, 2, 128, D), BF), v((2, 2, 128, D), BF), v((2, 2, 128, D), F32), v((4, 128, D), BF), v((4, 128, D), BF),
        v((2, 2, 128, D), BF), v((256, 512), F32), v((1536, 512), BF), v((512, 256), BF),
        v((CP, 3 * D), BF), v((CP, D), F32), v((CP, 512), BF), v((CP, 512), BF), v((CP, 512), BF), v((256, 512), F32),
        v((2, 96, D), BF), v((2, 96, D), BF), v((2, 96, D), BF),
        v((4, 256, 768), BF), v((4, STRIPS, 16, 128), BF), v((4, STRIPS, 16, 128), BF), v((7, 16, D), F32),
        v((D, D), BF), v((D, D), BF), v((768, D), BF), v((256, D), BF), v((4, 256, 768), BF), v((16, D), F32),
        v((128, D), BF), v((128, D), F32),
        pltpu.SemaphoreType.DMA((19,)), pltpu.SemaphoreType.REGULAR((6,)),
        pltpu.SemaphoreType.DMA((SENDS,)), pltpu.SemaphoreType.DMA((RECVS,)),
    ]
    return pl.pallas_call(
        layer_body,
        out_shape=outs,
        in_specs=[ANY] * 10 + [SMEM] * 3 + [VMEM] * 3,
        out_specs=tuple(VMEM if i == 1 else ANY for i in range(9)),
        scratch_shapes=scratch,
        compiler_params=pltpu.CompilerParams(collective_id=0, has_side_effects=True, vmem_limit_bytes=62 << 20),
    )(*args)


def widen_body(lout, sqz, gin, down, up, sq, outp, t, s, *refs):
    (o_lout, o_sqz, o_gin, o_again, o_q, o_kv, o_out, o_slopes, o_fgain, o_up, o_ubias, o_down, o_sq) = refs[:13]
    tin, lin, kv_wide, q_wide, wide, b_lout, b_gin, b_s, r_again, r_fgain, r_ubias, sem_in, sem_out = refs[13:]
    loads = []

    def load(src, dst):
        cp = pltpu.make_async_copy(src, dst, sem_in.at[len(loads)])
        cp.start()
        loads.append(cp)
        return cp

    s_load = load(s, b_s)
    t_load = load(t, tin)
    pieces = []
    for src, dst, n in ((down, o_down, 4), (up, o_up, 4), (sq, o_sq, 3), (outp, o_out, 1)):
        for i in range(n):
            k = len(pieces)
            pieces.append((load(src.at[pl.ds(256 * i, 256)], lin.at[k]), dst.at[pl.ds(256 * i, 256)]))
    plain = [(load(lout, b_lout), b_lout, o_lout), (load(gin, b_gin), b_gin, o_gin)]
    stores = []

    def leave(src, dst):
        stores.append(pltpu.make_async_copy(src, dst, sem_out.at[len(stores)]))
        stores[-1].start()

    s_load.wait()
    for row, to, dst in ((0, r_again, o_again), (1, r_fgain, o_fgain), (8, r_ubias, o_ubias)):
        to[...] = b_s[row : row + 1, :]
        leave(to, dst)
    o_slopes[...] = b_s[2:3, 0:8]
    o_sqz[...] = sqz[...]
    t_load.wait()
    for b in range(4):
        for part in range(2):
            kv_wide[:, pl.ds(part * D + b * 256, 256)] = tin[b, :, part * 256 : part * 256 + 256].astype(F32)
        q_wide[:, pl.ds(b * 256, 256)] = tin[b, :, 512:768].astype(F32)
    leave(kv_wide, o_kv)
    leave(q_wide, o_q)
    for i, (cp, dst) in enumerate(pieces):
        cp.wait()
        wide[i] = lin[i].astype(F32)
        leave(wide.at[i], dst)
    for cp, src, dst in plain:
        cp.wait()
        leave(src, dst)
    for cp in stores:
        cp.wait()


def widen(args):
    def out_shape(shape, dtype):
        return jax.ShapeDtypeStruct(shape, dtype)

    outs = (
        out_shape((128, D), BF), out_shape((43, D), BF), out_shape((128, D), F32), out_shape((1, D), F32),
        out_shape((256, D), F32), out_shape((256, 2 * D), F32), out_shape((256, D), F32), out_shape((1, 8), F32),
        out_shape((1, D), F32), out_shape((D, D), F32), out_shape((1, D), F32), out_shape((D, D), F32),
        out_shape((768, D), F32),
    )
    hbm = (0, 2, 3, 4, 5, 6, 8, 9, 10, 11, 12)
    v = pltpu.VMEM
    return pl.pallas_call(
        widen_body,
        out_shape=outs,
        in_specs=[ANY, VMEM, ANY, ANY, ANY, ANY, ANY, ANY, ANY],
        out_specs=tuple(ANY if i in hbm else VMEM for i in range(13)),
        scratch_shapes=[
            v((4, 256, 768), BF), v((12, 256, D), BF), v((256, 2 * D), F32), v((256, D), F32), v((12, 256, D), F32),
            v((128, D), BF), v((128, D), F32), v((16, D), F32), v((1, D), F32), v((1, D), F32), v((1, D), F32),
            pltpu.SemaphoreType.DMA((16,)), pltpu.SemaphoreType.DMA((19,)),
        ],
        compiler_params=pltpu.CompilerParams(vmem_limit_bytes=62 << 20),
    )(*args)


def per_device(
    layer_in, memory, squeezed_mem, memory_fill, squeezed_fill, grad_out, attn_gain, w_query, w_keyval,
    w_output, slopes, ffn_gain, w_up, up_bias, w_down, w_squeeze,
):
    done = layer((
        layer_in[0], memory[0], squeezed_mem[0], grad_out[0], w_query, w_keyval, w_output, w_up, w_down, w_squeeze,
        memory_fill, squeezed_fill, slopes, attn_gain[None], ffn_gain[None], up_bias[None],
    ))
    lout, sqz, gin, again, q, kv, out, slope, fgain, up, ubias, down, sq = widen(done)
    return (
        lout[None], sqz[None], gin[None], again[0], q, kv, out, slope[0], fgain[0], up, ubias[0], down, sq,
    )


def solution(mesh):
    rows = P("dp", "mp", None)
    in_specs = (
        rows, rows, rows, P("dp"), P("dp"), rows, P(), P(), P(), P(), P(), P(), P(None, "mp"), P("mp"), P("mp", None), P(),
    )
    out_specs = (
        rows, rows, rows, P(), P("mp", None), P("mp", None), P("mp", None), P(), P(), P(None, "mp"), P("mp"), P("mp", None), P("mp", None),
    )
    return jax.shard_map(per_device, mesh=mesh, in_specs=in_specs, out_specs=out_specs, check_vma=False)
```

```python
import functools

import jax
import jax.numpy as jnp
from jax import lax
from jax.experimental import pallas as pl
from jax.experimental.pallas import tpu as pltpu
from jax.sharding import PartitionSpec as P

D = 1024
H = 8
DH = 128
S = 512
M = 512
C = 512
CN = 172
CP = 192
EPS = 1e-05
NEG = -1e30
SCALE = DH ** (-0.5)
RECON = -2.0 / (S * D)
MESH = pl.DeviceIdType.MESH
BF = jnp.bfloat16
F32 = jnp.float32
VMEM = pl.BlockSpec(memory_space=pltpu.VMEM)
SMEM = pl.BlockSpec(memory_space=pltpu.SMEM)
ANY = pl.BlockSpec(memory_space=pl.ANY)
STRIPS = 6
SEG, MEM, OLD, GOUT = 0, 1, 2, 3
BASE = {OLD: 0, MEM: 512, SEG: 1024}
ORDER = (
    "send.s", "psend.m", "psend.s", "own.o", "psend.o", "own.s", "par.o", "send.o", "par.m", "own.m", "par.s",
    "psend.g", "pjo.s", "arr.s", "pjo.o", "pjo.m", "dia.s", "send.m", "far.s", "pjf.s", "arr.o", "at.s.0", "at.s.1",
    "far.o", "dia.o", "pjf.o", "at.o.1", "arr.m", "send.g", "far.m", "at.o.0", "dia.m", "pjf.m", "at.m.1", "at.m.0",
    "combine", "f0", "arr.g", "mf1", "squeeze", "gh0", "mix0a", "fw0", "gh1", "mix0b", "mix1a", "fw1", "ffn0",
    "mix1b", "ffn1", "gnmo", "up", "gnmw", "gS0", "f1", "down", "gS1", "r1", "s1", "s0", "U0", "dsq", "dno", "lnb0",
    "sqS", "lnb1", "D0", "U1", "xout", "att0.0", "sqT", "att0.1", "att0", "att1.0", "xsq", "att1.1", "D1", "att1",
    "t.0", "t.1", "U2", "t.2", "D2", "t", "dnw", "sego", "S0", "D3", "Q0", "dnS", "segw", "T0", "O0", "Q1", "U3",
    "S1", "D4", "O1", "T1", "Q2", "D5", "S2", "Q3", "U4", "O2", "T2", "D6", "Q4", "T3", "O3", "U5", "Q5", "D7", "U6",
    "T4", "Q6", "T5", "segS", "O4", "T6", "S3", "lout", "O5", "Q7", "U7", "O6", "T7", "S4", "T8", "gin", "O7", "U8",
    "S5", "Q8", "D8", "O8", "S6", "T9",
)
SENDS = 86
RECVS = 173


def dp_places():
    dp = lax.axis_index("dp")
    y, x, z = dp // 8, (dp // 2) % 4, dp % 2
    xa, xb = x + 1 - 2 * (x % 2), 3 - x
    ya, yb = y + 1 - 2 * (y % 2), 3 - y
    cube = [
        ((x + x // 2) % 2, y * 8 + xa * 2 + z),
        ((y + y // 2) % 2, ya * 8 + x * 2 + z),
        (x // 2, y * 8 + xb * 2 + z),
        (y // 2, yb * 8 + x * 2 + z),
    ]
    return cube, y * 8 + x * 2 + (1 - z)


def mp_places():
    mp = lax.axis_index("mp")
    zl, core = mp // 2, mp % 2
    return mp, zl, core, zl * 2 + (1 - core), (1 - zl) * 2 + core


class Flight:
    def __init__(self, links, cp, send, recv):
        self.links, self.cp, self.send, self.recv = links, cp, send, recv

    def wait_send(self):
        self.cp.wait_send()
        self.links.spare.append(self.send)

    def wait_recv(self):
        self.cp.wait_recv()

    def wait(self):
        self.wait_send()
        self.wait_recv()


class Links:
    def __init__(self, ssem, rsem):
        self.ssem, self.rsem, self.spare, self.sends, self.recvs = ssem, rsem, [], 0, 0

    def start(self, src, dst, place, like=None):
        if self.spare:
            k = self.spare.pop(0)
        else:
            k, self.sends = self.sends, self.sends + 1
        if like is not None:
            r = like.recv
        else:
            r, self.recvs = self.recvs, self.recvs + 1
        cp = pltpu.make_async_remote_copy(
            src_ref=src, dst_ref=dst, send_sem=self.ssem.at[k], recv_sem=self.rsem.at[r],
            device_id=place, device_id_type=MESH,
        )
        cp.start()
        return Flight(self, cp, k, r)

    def mp(self, src, dst, peer):
        return self.start(src, dst, (lax.axis_index("dp"), peer))

    def dp(self, src, dst, peer, like=None):
        return self.start(src, dst, (peer, lax.axis_index("mp")), like)


def loop(total, step, body, init=None):
    def run(i, carry):
        return body(pl.multiple_of(i * step, step), carry)

    return lax.fori_loop(0, total // step, run, init)


def each(total, step, body):
    def run(r, carry):
        body(r)
        return carry

    loop(total, step, run, 0)


def add_into(dst, dst_at, src, src_at, rows):
    step = 128 if rows % 128 == 0 else 64 if rows % 64 == 0 else 16

    def body(r):
        to, at = dst_at(r, step), src_at(r, step)
        dst[to] = dst[to] + src[at]

    each(rows, step, body)


def quarters(row0, rows, orders):
    return [(row0, rows, 256 * q, 256, order) for q, order in enumerate(orders)]


CUBE_FIRST = ((0, 1, 2, 3, 4), (1, 2, 3, 0, 4), (2, 3, 0, 1, 4), (3, 0, 1, 2, 4))
Z_FIRST = ((4, 0, 1, 2, 3), (4, 1, 2, 3, 0), (4, 2, 3, 0, 1), (4, 3, 0, 1, 2))


class Pieces:
    last = 8

    def __init__(self, links, ref, recv, base, free, pieces):
        self.links, self.ref, self.recv, self.base, self.free, self.pieces = links, ref, recv, base, free, pieces
        cube, zp = dp_places()
        self.dims = cube + [(lax.axis_index("dp") % 2, zp)]
        self.cur, self.old = [p[0] for p in pieces], [[] for _ in pieces]
        self.flying, self.sent, self.stage, self.out = [None] * len(pieces), [], 0, [[] for _ in pieces]

    def launch(self, i, s):
        row0, n, col0, width, order = self.pieces[i]
        cols, cur = pl.ds(col0, width), self.cur
        at = self.base + row0 + n - (n >> s)
        if s < 4:
            bit, peer = self.dims[order[s]]
            half = n >> (s + 1)
            give = pl.multiple_of(cur[i] + (1 - bit) * half, 16)
            self.old[i].append(cur[i])
            cur[i] = pl.multiple_of(cur[i] + bit * half, 16)
            cp = self.links.dp(self.ref.at[pl.ds(give, half), cols], self.recv.at[pl.ds(at, half), cols], peer)
        elif s == 4:
            size = n >> 4
            cp = self.links.dp(
                self.ref.at[pl.ds(cur[i], size), cols], self.recv.at[pl.ds(at, size), cols], self.dims[order[4]][1]
            )
        else:
            k = 8 - s
            here = self.ref.at[pl.ds(cur[i], n >> (k + 1)), cols]
            cp = self.links.dp(here, here, self.dims[order[k]][1], self.out[i][k])
            cur[i] = self.old[i][k]
        self.out[i].append(cp)
        self.flying[i] = cp

    def begin(self):
        for i in range(len(self.pieces)):
            self.launch(i, 0)

    def advance(self):
        s = self.stage
        if s == 4:
            pl.semaphore_wait(self.free, 5)
        earlier, self.sent = self.sent, []
        for i, (row0, n, col0, width, _) in enumerate(self.pieces):
            cp, cols = self.flying[i], pl.ds(col0, width)
            if s == 4:
                cp.wait_send()
            else:
                self.sent.append(cp)
            cp.wait_recv()
            if s <= 4:
                at, here = self.base + row0 + n - (n >> s), self.cur[i]
                add_into(
                    self.ref, lambda r, m: (pl.ds(here + r, m), cols),
                    self.recv, lambda r, m: (pl.ds(at + r, m), cols), n >> min(s + 1, 4),
                )
            if s < 8:
                self.launch(i, s + 1)
        for cp in earlier:
            cp.wait_send()
        if s == 3:
            for cp in self.sent:
                cp.wait_send()
            self.sent = []
            for _, peer in self.dims:
                pl.semaphore_signal(self.free, inc=1, device_id=(peer, lax.axis_index("mp")), device_id_type=MESH)
        self.stage += 1

    def finish(self):
        for cp in self.sent:
            cp.wait_send()


DOWN_PIECES = quarters(0, 1024, CUBE_FIRST)
UP_PIECES = quarters(0, 1024, CUBE_FIRST)
SQ_PIECES = quarters(0, 256, CUBE_FIRST) + quarters(256, 512, Z_FIRST)


class Strips:
    last = 9

    def __init__(self, links, ref, recv, pack, got, free):
        self.links, self.ref, self.recv, self.pack, self.got, self.free = links, ref, recv, pack, got, free
        self.cube, self.zp = dp_places()
        self.cur, self.old = [0] * 4, [[] for _ in range(4)]
        self.flying, self.sent, self.stage, self.out = [], [], 0, []

    def launch(self, s):
        ref, cur = self.ref, self.cur
        self.flying = []
        for j in range(STRIPS):
            q, cols = j % 4, pl.ds(128 * j, 128)
            if s < 4:
                bit, peer = self.cube[(q + s) % 4]
                half = 256 >> (s + 1)
                give = pl.multiple_of(cur[q] + (1 - bit) * half, 16)
                cp = self.links.dp(
                    ref.at[:, pl.ds(give, half), cols], self.recv.at[:, pl.ds(256 - (256 >> s), half), cols], peer
                )
            elif s == 4:
                cp = self.links.dp(ref.at[:, pl.ds(cur[q], 16), cols], self.recv.at[:, pl.ds(240, 16), cols], self.zp)
            else:
                k = 9 - s
                bit, peer = self.cube[(q + k) % 4]
                here = ref.at[:, pl.ds(cur[q], 256 >> (k + 1)), cols]
                cp = self.links.dp(here, here, peer, self.out[k][j])
            self.flying.append(cp)
        self.out.append(self.flying)
        for q in range(4):
            if s < 4:
                bit, _ = self.cube[(q + s) % 4]
                self.old[q].append(cur[q])
                cur[q] = pl.multiple_of(cur[q] + bit * (256 >> (s + 1)), 16)
            elif s > 4:
                cur[q] = self.old[q][9 - s]

    def begin(self):
        self.launch(0)

    def advance(self):
        s = self.stage
        if s > 9:
            return
        mp, zl, core, part, far = mp_places()
        earlier, self.sent = self.sent, []
        if s == 5:
            for cp in self.flying:
                cp.wait()
            self.got[mp] = self.pack[mp]
            for j in range(STRIPS):
                self.ref[:, pl.ds(self.cur[j % 4], 16), pl.ds(128 * j, 128)] = self.got[:, j]
            pl.semaphore_wait(self.free, 4)
            self.launch(6)
        else:
            for j, cp in enumerate(self.flying):
                cols = pl.ds(128 * j, 128)
                if s == 4:
                    cp.wait_send()
                else:
                    self.sent.append(cp)
                cp.wait_recv()
                if s <= 4:
                    rows, at, here = 256 >> min(s + 1, 4), 256 - (256 >> s), self.cur[j % 4]
                    add_into(
                        self.ref, lambda r, m: (slice(None), pl.ds(here + r, m), cols),
                        self.recv, lambda r, m: (slice(None), pl.ds(at + r, m), cols), rows,
                    )
            if s == 3:
                for cp in self.sent:
                    cp.wait_send()
                self.sent = []
                for _, peer in self.cube:
                    pl.semaphore_signal(self.free, inc=1, device_id=(peer, mp), device_id_type=MESH)
            if s == 4:
                for j in range(STRIPS):
                    self.pack[:, j] = self.ref[:, pl.ds(self.cur[j % 4], 16), pl.ds(128 * j, 128)]
                self.flying = [self.links.mp(self.pack.at[peer], self.got.at[mp], peer) for peer in (part, far, 3 - mp)]
            elif s < 9:
                self.launch(s + 1)
        for cp in earlier:
            cp.wait_send()
        self.stage += 1

    def finish(self):
        for cp in self.sent:
            cp.wait_send()


class Smalls:
    last = 6

    def __init__(self, links, ref, recv):
        self.links, self.ref, self.recv, self.stage = links, ref, recv, 0
        cube, zp = dp_places()
        self.peers = [peer for _, peer in cube] + [zp]

    def begin(self):
        s = self.stage
        mp, zl, core, part, far = mp_places()
        self.rows = pl.ds(0, 16 if s < 5 else 8)
        src, dst = self.ref.at[self.rows], self.recv.at[s, self.rows]
        if s < 5:
            self.cp = self.links.dp(src, dst, self.peers[s])
        else:
            self.cp = self.links.mp(src, dst, (part, far)[s - 5])

    def advance(self):
        if self.stage > 6:
            return
        self.cp.wait()
        self.ref[self.rows, :] = self.ref[self.rows, :] + self.recv[self.stage, self.rows, :]
        self.stage += 1
        if self.stage <= 6:
            self.begin()

    def finish(self):
        pass


def dg(a, b, left=1, right=0):
    return lax.dot_general(a, b, (((left,), (right,)), ((), ())), preferred_element_type=F32)


def normalize(rows):
    centre = rows - jnp.mean(rows, axis=-1, keepdims=True)
    inv = lax.rsqrt(jnp.mean(centre * centre, axis=-1, keepdims=True) + EPS)
    return centre * inv, inv


def norm_back(grad, gain, unit, inv):
    g = grad * gain
    return inv * (g - jnp.mean(g, axis=-1, keepdims=True) - unit * jnp.mean(g * unit, axis=-1, keepdims=True))


def iota(shape, dim):
    return lax.broadcasted_iota(jnp.int32, shape, dim)


def fold(x, op):
    out = x[:8]
    for i in range(1, x.shape[0] // 8):
        out = op(out, x[8 * i : 8 * i + 8])
    return out


def layer_body(
    seg_in, mem_in, old_in, gout_in, wq_in, wkv_in, wo_in, wup_in, wdn_in, wsq_in,
    mfill, sfill, slopes, again_in, fgain_in, ubias_in,
    lout_out, sqz_out, gin_out, down_out, up_out, sq_out, out_out, t_out, s_out,
    raw, normed, wkvq, wo, wup, wdn, wsq, kv, query, expo, tmp, tmp2, stat, acc, mixt, mixg, mid, nm, hid, gpre,
    out, got, keep, out2, got2, gb, gmix, gkv, gq, win, sqz, skv, esq, gsq, rec, sbuf, sgot, sqsum, trecv, tpack, tgot, srecv,
    x_down, x_up, x_sq, x_out, t_ref, s_ref, lout, gin, sqz_rows, again, fgain, ubias, lsem, free, ssem, rsem,
):
    links = Links(ssem, rsem)
    mp, zl, core, part, far = mp_places()
    diag = 3 - mp
    cube, zp = dp_places()
    dp = lax.axis_index("dp")
    mine = pl.ds(pl.multiple_of(mp * 256, 256), 256)

    sem = pltpu.get_barrier_semaphore()
    for peer in [peer for _, peer in cube] + [zp]:
        pl.semaphore_signal(sem, inc=1, device_id=(peer, mp), device_id_type=MESH)
    for peer in (part, far, diag):
        pl.semaphore_signal(sem, inc=1, device_id=(dp, peer), device_id_type=MESH)

    ins = {SEG: seg_in, MEM: mem_in, OLD: old_in, GOUT: gout_in}
    own_loads = {}
    nlocal = [0]

    def load(src, dst):
        cp = pltpu.make_async_copy(src, dst, lsem.at[nlocal[0]])
        nlocal[0] += 1
        cp.start()
        return cp

    for a in (SEG, MEM, OLD, GOUT):
        own_loads[a] = load(ins[a], raw.at[a, mp])
    gains = [load(again_in, again), load(fgain_in, fgain), load(ubias_in, ubias)]
    w_loads = [
        load(wkv_in.at[:, mine], wkvq.at[:, pl.ds(0, 256)]),
        load(wkv_in.at[:, pl.ds(pl.multiple_of(D + mp * 256, 256), 256)], wkvq.at[:, pl.ds(256, 256)]),
        load(wq_in.at[:, mine], wkvq.at[:, pl.ds(512, 256)]),
    ]

    pl.semaphore_wait(sem, 8)

    done = []

    far_cp, part_cp, fwd_cp = {}, {}, {}
    sq_load = load(wsq_in, wsq)
    late_loads = [load(wo_in, wo), load(wup_in, wup), load(wdn_in, wdn)]
    mem_limit = M - mfill[0]
    old_limit = C - sfill[0]

    def slope_of(h):
        return slopes[mp * 2 + h]

    def heads(h):
        return pl.ds(h * DH, DH)

    def column(r, rows):
        return iota((rows, 1), 0) + r

    def exponentials(src, dst, dst0, rows, colmask, causal=False):
        step = 64

        def one(r, top):
            s = src[pl.ds(r, step), :] * SCALE + colmask(r, step)
            if causal:
                s = jnp.where(iota((step, 512), 0) + r <= iota((step, 512), 1), s, NEG)
            src[pl.ds(r, step), :] = s
            return jnp.maximum(top, fold(s, jnp.maximum))

        top = loop(rows, step, one, jnp.full((8, 512), NEG, F32))
        top = jnp.max(top, axis=0, keepdims=True)

        def two(r, total):
            e = jnp.exp(src[pl.ds(r, step), :] - top).astype(BF)
            dst[pl.ds(dst0 + r, step), :] = e
            return total + fold(e.astype(F32), jnp.add)

        total = loop(rows, step, two, jnp.zeros((8, 512), F32))
        return top, jnp.sum(total, axis=0, keepdims=True)

    def attend(h, a):
        base = BASE[a]
        rows = pl.ds(base, 512)
        g = base // 512
        tmp[...] = dg(kv[rows, heads(h)], query[:, heads(h)], 1, 1)
        slope = slope_of(h)

        def colmask(r, step):
            j = column(r, step)
            bias = slope * (j + (base - 1536)).astype(F32)
            if a == MEM:
                bias = jnp.where(j >= mem_limit, bias, NEG)
            if a == OLD:
                bias = jnp.where(j >= old_limit, bias, NEG)
            return bias

        top, total = exponentials(tmp, expo.at[h], base, 512, colmask, a == SEG)
        stat[h * 6 + g : h * 6 + g + 1, :] = top
        stat[h * 6 + 3 + g : h * 6 + 4 + g, :] = total
        acc[h * 3 + g] = dg(kv[rows, pl.ds(256 + h * DH, DH)], expo[h, rows, :], 0, 0)

    def first_of(h):
        rows = pl.ds(BASE[MEM], 512)
        tmp[...] = dg(kv[rows, heads(h)], query[:, heads(h)], 1, 1)
        _, total = exponentials(
            tmp, gkv, 0, 512, lambda r, step: jnp.where(column(r, step) >= mem_limit, 0.0, NEG)
        )
        rec[heads(h), :] = dg(kv[rows, pl.ds(256 + h * DH, DH)], gkv[0:512, :], 0, 0) / total

    tasks, ran = {}, set()

    def task(name, *after):
        def keep_it(run):
            tasks[name] = (run, after)
            return run

        return keep_it

    sums = {
        "D": Pieces(links, x_down, wsq, 0, free.at[1], DOWN_PIECES),
        "U": Pieces(links, x_up, wsq, 1024, free.at[2], UP_PIECES),
        "Q": Pieces(links, x_sq, wsq, 2048, free.at[3], SQ_PIECES),
        "O": Pieces(links, x_out, wsq, 2816, free.at[4], quarters(0, 256, [CUBE_FIRST[q] for q in (2, 3, 2, 3)])),
        "T": Strips(links, t_ref, trecv, tpack, tgot, free.at[5]),
        "S": Smalls(links, s_ref, srecv),
    }
    results = {"D": (x_down, down_out), "U": (x_up, up_out), "Q": (x_sq, sq_out), "O": (x_out, out_out), "T": (t_ref, t_out), "S": (s_ref, s_out)}
    flights = {}
    leaving, roomy = [], []
    bias_rows = [jnp.zeros((8, 512), F32)] * 2
    totals = {"gain": jnp.zeros((1, D), F32), "slope": jnp.zeros((1, D), F32), "bias": bias_rows}

    def begin(name):
        if not roomy:
            pl.semaphore_wait(free.at[0], 5)
            roomy.append(True)
        sums[name].begin()

    def half_rows(z):
        return pl.ds(z * 256, 256)

    def block(z, other):
        return pl.ds(pl.multiple_of((2 * z + ((1 - core) if other else core)) * 128, 128), 128)

    waited = set()

    def once(name, copies):
        if name not in waited:
            waited.add(name)
            for cp in copies:
                cp.wait()

    def norm_rows(a, owner):
        once("gains", gains)
        unit, _ = normalize(raw[a, owner].astype(F32))
        normed[pl.ds(pl.multiple_of(BASE[a] + owner * 128, 128), 128), :] = (unit * again[...]).astype(BF)

    def send_rows(a, copies, peer):
        copies[a] = links.mp(ins[a], raw.at[a, mp], peer)
        done.append(copies[a])

    def norm_own(a):
        own_loads[a].wait()
        norm_rows(a, mp)

    def norm_part(a):
        part_cp[a].wait_recv()
        norm_rows(a, part)

    def arrive(a):
        far_cp[a].wait_recv()
        fwd_cp[a] = links.mp(raw.at[a, far], raw.at[a, far], part)
        done.append(fwd_cp[a])

    def norm_diag(a):
        fwd_cp[a].wait_recv()
        norm_rows(a, diag)

    def project(a, chip):
        once("wkvq", w_loads)
        own = pl.ds(pl.multiple_of(chip * 256, 256), 256)
        rows = pl.ds(pl.multiple_of(BASE[a] + chip * 256, 256), 256)
        kv[rows, :] = dg(normed[rows, :], wkvq[:, 0:512]).astype(BF)
        if a == SEG:
            query[own, :] = dg(normed[rows, :], wkvq[:, 512:768]).astype(BF)

    for c, a in (("s", SEG), ("m", MEM), ("o", OLD), ("g", GOUT)):
        task(f"send.{c}")(functools.partial(send_rows, a, far_cp, far))
        task(f"psend.{c}")(functools.partial(send_rows, a, part_cp, part))
        task(f"arr.{c}", f"send.{c}")(functools.partial(arrive, a))
        if a != GOUT:
            task(f"own.{c}")(functools.partial(norm_own, a))
            task(f"par.{c}", f"psend.{c}")(functools.partial(norm_part, a))
            task(f"far.{c}", f"arr.{c}")(functools.partial(norm_rows, a, far))
            task(f"dia.{c}", f"arr.{c}")(functools.partial(norm_diag, a))
            task(f"pjo.{c}", f"own.{c}", f"par.{c}")(functools.partial(project, a, zl))
            task(f"pjf.{c}", f"far.{c}", f"dia.{c}")(functools.partial(project, a, 1 - zl))
            for h in range(2):
                task(f"at.{c}.{h}", f"pjo.{c}", f"pjf.{c}", "pjo.s", "pjf.s")(functools.partial(attend, h, a))

    @task("combine", *(f"at.{c}.{h}" for c in "smo" for h in range(2)))
    def _():
        for h in range(2):
            tops = [stat[h * 6 + g : h * 6 + g + 1, :] for g in range(3)]
            sums = [stat[h * 6 + 3 + g : h * 6 + 4 + g, :] for g in range(3)]
            top = jnp.maximum(jnp.maximum(tops[0], tops[1]), tops[2])
            scales = [jnp.exp(t - top) for t in tops]
            total = scales[0] * sums[0] + scales[1] * sums[1] + scales[2] * sums[2]
            mixed = jnp.zeros((DH, 512), F32)
            for g in range(3):
                inv = scales[g] / total
                stat[12 + h * 3 + g : 13 + h * 3 + g, :] = inv
                mixed = mixed + acc[h * 3 + g] * inv
            mixt[heads(h), :] = mixed
            mixg[mp, :, heads(h)] = mixed.T.astype(BF)
        for z in range(2):
            here = mixg.at[mp, half_rows(z)]
            flights["mix_part", z] = links.mp(here, here, part)
            done.append(flights["mix_part", z])
        send_mix(0)

    def send_mix(z):
        here = mixg.at[mp, half_rows(z)]
        flights["mix_far", z] = links.mp(here, here, far)
        done.append(flights["mix_far", z])

    task("mf1", "combine")(functools.partial(send_mix, 1))

    @task("squeeze", "dia.m")
    def _():
        sq_load.wait()
        rows = raw[MEM].reshape(512, D)
        for tap in range(3):
            pick = (iota((CP, 512), 1) == 3 * iota((CP, 512), 0) + tap).astype(BF)
            win[:, tap * D : (tap + 1) * D] = dg(pick, rows).astype(BF)
        for half in range(2):
            cols = pl.ds(half * 512, 512)
            sqz[:, cols] = dg(win[...], wsq[:, cols])
        for peer in [peer for _, peer in cube] + [zp]:
            pl.semaphore_signal(free.at[0], inc=1, device_id=(peer, mp), device_id_type=MESH)

    @task("r1", "squeeze")
    def _():
        pick = (iota((48, CP), 1) == iota((48, CP), 0) + mp * 43).astype(BF)
        sqz_rows[...] = dg(pick, sqz[...].astype(BF))[0:43].astype(BF)
        leaving.append(load(sqz_rows, sqz_out))
        unit, _ = normalize(sqz[...])
        skv[...] = dg((unit * again[...]).astype(BF), wkvq[:, 0:512]).astype(BF)

    for h in range(2):
        task(f"f{h}", "pjo.m", "pjf.m", "pjo.s", "pjf.s")(functools.partial(first_of, h))

    def second_of(h):
        keys, values = skv[:, heads(h)], skv[:, pl.ds(256 + h * DH, DH)]
        tmp[0:CP, :] = dg(keys, query[:, heads(h)], 1, 1)

        def colmask(r, step):
            slot = column(r, step)
            return jnp.where((3 * slot < M) & (3 * slot + 2 >= mem_limit), 0.0, NEG)

        _, total = exponentials(tmp, esq, 0, CP, colmask)
        inv = 1.0 / total
        second = dg(values, esq[...], 0, 0) * inv
        grad = (rec[heads(h), :] - second) * RECON
        inner = inv * jnp.sum(grad * second, axis=0, keepdims=True)
        scaled = (grad * inv).astype(BF)
        gsq[:, pl.ds(256 + h * DH, DH)] = dg(esq[...], scaled, 1, 1).astype(BF)
        gp = dg(values, scaled)
        gs = (esq[...].astype(F32) * (gp - inner)).astype(BF)
        gsq[:, heads(h)] = (dg(gs, query[:, heads(h)]) * SCALE).astype(BF)

    for h in range(2):
        task(f"s{h}", "r1", f"f{h}", "pjo.s", "pjf.s")(functools.partial(second_of, h))

    @task("dsq", "s0", "s1")
    def _():
        unit, inv = normalize(sqz[...])
        sqz[...] = norm_back(dg(gsq[...], wkvq[:, 0:512], 1, 1), again[...], unit, inv)
        sbuf[0] = sqz[pl.ds(pl.multiple_of((1 - core) * 96, 16), 96), :].astype(BF)
        flights["sq_part"] = links.mp(sbuf.at[0], sgot.at[0], part)
        done.append(flights["sq_part"])

    @task("sqS", "dsq")
    def _():
        flights["sq_part"].wait_recv()
        sbuf[1] = (sqz[pl.ds(pl.multiple_of(core * 96, 16), 96), :] + sgot[0].astype(F32)).astype(BF)
        flights["sq_far"] = links.mp(sbuf.at[1], sgot.at[1], far)

    @task("sqT", "sqS")
    def _():
        flights["sq_far"].wait()
        sqsum[core] = (sbuf[1].astype(F32) + sgot[1].astype(F32)).astype(BF)
        flights["sq_back"] = links.mp(sqsum.at[core], sqsum.at[core], part)

    @task("xsq", "sqT")
    def _():
        flights["sq_back"].wait()
        for half in range(2):
            cols = pl.ds(half * 512, 512)
            x_sq[:, cols] = dg(win[:, pl.ds(pl.multiple_of(mp * 768, 256), 768)], sqsum[:, :, cols].reshape(CP, 512), 0, 0).astype(BF)
        begin("Q")

    def mix_into(z, owners, first=False):
        rows = half_rows(z)
        for half in range(2):
            cols = pl.ds(half * 512, 512)
            base = raw[SEG, 2 * z : 2 * z + 2, :, cols].reshape(256, 512).astype(F32) if first else mid[rows, cols]
            for owner in owners:
                base = base + dg(mixg[owner, rows, :], wo[pl.ds(pl.multiple_of(owner * 256, 256), 256), cols])
            mid[rows, cols] = base

    def mix_own(z):
        once("weights", late_loads)
        flights["mix_part", z].wait_recv()
        mix_into(z, (mp, part), True)

    def forward_mix(z):
        flights["mix_far", z].wait_recv()
        here = mixg.at[far, half_rows(z)]
        flights["mix_fwd", z] = links.mp(here, here, part)
        done.append(flights["mix_fwd", z])

    def grad_hidden(z):
        once("weights", late_loads)
        if z == 0:
            own_loads[GOUT].wait()
            part_cp[GOUT].wait_recv()
            fwd_cp[GOUT].wait_recv()
        for half in range(2):
            cols = pl.ds(half * 512, 512)
            keep[z, :, :, cols] = dg(raw[GOUT, 2 * z : 2 * z + 2].reshape(256, D), wdn[cols, :], 1, 1).reshape(2, 128, 512)

    def feed_forward(z):
        flights["mix_fwd", z].wait_recv()
        mix_into(z, (diag,))
        rows = half_rows(z)
        for i in range(2):
            at = pl.ds(z * 256 + i * 128, 128)
            unit, _ = normalize(mid[at, :])
            nm[at, :] = (unit * fgain[...]).astype(BF)
        for half in range(2):
            cols = pl.ds(half * 512, 512)
            tmp[half_rows(half), :] = dg(nm[rows, :], wup[:, cols])
        for half, i in ((0, 0), (0, 1), (1, 0), (1, 1)):
            cols = pl.ds(half * 512, 512)

            def gelu(r, total):
                to = pl.ds(r + z * 256 + i * 128, 64)
                v = tmp[pl.ds(r + half * 256 + i * 128, 64), :] + ubias[:, cols]
                square = v * v
                th = jnp.tanh(0.7978845608028654 * v * (1.0 + 0.044715 * square))
                hid[to, cols] = (0.5 * v * (1.0 + th)).astype(BF)
                slope = 0.5 * (1.0 + th) + (0.5 * 0.7978845608028654) * v * (1.0 - th * th) * (1.0 + 3 * 0.044715 * square)
                g = (slope * keep[z, i, pl.ds(r, 64), cols]).astype(BF)
                gpre[to, cols] = g
                return total + fold(g.astype(F32), jnp.add)

            totals["bias"][half] = loop(128, 64, gelu, totals["bias"][half])
        if z == 1:
            for half in range(2):
                s_ref[8:9, pl.ds(half * 512, 512)] = jnp.sum(totals["bias"][half], axis=0, keepdims=True)

    for z in range(2):
        task(f"mix{z}a", "combine", *(["mix0a"] if z else []))(functools.partial(mix_own, z))
        task(f"fw{z}", "combine", *(["fw0", "mf1"] if z else []))(functools.partial(forward_mix, z))
        task(f"gh{z}", "arr.g", "psend.g", *(["gh0"] if z else []))(functools.partial(grad_hidden, z))
        task(f"mix{z}b", f"mix{z}a", f"fw{z}")(functools.partial(mix_into, z, (far,)))
        task(f"ffn{z}", f"mix{z}b", f"gh{z}", *(["ffn0"] if z else []))(functools.partial(feed_forward, z))

    def tiles(dst, left, right):
        for half in range(2):
            rows = pl.ds(half * 512, 512)
            for quarter in range(2):
                cols = pl.ds(quarter * 512, 512)
                dst[rows, cols] = dg(left(rows), right(cols), 0, 0).astype(BF)

    @task("down", "ffn1", "squeeze")
    def _():
        tiles(x_down, lambda rows: hid[:, rows], lambda cols: raw[GOUT, :, :, cols].reshape(512, 512))
        begin("D")

    @task("up", "ffn1", "squeeze")
    def _():
        tiles(x_up, lambda rows: nm[:, rows], lambda cols: gpre[:, cols])
        begin("U")

    @task("gnmo", "ffn1")
    def _():
        for z in range(2):
            out[0, z] = dg(gpre[block(z, True), :], wup[...], 1, 1).astype(BF)
            flights["gnm_part", z] = links.mp(out.at[0, z], got.at[0, z], part)

    @task("gnmw", "gnmo")
    def _():
        for z in range(2):
            keep[0, z] = dg(gpre[block(z, False), :], wup[...], 1, 1)

    def gnm_sum(z):
        flights["gnm_part", z].wait_recv()
        out2[z] = (keep[0, z] + got[0, z].astype(F32)).astype(BF)
        flights["gnm_far", z] = links.mp(out2.at[z], got2.at[z], far)

    @task("dno", "ffn1")
    def _():
        for z in range(2):
            out[1, z] = dg(hid[block(z, True), :], wdn[...]).astype(BF)
            flights["down_part", z] = links.mp(out.at[1, z], got.at[1, z], part)
            done.append(flights["down_part", z])

    @task("dnw", "ffn1")
    def _():
        for z in range(2):
            keep[1, z] = dg(hid[block(z, False), :], wdn[...])

    @task("dnS", "dno", "dnw")
    def _():
        for z in range(2):
            flights["down_part", z].wait_recv()
        out2[2] = (keep[1, 1 - zl] + got[1, 1 - zl].astype(F32)).astype(BF)
        flights["down_far"] = links.mp(out2.at[2], got2.at[2], far)

    @task("lout", "dnS")
    def _():
        flights["down_far"].wait()
        lout[...] = (
            mid[pl.ds(pl.multiple_of(mp * 128, 128), 128), :]
            + keep[1, zl] + got[1, zl].astype(F32) + got2[2].astype(F32)
        ).astype(BF)
        leaving.append(load(lout, lout_out))

    def norm_mid_back(z):
        flights["gnm_far", z].wait()
        rows = block(z, False)
        unit, inv = normalize(mid[rows, :])
        g = out2[z].astype(F32) + got2[z].astype(F32)
        totals["gain"] = totals["gain"] + jnp.sum(g * unit, axis=0, keepdims=True) * jnp.where(zl == z, 1.0, 0.0)
        gmid = raw[GOUT, 2 * z + core].astype(F32) + norm_back(g, fgain[...], unit, inv)
        keep[0, z] = gmid
        gb[z, core] = gmid.astype(BF)
        flights["gb", z] = links.mp(gb.at[z, core], gb.at[z, core], part)
        if z == 1:
            s_ref[1:2, :] = totals["gain"]

    for z in range(2):
        task(f"gS{z}", "gnmw", *(["gS0"] if z else []))(functools.partial(gnm_sum, z))
        task(f"lnb{z}", f"gS{z}", *(["lnb0"] if z else []))(functools.partial(norm_mid_back, z))

    @task("xout", "lnb1", "squeeze")
    def _():
        for z in range(2):
            flights["gb", z].wait()
        gmix[...] = dg(wo[mine, :], gb[...].reshape(512, D), 1, 1)
        for half in range(2):
            cols = pl.ds(half * 512, 512)
            x_out[:, cols] = dg(mixg[mp], gb[:, :, :, cols].reshape(512, 512), 0, 0).astype(BF)
        begin("O")

    carried = {}

    def attend_back(h, a):
        base = BASE[a]
        rows = pl.ds(base, 512)
        grad = gmix[heads(h), :]
        if a == OLD:
            carried["inner"] = jnp.sum(grad * mixt[heads(h), :], axis=0, keepdims=True)
            carried["slope"] = jnp.zeros((8, 512), F32)
        inv = stat[12 + h * 3 + base // 512 : 13 + h * 3 + base // 512, :]
        scaled = (grad * inv).astype(BF)
        shift = inv * carried["inner"]
        tmp[...] = dg(kv[rows, pl.ds(256 + h * DH, DH)], scaled)
        gkv[rows, pl.ds(256 + h * DH, DH)] = dg(expo[h, rows, :], scaled, 1, 1).astype(BF)

        def score_grads(r, total):
            at = pl.ds(base + r, 64)
            gs = (expo[h, at, :].astype(F32) * (tmp[pl.ds(r, 64), :] - shift)).astype(BF)
            expo[h, at, :] = gs
            dist = (iota((64, 512), 1) - iota((64, 512), 0) + (1024 - base - r)).astype(F32)
            return total + fold(gs.astype(F32) * dist, jnp.add)

        carried["slope"] = loop(512, 64, score_grads, carried["slope"])
        gkv[rows, heads(h)] = (dg(expo[h, rows, :], query[:, heads(h)]) * SCALE).astype(BF)
        if a == SEG:
            gqt = dg(kv[:, heads(h)], expo[h], 0, 0)
            gq[:, heads(h)] = (gqt * SCALE).T.astype(BF)
            value = -jnp.sum(jnp.sum(carried["slope"], axis=0, keepdims=True), axis=1, keepdims=True)
            totals["slope"] = totals["slope"] + jnp.where(iota((1, D), 1) == mp * 2 + h, value, 0.0)

    before = ("xout", "f0", "f1")
    for h in range(2):
        for name, a in ((f"att{h}.0", OLD), (f"att{h}.1", MEM), (f"att{h}", SEG)):
            task(name, *before)(functools.partial(attend_back, h, a))
            before = (name,)

    def projections(b):
        feats = pl.ds(b * 256, 256)
        big = dg(normed[:, feats], gkv[...], 0, 0)
        small = dg(normed[1024:1536, feats], gq[...], 0, 0)
        t_ref[b, :, 0:512] = big.astype(BF)
        t_ref[b, :, 512:768] = small.astype(BF)
        terms = small[:, 0:128] * wkvq[feats, 512:640].astype(F32) + small[:, 128:256] * wkvq[feats, 640:768].astype(F32)
        for j in range(4):
            terms = terms + big[:, j * 128 : (j + 1) * 128] * wkvq[feats, j * 128 : (j + 1) * 128].astype(F32)
        s_ref[0:1, feats] = jnp.sum(terms.T, axis=0, keepdims=True) / again[:, feats]
        if b == 3:
            begin("T")
            s_ref[2:3, :] = totals["slope"]
            s_ref[3:8, :] = jnp.zeros((5, D), F32)
            s_ref[9:16, :] = jnp.zeros((7, D), F32)
            begin("S")

    for b in range(4):
        task(("t.0", "t.1", "t.2", "t")[b], "att1", *([("t.0", "t.1", "t.2")[b - 1]] if b else []))(functools.partial(projections, b))

    def seg_terms(z, other):
        rows = block(z, other)
        at = pl.ds(pl.multiple_of(BASE[SEG] + (2 * z + ((1 - core) if other else core)) * 128, 128), 128)
        return dg(gkv[at, :], wkvq[:, 0:512], 1, 1) + dg(gq[rows, :], wkvq[:, 512:768], 1, 1)

    @task("sego", "att1")
    def _():
        for z in range(2):
            flights["gnm_part", z].wait_send()
            out[0, z] = seg_terms(z, True).astype(BF)
            flights["seg_part", z] = links.mp(out.at[0, z], got.at[0, z], part)
            done.append(flights["seg_part", z])

    @task("segw", "att1")
    def _():
        for z in range(2):
            terms = seg_terms(z, False)
            for half in range(2):
                tmp2[(2 * z + half) * 128 : (2 * z + half + 1) * 128, :] = terms[:, half * 512 : (half + 1) * 512]

    @task("segS", "sego", "segw")
    def _():
        for z in range(2):
            flights["seg_part", z].wait_recv()
        for half in range(2):
            cols = pl.ds(half * 512, 512)
            at = pl.ds(pl.multiple_of((2 * (1 - zl) + half) * 128, 128), 128)
            out2[3, :, cols] = (tmp2[at, :] + got[0, 1 - zl, :, cols].astype(F32)).astype(BF)
        flights["seg_far"] = links.mp(out2.at[3], got2.at[3], far)

    @task("gin", "segS")
    def _():
        flights["seg_far"].wait()
        unit, inv = normalize(raw[SEG, mp].astype(F32))
        own = [tmp2[pl.ds(pl.multiple_of((2 * zl + half) * 128, 128), 128), :] for half in range(2)]
        total = jnp.concatenate(own, axis=1) + got[0, zl].astype(F32) + got2[3].astype(F32)
        gin[...] = keep[0, zl] + norm_back(total, again[...], unit, inv)
        leaving.append(load(gin, gin_out))

    for name in ORDER:
        if name in tasks:
            run, after = tasks[name]
            assert all(other in ran for other in after), name
            run()
        else:
            part_sum = sums[name[0]]
            assert part_sum.stage == int(name[1:]), name
            part_sum.advance()
            if part_sum.stage > part_sum.last:
                leaving.append(load(*results[name[0]]))
        ran.add(name)
    assert len(ran) == len(tasks) + sum(part_sum.last + 1 for part_sum in sums.values())
    for part_sum in sums.values():
        part_sum.finish()
    for cp in leaving:
        cp.wait()
    for cp in done:
        cp.wait_send()
    assert links.sends <= SENDS and links.recvs <= RECVS, (links.sends, links.recvs)


def layer(args):
    def out_shape(shape, dtype):
        return jax.ShapeDtypeStruct(shape, dtype)

    outs = (
        out_shape((128, D), BF), out_shape((43, D), BF), out_shape((128, D), F32), out_shape((1024, D), BF),
        out_shape((1024, D), BF), out_shape((768, D), BF), out_shape((256, D), BF), out_shape((4, 256, 768), BF),
        out_shape((16, D), F32),
    )
    v = pltpu.VMEM
    scratch = [
        v((4, 4, 128, D), BF), v((1536, D), BF), v((D, 768), BF), v((D, D), BF), v((D, D), BF), v((D, D), BF),
        v((3072, D), BF), v((1536, 512), BF), v((512, 256), BF), v((2, 1536, 512), BF), v((512, 512), F32),
        v((512, 512), F32), v((24, 512), F32), v((6, DH, 512), F32), v((256, 512), F32), v((4, 512, 256), BF),
        v((512, D), F32), v((512, D), BF), v((512, D), BF), v((512, D), BF),
        v((2, 2, 128, D), BF), v((2, 2, 128, D), BF), v((2, 2, 128, D), F32), v((4, 128, D), BF), v((4, 128, D), BF),
        v((2, 2, 128, D), BF), v((256, 512), F32), v((1536, 512), BF), v((512, 256), BF),
        v((CP, 3 * D), BF), v((CP, D), F32), v((CP, 512), BF), v((CP, 512), BF), v((CP, 512), BF), v((256, 512), F32),
        v((2, 96, D), BF), v((2, 96, D), BF), v((2, 96, D), BF),
        v((4, 256, 768), BF), v((4, STRIPS, 16, 128), BF), v((4, STRIPS, 16, 128), BF), v((7, 16, D), F32),
        v((D, D), BF), v((D, D), BF), v((768, D), BF), v((256, D), BF), v((4, 256, 768), BF), v((16, D), F32),
        v((128, D), BF), v((128, D), F32), v((43, D), BF), v((1, D), F32), v((1, D), F32), v((1, D), F32),
        pltpu.SemaphoreType.DMA((23,)), pltpu.SemaphoreType.REGULAR((6,)),
        pltpu.SemaphoreType.DMA((SENDS,)), pltpu.SemaphoreType.DMA((RECVS,)),
    ]
    return pl.pallas_call(
        layer_body,
        out_shape=outs,
        in_specs=[ANY] * 10 + [SMEM] * 3 + [ANY] * 3,
        out_specs=(ANY,) * 9,
        scratch_shapes=scratch,
        compiler_params=pltpu.CompilerParams(collective_id=0, has_side_effects=True, vmem_limit_bytes=62 << 20),
    )(*args)


def widen_body(lout, sqz, gin, down, up, sq, outp, t, s, *refs):
    (o_lout, o_sqz, o_gin, o_again, o_q, o_kv, o_out, o_slopes, o_fgain, o_up, o_ubias, o_down, o_sq) = refs[:13]
    tin, lin, kv_wide, q_wide, wide, b_lout, b_gin, b_s, b_sqz, r_again, r_fgain, r_ubias, r_slopes, sem_in, sem_out = refs[13:]
    loads = []

    def load(src, dst):
        cp = pltpu.make_async_copy(src, dst, sem_in.at[len(loads)])
        cp.start()
        loads.append(cp)
        return cp

    s_load = load(s, b_s)
    t_load = load(t, tin)
    pieces = []
    for src, dst, n in ((down, o_down, 4), (up, o_up, 4), (sq, o_sq, 3), (outp, o_out, 1)):
        for i in range(n):
            k = len(pieces)
            pieces.append((load(src.at[pl.ds(256 * i, 256)], lin.at[k]), dst.at[pl.ds(256 * i, 256)]))
    plain = [(load(lout, b_lout), b_lout, o_lout), (load(gin, b_gin), b_gin, o_gin), (load(sqz, b_sqz), b_sqz, o_sqz)]
    stores = []

    def leave(src, dst):
        stores.append(pltpu.make_async_copy(src, dst, sem_out.at[len(stores)]))
        stores[-1].start()

    s_load.wait()
    for row, to, dst in ((0, r_again, o_again), (1, r_fgain, o_fgain), (8, r_ubias, o_ubias)):
        to[...] = b_s[row : row + 1, :]
        leave(to, dst)
    r_slopes[...] = b_s[2:3, 0:8]
    leave(r_slopes, o_slopes)
    t_load.wait()
    for b in range(4):
        for part in range(2):
            kv_wide[:, pl.ds(part * D + b * 256, 256)] = tin[b, :, part * 256 : part * 256 + 256].astype(F32)
        q_wide[:, pl.ds(b * 256, 256)] = tin[b, :, 512:768].astype(F32)
    leave(kv_wide, o_kv)
    leave(q_wide, o_q)
    for i, (cp, dst) in enumerate(pieces):
        cp.wait()
        wide[i] = lin[i].astype(F32)
        leave(wide.at[i], dst)
    for cp, src, dst in plain:
        cp.wait()
        leave(src, dst)
    for cp in stores:
        cp.wait()


def widen(args):
    def out_shape(shape, dtype):
        return jax.ShapeDtypeStruct(shape, dtype)

    outs = (
        out_shape((128, D), BF), out_shape((43, D), BF), out_shape((128, D), F32), out_shape((1, D), F32),
        out_shape((256, D), F32), out_shape((256, 2 * D), F32), out_shape((256, D), F32), out_shape((1, 8), F32),
        out_shape((1, D), F32), out_shape((D, D), F32), out_shape((1, D), F32), out_shape((D, D), F32),
        out_shape((768, D), F32),
    )
    v = pltpu.VMEM
    return pl.pallas_call(
        widen_body,
        out_shape=outs,
        in_specs=[ANY] * 9,
        out_specs=(ANY,) * 13,
        scratch_shapes=[
            v((4, 256, 768), BF), v((12, 256, D), BF), v((256, 2 * D), F32), v((256, D), F32), v((12, 256, D), F32),
            v((128, D), BF), v((128, D), F32), v((16, D), F32), v((43, D), BF),
            v((1, D), F32), v((1, D), F32), v((1, D), F32), v((1, 8), F32),
            pltpu.SemaphoreType.DMA((17,)), pltpu.SemaphoreType.DMA((21,)),
        ],
        compiler_params=pltpu.CompilerParams(vmem_limit_bytes=62 << 20),
    )(*args)


def per_device(
    layer_in, memory, squeezed_mem, memory_fill, squeezed_fill, grad_out, attn_gain, w_query, w_keyval,
    w_output, slopes, ffn_gain, w_up, up_bias, w_down, w_squeeze,
):
    done = layer((
        layer_in[0], memory[0], squeezed_mem[0], grad_out[0], w_query, w_keyval, w_output, w_up, w_down, w_squeeze,
        memory_fill, squeezed_fill, slopes, attn_gain[None], ffn_gain[None], up_bias[None],
    ))
    lout, sqz, gin, again, q, kv, out, slope, fgain, up, ubias, down, sq = widen(done)
    return (
        lout[None], sqz[None], gin[None], again[0], q, kv, out, slope[0], fgain[0], up, ubias[0], down, sq,
    )


def solution(mesh):
    rows = P("dp", "mp", None)
    in_specs = (
        rows, rows, rows, P("dp"), P("dp"), rows, P(), P(), P(), P(), P(), P(), P(None, "mp"), P("mp"), P("mp", None), P(),
    )
    out_specs = (
        rows, rows, rows, P(), P("mp", None), P("mp", None), P("mp", None), P(), P(), P(None, "mp"), P("mp"), P("mp", None), P("mp", None),
    )
    return jax.shard_map(per_device, mesh=mesh, in_specs=in_specs, out_specs=out_specs, check_vma=False)
```

```python
import functools

import jax
import jax.numpy as jnp
from jax import lax
from jax.experimental import pallas as pl
from jax.experimental.pallas import tpu as pltpu
from jax.sharding import PartitionSpec as P

D = 1024
H = 8
DH = 128
S = 512
M = 512
C = 512
CN = 172
CP = 192
EPS = 1e-05
NEG = -1e30
SCALE = DH ** (-0.5)
RECON = -2.0 / (S * D)
MESH = pl.DeviceIdType.MESH
BF = jnp.bfloat16
F32 = jnp.float32
VMEM = pl.BlockSpec(memory_space=pltpu.VMEM)
SMEM = pl.BlockSpec(memory_space=pltpu.SMEM)
ANY = pl.BlockSpec(memory_space=pl.ANY)
STRIPS = 6
SEG, MEM, OLD, GOUT = 0, 1, 2, 3
BASE = {OLD: 0, MEM: 512, SEG: 1024}
ORDER = (
    "send.s", "psend.m", "psend.o", "psend.s", "own.s", "par.m", "send.m", "arr.s", "far.s", "own.o", "own.m",
    "par.s", "pjo.s", "send.o", "dia.s", "pjf.s", "at.s.1", "par.o", "arr.m", "pjo.m", "far.m", "pjo.o", "at.s.0",
    "dia.m", "send.g", "psend.g", "pjf.m", "arr.o", "at.m.0", "far.o", "at.m.1", "dia.o", "pjf.o", "at.o.1", "at.o.0",
    "combine", "arr.g", "squeeze", "mf1", "gh0", "mix0a", "fw0", "mix1a", "mix0b", "ffn0", "fw1", "gh1",
    "mix1b", "ffn1", "gnmo", "down", "gnmw", "gS0", "f1", "up", "r1", "gS1", "f0", "s1", "s0", "lnb0", "D0", "dsq",
    "U0", "lnb1", "sqS", "D1", "xout", "att0.0", "U1", "att0.1", "att0", "sqT", "D2", "att1.0", "att1.1", "xsq",
    "att1", "t.0", "U2", "t.1", "t.2", "t", "D3", "S0", "Q0", "T0", "O0", "U3", "Q1", "D4", "T1", "O1", "S1", "Q2",
    "D5", "T2", "U4", "Q3", "S2", "D6", "T3", "Q4", "dno", "U5", "T4", "sego", "O2", "D7", "segw", "O3", "U6", "Q5",
    "S3", "dnw", "O4", "dnS", "T5", "Q6", "T6", "O5", "D8", "S4", "segS", "U7", "T7", "S5", "O6", "lout", "Q7", "T8",
    "O7", "gin", "S6", "Q8", "U8", "O8", "T9",
)
SENDS = 116
RECVS = 252


def dp_places():
    dp = lax.axis_index("dp")
    y, x, z = dp // 8, (dp // 2) % 4, dp % 2
    xa, xb = x + 1 - 2 * (x % 2), 3 - x
    ya, yb = y + 1 - 2 * (y % 2), 3 - y
    cube = [
        ((x + x // 2) % 2, y * 8 + xa * 2 + z),
        ((y + y // 2) % 2, ya * 8 + x * 2 + z),
        (x // 2, y * 8 + xb * 2 + z),
        (y // 2, yb * 8 + x * 2 + z),
    ]
    return cube, y * 8 + x * 2 + (1 - z)


def mp_places():
    mp = lax.axis_index("mp")
    zl, core = mp // 2, mp % 2
    return mp, zl, core, zl * 2 + (1 - core), (1 - zl) * 2 + core


class Flight:
    def __init__(self, links, cp, send, recv):
        self.links, self.cp, self.send, self.recv = links, cp, send, recv

    def wait_send(self):
        self.cp.wait_send()
        self.links.spare.append(self.send)

    def wait_recv(self):
        self.cp.wait_recv()

    def wait(self):
        self.wait_send()
        self.wait_recv()


class Links:
    def __init__(self, ssem, rsem):
        self.ssem, self.rsem, self.spare, self.sends, self.recvs = ssem, rsem, [], 0, 0

    def start(self, src, dst, place, like=None):
        if self.spare:
            k = self.spare.pop(0)
        else:
            k, self.sends = self.sends, self.sends + 1
        if like is not None:
            r = like.recv
        else:
            r, self.recvs = self.recvs, self.recvs + 1
        cp = pltpu.make_async_remote_copy(
            src_ref=src, dst_ref=dst, send_sem=self.ssem.at[k], recv_sem=self.rsem.at[r],
            device_id=place, device_id_type=MESH,
        )
        cp.start()
        return Flight(self, cp, k, r)

    def mp(self, src, dst, peer):
        return self.start(src, dst, (lax.axis_index("dp"), peer))

    def dp(self, src, dst, peer, like=None):
        return self.start(src, dst, (peer, lax.axis_index("mp")), like)


def loop(total, step, body, init=None):
    def run(i, carry):
        return body(pl.multiple_of(i * step, step), carry)

    return lax.fori_loop(0, total // step, run, init)


def each(total, step, body):
    def run(r, carry):
        body(r)
        return carry

    loop(total, step, run, 0)


def add_into(dst, dst_at, src, src_at, rows):
    step = 128 if rows % 128 == 0 else 64 if rows % 64 == 0 else 16

    def body(r):
        to, at = dst_at(r, step), src_at(r, step)
        dst[to] = dst[to] + src[at]

    each(rows, step, body)


def quarters(row0, rows, orders):
    return [(row0, rows, 256 * q, 256, order) for q, order in enumerate(orders)]


CUBE_FIRST = ((0, 1, 2, 3, 4), (1, 2, 3, 0, 4), (2, 3, 0, 1, 4), (3, 0, 1, 2, 4))
Z_FIRST = ((4, 0, 1, 2, 3), (4, 1, 2, 3, 0), (4, 2, 3, 0, 1), (4, 3, 0, 1, 2))


class Pieces:
    last = 8

    def __init__(self, links, ref, recv, base, free, pieces):
        self.links, self.ref, self.recv, self.base, self.free, self.pieces = links, ref, recv, base, free, pieces
        cube, zp = dp_places()
        self.dims = cube + [(lax.axis_index("dp") % 2, zp)]
        self.at = [[p[0]] for p in pieces]
        self.flying, self.sent, self.stage, self.out = [None] * len(pieces), [], 0, [[] for _ in pieces]
        self.back = [[[] for _ in range(4)] for _ in pieces]

    def launch(self, i, s):
        row0, n, col0, width, order = self.pieces[i]
        cols = pl.ds(col0, width)
        room = self.base + row0 + n - (n >> s)
        bit, peer = self.dims[order[s]]
        if s < 4:
            half = n >> (s + 1)
            give = pl.multiple_of(self.at[i][s] + (1 - bit) * half, 16)
            self.at[i].append(pl.multiple_of(self.at[i][s] + bit * half, 16))
        else:
            half, give = n >> 4, self.at[i][4]
        cp = self.links.dp(self.ref.at[pl.ds(give, half), cols], self.recv.at[pl.ds(room, half), cols], peer)
        self.out[i].append(cp)
        self.flying[i] = cp

    def give_back(self, i, k, later):
        row0, n, col0, width, order = self.pieces[i]
        start, size, like = self.at[i][min(k + 2, 4)], n >> min(k + 2, 4), self.out[i][k]
        if later:
            start, like = pl.multiple_of(2 * self.at[i][k + 1] + size - start, 16), None
        here = self.ref.at[pl.ds(start, size), pl.ds(col0, width)]
        self.back[i][k].append(self.links.dp(here, here, self.dims[order[k]][1], like))

    def begin(self):
        for i in range(len(self.pieces)):
            self.launch(i, 0)

    def advance(self):
        s = self.stage
        if s == 4:
            pl.semaphore_wait(self.free, 5)
        earlier, self.sent = self.sent, []
        for i, (row0, n, col0, width, _) in enumerate(self.pieces):
            if s > 4:
                k = 8 - s
                for cp in self.back[i][k]:
                    cp.wait_recv()
                self.back[i][k][0].wait_send()
                self.sent.extend(self.back[i][k][1:])
                if k >= 1:
                    self.give_back(i, k - 1, True)
                if k >= 2:
                    self.give_back(i, k - 2, False)
                continue
            cp, cols = self.flying[i], pl.ds(col0, width)
            if s == 4:
                cp.wait_send()
            else:
                self.sent.append(cp)
            cp.wait_recv()
            room, here = self.base + row0 + n - (n >> s), self.at[i][min(s + 1, 4)]
            add_into(
                self.ref, lambda r, m: (pl.ds(here + r, m), cols),
                self.recv, lambda r, m: (pl.ds(room + r, m), cols), n >> min(s + 1, 4),
            )
            if s < 4:
                self.launch(i, s + 1)
            else:
                self.give_back(i, 3, False)
                self.give_back(i, 2, False)
        for cp in earlier:
            cp.wait_send()
        if s == 3:
            for cp in self.sent:
                cp.wait_send()
            self.sent = []
            for _, peer in self.dims:
                pl.semaphore_signal(self.free, inc=1, device_id=(peer, lax.axis_index("mp")), device_id_type=MESH)
        self.stage += 1

    def finish(self):
        for cp in self.sent:
            cp.wait_send()


DOWN_PIECES = quarters(0, 1024, CUBE_FIRST)
UP_PIECES = quarters(0, 1024, CUBE_FIRST)
SQ_PIECES = quarters(0, 512, CUBE_FIRST) + quarters(512, 256, Z_FIRST)


class Strips:
    last = 9

    def __init__(self, links, ref, recv, pack, got, free):
        self.links, self.ref, self.recv, self.pack, self.got, self.free = links, ref, recv, pack, got, free
        self.cube, self.zp = dp_places()
        self.at = [[0] for _ in range(4)]
        self.flying, self.sent, self.stage, self.out = [], [], 0, []
        self.back = [[[] for _ in range(4)] for _ in range(STRIPS)]

    def launch(self, s):
        ref = self.ref
        self.flying = []
        if s < 4:
            for q in range(4):
                bit, _ = self.cube[(q + s) % 4]
                self.at[q].append(pl.multiple_of(self.at[q][s] + bit * (256 >> (s + 1)), 16))
        for j in range(STRIPS):
            q, cols = j % 4, pl.ds(128 * j, 128)
            if s < 4:
                bit, peer = self.cube[(q + s) % 4]
                half = 256 >> (s + 1)
                give = pl.multiple_of(self.at[q][s] + (1 - bit) * half, 16)
                cp = self.links.dp(
                    ref.at[:, pl.ds(give, half), cols], self.recv.at[:, pl.ds(256 - (256 >> s), half), cols], peer
                )
            else:
                cp = self.links.dp(ref.at[:, pl.ds(self.at[q][4], 16), cols], self.recv.at[:, pl.ds(240, 16), cols], self.zp)
            self.flying.append(cp)
        self.out.append(self.flying)

    def give_back(self, j, k, later):
        at = self.at[j % 4]
        start, size, like = at[min(k + 2, 4)], 256 >> min(k + 2, 4), self.out[k][j]
        if later:
            start, like = pl.multiple_of(2 * at[k + 1] + size - start, 16), None
        here = self.ref.at[:, pl.ds(start, size), pl.ds(128 * j, 128)]
        self.back[j][k].append(self.links.dp(here, here, self.cube[(j % 4 + k) % 4][1], like))

    def begin(self):
        self.launch(0)

    def advance(self):
        s = self.stage
        mp, zl, core, part, far = mp_places()
        earlier, self.sent = self.sent, []
        if s > 5:
            k = 9 - s
            for j in range(STRIPS):
                for cp in self.back[j][k]:
                    cp.wait_recv()
                self.back[j][k][0].wait_send()
                self.sent.extend(self.back[j][k][1:])
                if k >= 1:
                    self.give_back(j, k - 1, True)
                if k >= 2:
                    self.give_back(j, k - 2, False)
        elif s == 5:
            for cp in self.flying:
                cp.wait()
            self.got[mp] = self.pack[mp]
            for j in range(STRIPS):
                self.ref[:, pl.ds(self.at[j % 4][4], 16), pl.ds(128 * j, 128)] = self.got[:, j]
            pl.semaphore_wait(self.free, 4)
            for j in range(STRIPS):
                self.give_back(j, 3, False)
                self.give_back(j, 2, False)
        else:
            for j, cp in enumerate(self.flying):
                cols = pl.ds(128 * j, 128)
                if s == 4:
                    cp.wait_send()
                else:
                    self.sent.append(cp)
                cp.wait_recv()
                rows, room, here = 256 >> min(s + 1, 4), 256 - (256 >> s), self.at[j % 4][min(s + 1, 4)]
                add_into(
                    self.ref, lambda r, m: (slice(None), pl.ds(here + r, m), cols),
                    self.recv, lambda r, m: (slice(None), pl.ds(room + r, m), cols), rows,
                )
            if s == 3:
                for cp in self.sent:
                    cp.wait_send()
                self.sent = []
                for _, peer in self.cube:
                    pl.semaphore_signal(self.free, inc=1, device_id=(peer, mp), device_id_type=MESH)
            if s == 4:
                for j in range(STRIPS):
                    self.pack[:, j] = self.ref[:, pl.ds(self.at[j % 4][4], 16), pl.ds(128 * j, 128)]
                self.flying = [self.links.mp(self.pack.at[peer], self.got.at[mp], peer) for peer in (part, far, 3 - mp)]
            else:
                self.launch(s + 1)
        for cp in earlier:
            cp.wait_send()
        self.stage += 1

    def finish(self):
        for cp in self.sent:
            cp.wait_send()


class Smalls:
    last = 6

    def __init__(self, links, ref, recv):
        self.links, self.ref, self.recv, self.stage = links, ref, recv, 0
        cube, zp = dp_places()
        self.peers = [peer for _, peer in cube] + [zp]

    def begin(self):
        s = self.stage
        mp, zl, core, part, far = mp_places()
        self.rows = pl.ds(0, 16 if s < 5 else 8)
        src, dst = self.ref.at[self.rows], self.recv.at[s, self.rows]
        if s < 5:
            self.cp = self.links.dp(src, dst, self.peers[s])
        else:
            self.cp = self.links.mp(src, dst, (part, far)[s - 5])

    def advance(self):
        if self.stage > 6:
            return
        self.cp.wait()
        self.ref[self.rows, :] = self.ref[self.rows, :] + self.recv[self.stage, self.rows, :]
        self.stage += 1
        if self.stage <= 6:
            self.begin()

    def finish(self):
        pass


def dg(a, b, left=1, right=0):
    return lax.dot_general(a, b, (((left,), (right,)), ((), ())), preferred_element_type=F32)


def normalize(rows):
    centre = rows - jnp.mean(rows, axis=-1, keepdims=True)
    inv = lax.rsqrt(jnp.mean(centre * centre, axis=-1, keepdims=True) + EPS)
    return centre * inv, inv


def norm_back(grad, gain, unit, inv):
    g = grad * gain
    return inv * (g - jnp.mean(g, axis=-1, keepdims=True) - unit * jnp.mean(g * unit, axis=-1, keepdims=True))


def iota(shape, dim):
    return lax.broadcasted_iota(jnp.int32, shape, dim)


def fold(x, op):
    out = x[:8]
    for i in range(1, x.shape[0] // 8):
        out = op(out, x[8 * i : 8 * i + 8])
    return out


def layer_body(
    seg_in, mem_in, old_in, gout_in, wq_in, wkv_in, wo_in, wup_in, wdn_in, wsq_in,
    mfill, sfill, slopes, again_in, fgain_in, ubias_in,
    lout_out, sqz_out, gin_out, down_out, up_out, sq_out, out_out, t_out, s_out,
    raw, normed, wkvq, wo, wup, wdn, wsq, kv, query, expo, tmp, tmp2, stat, acc, mixt, mixg, mid, nm, hid, gpre,
    out, got, keep, out2, got2, gb, gmix, gkv, gq, win, sqz, skv, esq, gsq, rec, sbuf, sgot, sqsum, trecv, tpack, tgot, srecv,
    x_down, x_up, x_sq, x_out, t_ref, s_ref, lout, gin, sqz_rows, again, fgain, ubias, lsem, free, ssem, rsem,
):
    links = Links(ssem, rsem)
    mp, zl, core, part, far = mp_places()
    diag = 3 - mp
    cube, zp = dp_places()
    dp = lax.axis_index("dp")
    mine = pl.ds(pl.multiple_of(mp * 256, 256), 256)

    sem = pltpu.get_barrier_semaphore()
    for peer in [peer for _, peer in cube] + [zp]:
        pl.semaphore_signal(sem, inc=1, device_id=(peer, mp), device_id_type=MESH)
    for peer in (part, far, diag):
        pl.semaphore_signal(sem, inc=1, device_id=(dp, peer), device_id_type=MESH)

    ins = {SEG: seg_in, MEM: mem_in, OLD: old_in, GOUT: gout_in}
    own_loads = {}
    nlocal = [0]

    def load(src, dst):
        cp = pltpu.make_async_copy(src, dst, lsem.at[nlocal[0]])
        nlocal[0] += 1
        cp.start()
        return cp

    for a in (SEG, MEM, OLD, GOUT):
        own_loads[a] = load(ins[a], raw.at[a, mp])
    gains = [load(again_in, again), load(fgain_in, fgain), load(ubias_in, ubias)]
    w_loads = [
        load(wkv_in.at[:, mine], wkvq.at[:, pl.ds(0, 256)]),
        load(wkv_in.at[:, pl.ds(pl.multiple_of(D + mp * 256, 256), 256)], wkvq.at[:, pl.ds(256, 256)]),
        load(wq_in.at[:, mine], wkvq.at[:, pl.ds(512, 256)]),
    ]

    pl.semaphore_wait(sem, 8)

    done = []

    far_cp, part_cp, fwd_cp = {}, {}, {}
    sq_load = load(wsq_in, wsq)
    late_loads = [load(wo_in, wo), load(wup_in, wup), load(wdn_in, wdn)]
    mem_limit = M - mfill[0]
    old_limit = C - sfill[0]

    def slope_of(h):
        return slopes[mp * 2 + h]

    def heads(h):
        return pl.ds(h * DH, DH)

    def column(r, rows):
        return iota((rows, 1), 0) + r

    def exponentials(src, dst, dst0, rows, colmask, causal=False):
        step = 64

        def one(r, top):
            s = src[pl.ds(r, step), :] * SCALE + colmask(r, step)
            if causal:
                s = jnp.where(iota((step, 512), 0) + r <= iota((step, 512), 1), s, NEG)
            src[pl.ds(r, step), :] = s
            return jnp.maximum(top, fold(s, jnp.maximum))

        top = loop(rows, step, one, jnp.full((8, 512), NEG, F32))
        top = jnp.max(top, axis=0, keepdims=True)

        def two(r, total):
            e = jnp.exp(src[pl.ds(r, step), :] - top).astype(BF)
            dst[pl.ds(dst0 + r, step), :] = e
            return total + fold(e.astype(F32), jnp.add)

        total = loop(rows, step, two, jnp.zeros((8, 512), F32))
        return top, jnp.sum(total, axis=0, keepdims=True)

    def attend(h, a):
        base = BASE[a]
        rows = pl.ds(base, 512)
        g = base // 512
        tmp[...] = dg(kv[rows, heads(h)], query[:, heads(h)], 1, 1)
        slope = slope_of(h)

        def colmask(r, step):
            j = column(r, step)
            bias = slope * (j + (base - 1536)).astype(F32)
            if a == MEM:
                bias = jnp.where(j >= mem_limit, bias, NEG)
            if a == OLD:
                bias = jnp.where(j >= old_limit, bias, NEG)
            return bias

        top, total = exponentials(tmp, expo.at[h], base, 512, colmask, a == SEG)
        stat[h * 6 + g : h * 6 + g + 1, :] = top
        stat[h * 6 + 3 + g : h * 6 + 4 + g, :] = total
        acc[h * 3 + g] = dg(kv[rows, pl.ds(256 + h * DH, DH)], expo[h, rows, :], 0, 0)

    def first_of(h):
        rows = pl.ds(BASE[MEM], 512)
        tmp[...] = dg(kv[rows, heads(h)], query[:, heads(h)], 1, 1)
        _, total = exponentials(
            tmp, gkv, 0, 512, lambda r, step: jnp.where(column(r, step) >= mem_limit, 0.0, NEG)
        )
        rec[heads(h), :] = dg(kv[rows, pl.ds(256 + h * DH, DH)], gkv[0:512, :], 0, 0) / total

    tasks, ran = {}, set()

    def task(name, *after):
        def keep_it(run):
            tasks[name] = (run, after)
            return run

        return keep_it

    sums = {
        "D": Pieces(links, x_down, wsq, 0, free.at[1], DOWN_PIECES),
        "U": Pieces(links, x_up, wsq, 1024, free.at[2], UP_PIECES),
        "Q": Pieces(links, x_sq, wsq, 2048, free.at[3], SQ_PIECES),
        "O": Pieces(links, x_out, wsq, 2816, free.at[4], quarters(0, 256, [CUBE_FIRST[q] for q in (2, 3, 2, 3)])),
        "T": Strips(links, t_ref, trecv, tpack, tgot, free.at[5]),
        "S": Smalls(links, s_ref, srecv),
    }
    results = {"D": (x_down, down_out), "U": (x_up, up_out), "Q": (x_sq, sq_out), "O": (x_out, out_out), "T": (t_ref, t_out), "S": (s_ref, s_out)}
    flights = {}
    leaving, roomy = [], []
    bias_rows = [jnp.zeros((8, 512), F32)] * 2
    totals = {"gain": jnp.zeros((1, D), F32), "slope": jnp.zeros((1, D), F32), "bias": bias_rows}

    def begin(name):
        if not roomy:
            pl.semaphore_wait(free.at[0], 5)
            roomy.append(True)
        sums[name].begin()

    def half_rows(z):
        return pl.ds(z * 256, 256)

    def block(z, other):
        return pl.ds(pl.multiple_of((2 * z + ((1 - core) if other else core)) * 128, 128), 128)

    waited = set()

    def once(name, copies):
        if name not in waited:
            waited.add(name)
            for cp in copies:
                cp.wait()

    def norm_rows(a, owner):
        once("gains", gains)
        unit, _ = normalize(raw[a, owner].astype(F32))
        normed[pl.ds(pl.multiple_of(BASE[a] + owner * 128, 128), 128), :] = (unit * again[...]).astype(BF)

    def send_rows(a, copies, peer):
        copies[a] = links.mp(ins[a], raw.at[a, mp], peer)
        done.append(copies[a])

    def norm_own(a):
        own_loads[a].wait()
        norm_rows(a, mp)

    def norm_part(a):
        part_cp[a].wait_recv()
        norm_rows(a, part)

    def arrive(a):
        far_cp[a].wait_recv()
        fwd_cp[a] = links.mp(raw.at[a, far], raw.at[a, far], part)
        done.append(fwd_cp[a])

    def norm_diag(a):
        fwd_cp[a].wait_recv()
        norm_rows(a, diag)

    def project(a, chip):
        once("wkvq", w_loads)
        own = pl.ds(pl.multiple_of(chip * 256, 256), 256)
        rows = pl.ds(pl.multiple_of(BASE[a] + chip * 256, 256), 256)
        kv[rows, :] = dg(normed[rows, :], wkvq[:, 0:512]).astype(BF)
        if a == SEG:
            query[own, :] = dg(normed[rows, :], wkvq[:, 512:768]).astype(BF)

    for c, a in (("s", SEG), ("m", MEM), ("o", OLD), ("g", GOUT)):
        task(f"send.{c}")(functools.partial(send_rows, a, far_cp, far))
        task(f"psend.{c}")(functools.partial(send_rows, a, part_cp, part))
        task(f"arr.{c}", f"send.{c}")(functools.partial(arrive, a))
        if a != GOUT:
            task(f"own.{c}")(functools.partial(norm_own, a))
            task(f"par.{c}", f"psend.{c}")(functools.partial(norm_part, a))
            task(f"far.{c}", f"arr.{c}")(functools.partial(norm_rows, a, far))
            task(f"dia.{c}", f"arr.{c}")(functools.partial(norm_diag, a))
            task(f"pjo.{c}", f"own.{c}", f"par.{c}")(functools.partial(project, a, zl))
            task(f"pjf.{c}", f"far.{c}", f"dia.{c}")(functools.partial(project, a, 1 - zl))
            for h in range(2):
                task(f"at.{c}.{h}", f"pjo.{c}", f"pjf.{c}", "pjo.s", "pjf.s")(functools.partial(attend, h, a))

    @task("combine", *(f"at.{c}.{h}" for c in "smo" for h in range(2)))
    def _():
        for h in range(2):
            tops = [stat[h * 6 + g : h * 6 + g + 1, :] for g in range(3)]
            sums = [stat[h * 6 + 3 + g : h * 6 + 4 + g, :] for g in range(3)]
            top = jnp.maximum(jnp.maximum(tops[0], tops[1]), tops[2])
            scales = [jnp.exp(t - top) for t in tops]
            total = scales[0] * sums[0] + scales[1] * sums[1] + scales[2] * sums[2]
            mixed = jnp.zeros((DH, 512), F32)
            for g in range(3):
                inv = scales[g] / total
                stat[12 + h * 3 + g : 13 + h * 3 + g, :] = inv
                mixed = mixed + acc[h * 3 + g] * inv
            mixt[heads(h), :] = mixed
            mixg[mp, :, heads(h)] = mixed.T.astype(BF)
        for z in range(2):
            here = mixg.at[mp, half_rows(z)]
            flights["mix_part", z] = links.mp(here, here, part)
            done.append(flights["mix_part", z])
        send_mix(0)

    def send_mix(z):
        here = mixg.at[mp, half_rows(z)]
        flights["mix_far", z] = links.mp(here, here, far)
        done.append(flights["mix_far", z])

    task("mf1", "combine")(functools.partial(send_mix, 1))

    @task("squeeze", "dia.m")
    def _():
        sq_load.wait()
        rows = raw[MEM].reshape(512, D)
        for tap in range(3):
            pick = (iota((CP, 512), 1) == 3 * iota((CP, 512), 0) + tap).astype(BF)
            win[:, tap * D : (tap + 1) * D] = dg(pick, rows).astype(BF)
        for half in range(2):
            cols = pl.ds(half * 512, 512)
            sqz[:, cols] = dg(win[...], wsq[:, cols])
        for peer in [peer for _, peer in cube] + [zp]:
            pl.semaphore_signal(free.at[0], inc=1, device_id=(peer, mp), device_id_type=MESH)

    @task("r1", "squeeze")
    def _():
        pick = (iota((48, CP), 1) == iota((48, CP), 0) + mp * 43).astype(BF)
        sqz_rows[...] = dg(pick, sqz[...].astype(BF))[0:43].astype(BF)
        leaving.append(load(sqz_rows, sqz_out))
        unit, _ = normalize(sqz[...])
        skv[...] = dg((unit * again[...]).astype(BF), wkvq[:, 0:512]).astype(BF)

    for h in range(2):
        task(f"f{h}", "pjo.m", "pjf.m", "pjo.s", "pjf.s")(functools.partial(first_of, h))

    def second_of(h):
        keys, values = skv[:, heads(h)], skv[:, pl.ds(256 + h * DH, DH)]
        tmp[0:CP, :] = dg(keys, query[:, heads(h)], 1, 1)

        def colmask(r, step):
            slot = column(r, step)
            return jnp.where((3 * slot < M) & (3 * slot + 2 >= mem_limit), 0.0, NEG)

        _, total = exponentials(tmp, esq, 0, CP, colmask)
        inv = 1.0 / total
        second = dg(values, esq[...], 0, 0) * inv
        grad = (rec[heads(h), :] - second) * RECON
        inner = inv * jnp.sum(grad * second, axis=0, keepdims=True)
        scaled = (grad * inv).astype(BF)
        gsq[:, pl.ds(256 + h * DH, DH)] = dg(esq[...], scaled, 1, 1).astype(BF)
        gp = dg(values, scaled)
        gs = (esq[...].astype(F32) * (gp - inner)).astype(BF)
        gsq[:, heads(h)] = (dg(gs, query[:, heads(h)]) * SCALE).astype(BF)

    for h in range(2):
        task(f"s{h}", "r1", f"f{h}", "pjo.s", "pjf.s")(functools.partial(second_of, h))

    @task("dsq", "s0", "s1")
    def _():
        unit, inv = normalize(sqz[...])
        sqz[...] = norm_back(dg(gsq[...], wkvq[:, 0:512], 1, 1), again[...], unit, inv)
        sbuf[0] = sqz[pl.ds(pl.multiple_of((1 - core) * 96, 16), 96), :].astype(BF)
        flights["sq_part"] = links.mp(sbuf.at[0], sgot.at[0], part)
        done.append(flights["sq_part"])

    @task("sqS", "dsq")
    def _():
        flights["sq_part"].wait_recv()
        sbuf[1] = (sqz[pl.ds(pl.multiple_of(core * 96, 16), 96), :] + sgot[0].astype(F32)).astype(BF)
        flights["sq_far"] = links.mp(sbuf.at[1], sgot.at[1], far)

    @task("sqT", "sqS")
    def _():
        flights["sq_far"].wait()
        sqsum[core] = (sbuf[1].astype(F32) + sgot[1].astype(F32)).astype(BF)
        flights["sq_back"] = links.mp(sqsum.at[core], sqsum.at[core], part)

    @task("xsq", "sqT")
    def _():
        flights["sq_back"].wait()
        for half in range(2):
            cols = pl.ds(half * 512, 512)
            x_sq[:, cols] = dg(win[:, pl.ds(pl.multiple_of(mp * 768, 256), 768)], sqsum[:, :, cols].reshape(CP, 512), 0, 0).astype(BF)
        begin("Q")

    def mix_into(z, owners, first=False):
        rows = half_rows(z)
        for half in range(2):
            cols = pl.ds(half * 512, 512)
            base = raw[SEG, 2 * z : 2 * z + 2, :, cols].reshape(256, 512).astype(F32) if first else mid[rows, cols]
            for owner in owners:
                base = base + dg(mixg[owner, rows, :], wo[pl.ds(pl.multiple_of(owner * 256, 256), 256), cols])
            mid[rows, cols] = base

    def mix_own(z):
        once("weights", late_loads)
        flights["mix_part", z].wait_recv()
        mix_into(z, (mp, part), True)

    def forward_mix(z):
        flights["mix_far", z].wait_recv()
        here = mixg.at[far, half_rows(z)]
        flights["mix_fwd", z] = links.mp(here, here, part)
        done.append(flights["mix_fwd", z])

    def grad_hidden(z):
        once("weights", late_loads)
        if z == 0:
            own_loads[GOUT].wait()
            part_cp[GOUT].wait_recv()
            fwd_cp[GOUT].wait_recv()
        for half in range(2):
            cols = pl.ds(half * 512, 512)
            keep[z, :, :, cols] = dg(raw[GOUT, 2 * z : 2 * z + 2].reshape(256, D), wdn[cols, :], 1, 1).reshape(2, 128, 512)

    def feed_forward(z):
        flights["mix_fwd", z].wait_recv()
        mix_into(z, (diag,))
        rows = half_rows(z)
        for i in range(2):
            at = pl.ds(z * 256 + i * 128, 128)
            unit, _ = normalize(mid[at, :])
            nm[at, :] = (unit * fgain[...]).astype(BF)
        for half in range(2):
            cols = pl.ds(half * 512, 512)
            tmp[half_rows(half), :] = dg(nm[rows, :], wup[:, cols])
        for half, i in ((0, 0), (0, 1), (1, 0), (1, 1)):
            cols = pl.ds(half * 512, 512)

            def gelu(r, total):
                to = pl.ds(r + z * 256 + i * 128, 64)
                v = tmp[pl.ds(r + half * 256 + i * 128, 64), :] + ubias[:, cols]
                square = v * v
                th = jnp.tanh(0.7978845608028654 * v * (1.0 + 0.044715 * square))
                hid[to, cols] = (0.5 * v * (1.0 + th)).astype(BF)
                slope = 0.5 * (1.0 + th) + (0.5 * 0.7978845608028654) * v * (1.0 - th * th) * (1.0 + 3 * 0.044715 * square)
                g = (slope * keep[z, i, pl.ds(r, 64), cols]).astype(BF)
                gpre[to, cols] = g
                return total + fold(g.astype(F32), jnp.add)

            totals["bias"][half] = loop(128, 64, gelu, totals["bias"][half])
        if z == 1:
            for half in range(2):
                s_ref[8:9, pl.ds(half * 512, 512)] = jnp.sum(totals["bias"][half], axis=0, keepdims=True)

    for z in range(2):
        task(f"mix{z}a", "combine", *(["mix0a"] if z else []))(functools.partial(mix_own, z))
        task(f"fw{z}", "combine", *(["fw0", "mf1"] if z else []))(functools.partial(forward_mix, z))
        task(f"gh{z}", "arr.g", "psend.g", *(["gh0"] if z else []))(functools.partial(grad_hidden, z))
        task(f"mix{z}b", f"mix{z}a", f"fw{z}")(functools.partial(mix_into, z, (far,)))
        task(f"ffn{z}", f"mix{z}b", f"gh{z}", *(["ffn0"] if z else []))(functools.partial(feed_forward, z))

    def tiles(dst, left, right):
        for half in range(2):
            rows = pl.ds(half * 512, 512)
            for quarter in range(2):
                cols = pl.ds(quarter * 512, 512)
                dst[rows, cols] = dg(left(rows), right(cols), 0, 0).astype(BF)

    @task("down", "ffn1", "squeeze")
    def _():
        tiles(x_down, lambda rows: hid[:, rows], lambda cols: raw[GOUT, :, :, cols].reshape(512, 512))
        begin("D")

    @task("up", "ffn1", "squeeze")
    def _():
        tiles(x_up, lambda rows: nm[:, rows], lambda cols: gpre[:, cols])
        begin("U")

    @task("gnmo", "ffn1")
    def _():
        for z in range(2):
            out[0, z] = dg(gpre[block(z, True), :], wup[...], 1, 1).astype(BF)
            flights["gnm_part", z] = links.mp(out.at[0, z], got.at[0, z], part)

    @task("gnmw", "gnmo")
    def _():
        for z in range(2):
            keep[0, z] = dg(gpre[block(z, False), :], wup[...], 1, 1)

    def gnm_sum(z):
        flights["gnm_part", z].wait_recv()
        out2[z] = (keep[0, z] + got[0, z].astype(F32)).astype(BF)
        flights["gnm_far", z] = links.mp(out2.at[z], got2.at[z], far)

    @task("dno", "ffn1")
    def _():
        for z in range(2):
            out[1, z] = dg(hid[block(z, True), :], wdn[...]).astype(BF)
            flights["down_part", z] = links.mp(out.at[1, z], got.at[1, z], part)
            done.append(flights["down_part", z])

    @task("dnw", "ffn1")
    def _():
        for z in range(2):
            keep[1, z] = dg(hid[block(z, False), :], wdn[...])

    @task("dnS", "dno", "dnw")
    def _():
        for z in range(2):
            flights["down_part", z].wait_recv()
        out2[2] = (keep[1, 1 - zl] + got[1, 1 - zl].astype(F32)).astype(BF)
        flights["down_far"] = links.mp(out2.at[2], got2.at[2], far)

    @task("lout", "dnS")
    def _():
        flights["down_far"].wait()
        lout[...] = (
            mid[pl.ds(pl.multiple_of(mp * 128, 128), 128), :]
            + keep[1, zl] + got[1, zl].astype(F32) + got2[2].astype(F32)
        ).astype(BF)
        leaving.append(load(lout, lout_out))

    def norm_mid_back(z):
        flights["gnm_far", z].wait()
        rows = block(z, False)
        unit, inv = normalize(mid[rows, :])
        g = out2[z].astype(F32) + got2[z].astype(F32)
        totals["gain"] = totals["gain"] + jnp.sum(g * unit, axis=0, keepdims=True) * jnp.where(zl == z, 1.0, 0.0)
        gmid = raw[GOUT, 2 * z + core].astype(F32) + norm_back(g, fgain[...], unit, inv)
        keep[0, z] = gmid
        gb[z, core] = gmid.astype(BF)
        flights["gb", z] = links.mp(gb.at[z, core], gb.at[z, core], part)
        if z == 1:
            s_ref[1:2, :] = totals["gain"]

    for z in range(2):
        task(f"gS{z}", "gnmw", *(["gS0"] if z else []))(functools.partial(gnm_sum, z))
        task(f"lnb{z}", f"gS{z}", *(["lnb0"] if z else []))(functools.partial(norm_mid_back, z))

    @task("xout", "lnb1", "squeeze")
    def _():
        for z in range(2):
            flights["gb", z].wait()
        gmix[...] = dg(wo[mine, :], gb[...].reshape(512, D), 1, 1)
        for half in range(2):
            cols = pl.ds(half * 512, 512)
            x_out[:, cols] = dg(mixg[mp], gb[:, :, :, cols].reshape(512, 512), 0, 0).astype(BF)
        begin("O")

    carried = {}

    def attend_back(h, a):
        base = BASE[a]
        rows = pl.ds(base, 512)
        grad = gmix[heads(h), :]
        if a == OLD:
            carried["inner"] = jnp.sum(grad * mixt[heads(h), :], axis=0, keepdims=True)
            carried["slope"] = jnp.zeros((8, 512), F32)
        inv = stat[12 + h * 3 + base // 512 : 13 + h * 3 + base // 512, :]
        scaled = (grad * inv).astype(BF)
        shift = inv * carried["inner"]
        tmp[...] = dg(kv[rows, pl.ds(256 + h * DH, DH)], scaled)
        gkv[rows, pl.ds(256 + h * DH, DH)] = dg(expo[h, rows, :], scaled, 1, 1).astype(BF)

        def score_grads(r, total):
            at = pl.ds(base + r, 64)
            gs = (expo[h, at, :].astype(F32) * (tmp[pl.ds(r, 64), :] - shift)).astype(BF)
            expo[h, at, :] = gs
            dist = (iota((64, 512), 1) - iota((64, 512), 0) + (1024 - base - r)).astype(F32)
            return total + fold(gs.astype(F32) * dist, jnp.add)

        carried["slope"] = loop(512, 64, score_grads, carried["slope"])
        gkv[rows, heads(h)] = (dg(expo[h, rows, :], query[:, heads(h)]) * SCALE).astype(BF)
        if a == SEG:
            gqt = dg(kv[:, heads(h)], expo[h], 0, 0)
            gq[:, heads(h)] = (gqt * SCALE).T.astype(BF)
            value = -jnp.sum(jnp.sum(carried["slope"], axis=0, keepdims=True), axis=1, keepdims=True)
            totals["slope"] = totals["slope"] + jnp.where(iota((1, D), 1) == mp * 2 + h, value, 0.0)

    before = ("xout", "f0", "f1")
    for h in range(2):
        for name, a in ((f"att{h}.0", OLD), (f"att{h}.1", MEM), (f"att{h}", SEG)):
            task(name, *before)(functools.partial(attend_back, h, a))
            before = (name,)

    def projections(b):
        feats = pl.ds(b * 256, 256)
        big = dg(normed[:, feats], gkv[...], 0, 0)
        small = dg(normed[1024:1536, feats], gq[...], 0, 0)
        t_ref[b, :, 0:512] = big.astype(BF)
        t_ref[b, :, 512:768] = small.astype(BF)
        terms = small[:, 0:128] * wkvq[feats, 512:640].astype(F32) + small[:, 128:256] * wkvq[feats, 640:768].astype(F32)
        for j in range(4):
            terms = terms + big[:, j * 128 : (j + 1) * 128] * wkvq[feats, j * 128 : (j + 1) * 128].astype(F32)
        s_ref[0:1, feats] = jnp.sum(terms.T, axis=0, keepdims=True) / again[:, feats]
        if b == 3:
            begin("T")
            s_ref[2:3, :] = totals["slope"]
            s_ref[3:8, :] = jnp.zeros((5, D), F32)
            s_ref[9:16, :] = jnp.zeros((7, D), F32)
            begin("S")

    for b in range(4):
        task(("t.0", "t.1", "t.2", "t")[b], "att1", *([("t.0", "t.1", "t.2")[b - 1]] if b else []))(functools.partial(projections, b))

    def seg_terms(z, other):
        rows = block(z, other)
        at = pl.ds(pl.multiple_of(BASE[SEG] + (2 * z + ((1 - core) if other else core)) * 128, 128), 128)
        return dg(gkv[at, :], wkvq[:, 0:512], 1, 1) + dg(gq[rows, :], wkvq[:, 512:768], 1, 1)

    @task("sego", "att1")
    def _():
        for z in range(2):
            flights["gnm_part", z].wait_send()
            out[0, z] = seg_terms(z, True).astype(BF)
            flights["seg_part", z] = links.mp(out.at[0, z], got.at[0, z], part)
            done.append(flights["seg_part", z])

    @task("segw", "att1")
    def _():
        for z in range(2):
            terms = seg_terms(z, False)
            for half in range(2):
                tmp2[(2 * z + half) * 128 : (2 * z + half + 1) * 128, :] = terms[:, half * 512 : (half + 1) * 512]

    @task("segS", "sego", "segw")
    def _():
        for z in range(2):
            flights["seg_part", z].wait_recv()
        for half in range(2):
            cols = pl.ds(half * 512, 512)
            at = pl.ds(pl.multiple_of((2 * (1 - zl) + half) * 128, 128), 128)
            out2[3, :, cols] = (tmp2[at, :] + got[0, 1 - zl, :, cols].astype(F32)).astype(BF)
        flights["seg_far"] = links.mp(out2.at[3], got2.at[3], far)

    @task("gin", "segS")
    def _():
        flights["seg_far"].wait()
        unit, inv = normalize(raw[SEG, mp].astype(F32))
        own = [tmp2[pl.ds(pl.multiple_of((2 * zl + half) * 128, 128), 128), :] for half in range(2)]
        total = jnp.concatenate(own, axis=1) + got[0, zl].astype(F32) + got2[3].astype(F32)
        gin[...] = keep[0, zl] + norm_back(total, again[...], unit, inv)
        leaving.append(load(gin, gin_out))

    for name in ORDER:
        if name in tasks:
            run, after = tasks[name]
            assert all(other in ran for other in after), name
            run()
        else:
            part_sum = sums[name[0]]
            assert part_sum.stage == int(name[1:]), name
            part_sum.advance()
            if part_sum.stage > part_sum.last:
                leaving.append(load(*results[name[0]]))
        ran.add(name)
    assert len(ran) == len(tasks) + sum(part_sum.last + 1 for part_sum in sums.values())
    for part_sum in sums.values():
        part_sum.finish()
    for cp in leaving:
        cp.wait()
    for cp in done:
        cp.wait_send()
    assert links.sends <= SENDS and links.recvs <= RECVS, (links.sends, links.recvs)


def layer(args):
    def out_shape(shape, dtype):
        return jax.ShapeDtypeStruct(shape, dtype)

    outs = (
        out_shape((128, D), BF), out_shape((43, D), BF), out_shape((128, D), F32), out_shape((1024, D), BF),
        out_shape((1024, D), BF), out_shape((768, D), BF), out_shape((256, D), BF), out_shape((4, 256, 768), BF),
        out_shape((16, D), F32),
    )
    v = pltpu.VMEM
    scratch = [
        v((4, 4, 128, D), BF), v((1536, D), BF), v((D, 768), BF), v((D, D), BF), v((D, D), BF), v((D, D), BF),
        v((3072, D), BF), v((1536, 512), BF), v((512, 256), BF), v((2, 1536, 512), BF), v((512, 512), F32),
        v((512, 512), F32), v((24, 512), F32), v((6, DH, 512), F32), v((256, 512), F32), v((4, 512, 256), BF),
        v((512, D), F32), v((512, D), BF), v((512, D), BF), v((512, D), BF),
        v((2, 2, 128, D), BF), v((2, 2, 128, D), BF), v((2, 2, 128, D), F32), v((4, 128, D), BF), v((4, 128, D), BF),
        v((2, 2, 128, D), BF), v((256, 512), F32), v((1536, 512), BF), v((512, 256), BF),
        v((CP, 3 * D), BF), v((CP, D), F32), v((CP, 512), BF), v((CP, 512), BF), v((CP, 512), BF), v((256, 512), F32),
        v((2, 96, D), BF), v((2, 96, D), BF), v((2, 96, D), BF),
        v((4, 256, 768), BF), v((4, STRIPS, 16, 128), BF), v((4, STRIPS, 16, 128), BF), v((7, 16, D), F32),
        v((D, D), BF), v((D, D), BF), v((768, D), BF), v((256, D), BF), v((4, 256, 768), BF), v((16, D), F32),
        v((128, D), BF), v((128, D), F32), v((43, D), BF), v((1, D), F32), v((1, D), F32), v((1, D), F32),
        pltpu.SemaphoreType.DMA((23,)), pltpu.SemaphoreType.REGULAR((6,)),
        pltpu.SemaphoreType.DMA((SENDS,)), pltpu.SemaphoreType.DMA((RECVS,)),
    ]
    return pl.pallas_call(
        layer_body,
        out_shape=outs,
        in_specs=[ANY] * 10 + [SMEM] * 3 + [ANY] * 3,
        out_specs=(ANY,) * 9,
        scratch_shapes=scratch,
        compiler_params=pltpu.CompilerParams(collective_id=0, has_side_effects=True, vmem_limit_bytes=62 << 20),
    )(*args)


def widen_body(lout, sqz, gin, down, up, sq, outp, t, s, *refs):
    (o_lout, o_sqz, o_gin, o_again, o_q, o_kv, o_out, o_slopes, o_fgain, o_up, o_ubias, o_down, o_sq) = refs[:13]
    tin, lin, kv_wide, q_wide, wide, b_lout, b_gin, b_s, b_sqz, r_again, r_fgain, r_ubias, r_slopes, sem_in, sem_out = refs[13:]
    loads = []

    def load(src, dst):
        cp = pltpu.make_async_copy(src, dst, sem_in.at[len(loads)])
        cp.start()
        loads.append(cp)
        return cp

    s_load = load(s, b_s)
    t_load = load(t, tin)
    pieces = []
    for src, dst, n in ((down, o_down, 4), (up, o_up, 4), (sq, o_sq, 3), (outp, o_out, 1)):
        for i in range(n):
            k = len(pieces)
            pieces.append((load(src.at[pl.ds(256 * i, 256)], lin.at[k]), dst.at[pl.ds(256 * i, 256)]))
    plain = [(load(lout, b_lout), b_lout, o_lout), (load(gin, b_gin), b_gin, o_gin), (load(sqz, b_sqz), b_sqz, o_sqz)]
    stores = []

    def leave(src, dst):
        stores.append(pltpu.make_async_copy(src, dst, sem_out.at[len(stores)]))
        stores[-1].start()

    s_load.wait()
    for row, to, dst in ((0, r_again, o_again), (1, r_fgain, o_fgain), (8, r_ubias, o_ubias)):
        to[...] = b_s[row : row + 1, :]
        leave(to, dst)
    r_slopes[...] = b_s[2:3, 0:8]
    leave(r_slopes, o_slopes)
    t_load.wait()
    for b in range(4):
        for part in range(2):
            kv_wide[:, pl.ds(part * D + b * 256, 256)] = tin[b, :, part * 256 : part * 256 + 256].astype(F32)
        q_wide[:, pl.ds(b * 256, 256)] = tin[b, :, 512:768].astype(F32)
    leave(kv_wide, o_kv)
    leave(q_wide, o_q)
    for i, (cp, dst) in enumerate(pieces):
        cp.wait()
        wide[i] = lin[i].astype(F32)
        leave(wide.at[i], dst)
    for cp, src, dst in plain:
        cp.wait()
        leave(src, dst)
    for cp in stores:
        cp.wait()


def widen(args):
    def out_shape(shape, dtype):
        return jax.ShapeDtypeStruct(shape, dtype)

    outs = (
        out_shape((128, D), BF), out_shape((43, D), BF), out_shape((128, D), F32), out_shape((1, D), F32),
        out_shape((256, D), F32), out_shape((256, 2 * D), F32), out_shape((256, D), F32), out_shape((1, 8), F32),
        out_shape((1, D), F32), out_shape((D, D), F32), out_shape((1, D), F32), out_shape((D, D), F32),
        out_shape((768, D), F32),
    )
    v = pltpu.VMEM
    return pl.pallas_call(
        widen_body,
        out_shape=outs,
        in_specs=[ANY] * 9,
        out_specs=(ANY,) * 13,
        scratch_shapes=[
            v((4, 256, 768), BF), v((12, 256, D), BF), v((256, 2 * D), F32), v((256, D), F32), v((12, 256, D), F32),
            v((128, D), BF), v((128, D), F32), v((16, D), F32), v((43, D), BF),
            v((1, D), F32), v((1, D), F32), v((1, D), F32), v((1, 8), F32),
            pltpu.SemaphoreType.DMA((17,)), pltpu.SemaphoreType.DMA((21,)),
        ],
        compiler_params=pltpu.CompilerParams(vmem_limit_bytes=62 << 20),
    )(*args)


def per_device(
    layer_in, memory, squeezed_mem, memory_fill, squeezed_fill, grad_out, attn_gain, w_query, w_keyval,
    w_output, slopes, ffn_gain, w_up, up_bias, w_down, w_squeeze,
):
    done = layer((
        layer_in[0], memory[0], squeezed_mem[0], grad_out[0], w_query, w_keyval, w_output, w_up, w_down, w_squeeze,
        memory_fill, squeezed_fill, slopes, attn_gain[None], ffn_gain[None], up_bias[None],
    ))
    lout, sqz, gin, again, q, kv, out, slope, fgain, up, ubias, down, sq = widen(done)
    return (
        lout[None], sqz[None], gin[None], again[0], q, kv, out, slope[0], fgain[0], up, ubias[0], down, sq,
    )


def solution(mesh):
    rows = P("dp", "mp", None)
    in_specs = (
        rows, rows, rows, P("dp"), P("dp"), rows, P(), P(), P(), P(), P(), P(), P(None, "mp"), P("mp"), P("mp", None), P(),
    )
    out_specs = (
        rows, rows, rows, P(), P("mp", None), P("mp", None), P("mp", None), P(), P(), P(None, "mp"), P("mp"), P("mp", None), P("mp", None),
    )
    return jax.shard_map(per_device, mesh=mesh, in_specs=in_specs, out_specs=out_specs, check_vma=False)
```

```python
import functools

import jax
import jax.numpy as jnp
from jax import lax
from jax.experimental import pallas as pl
from jax.experimental.pallas import tpu as pltpu
from jax.sharding import PartitionSpec as P

D = 1024
H = 8
DH = 128
S = 512
M = 512
C = 512
CN = 172
CP = 192
EPS = 1e-05
NEG = -1e30
SCALE = DH ** (-0.5)
RECON = -2.0 / (S * D)
MESH = pl.DeviceIdType.MESH
BF = jnp.bfloat16
F32 = jnp.float32
VMEM = pl.BlockSpec(memory_space=pltpu.VMEM)
SMEM = pl.BlockSpec(memory_space=pltpu.SMEM)
ANY = pl.BlockSpec(memory_space=pl.ANY)
STRIPS = 6
SEG, MEM, OLD, GOUT = 0, 1, 2, 3
BASE = {OLD: 0, MEM: 512, SEG: 1024}
ORDER = (
    "send.s", "psend.m", "psend.o", "psend.s", "own.s", "par.m", "send.m", "arr.s", "far.s", "own.o", "own.m",
    "par.s", "pjo.s", "send.o", "dia.s", "pjf.s", "at.s.1", "par.o", "arr.m", "pjo.m", "far.m", "pjo.o", "at.s.0",
    "dia.m", "send.g", "psend.g", "pjf.m", "arr.o", "at.m.0", "far.o", "at.m.1", "dia.o", "pjf.o", "at.o.1", "at.o.0",
    "combine", "arr.g", "squeeze", "mf1", "gh0", "mix0a", "fw0", "mix1a", "mix0b", "ffn0", "fw1", "gh1",
    "mix1b", "ffn1", "gnmo", "down", "gnmw", "gS0", "f1", "up", "r1", "gS1", "f0", "s1", "s0", "lnb0", "D0", "dsq",
    "U0", "lnb1", "sqS", "D1", "xout", "att0.0", "U1", "att0.1", "att0", "sqT", "D2", "att1.0", "att1.1", "xsq",
    "att1", "t.0", "U2", "t.1", "t.2", "t", "D3", "S0", "Q0", "T0", "O0", "U3", "Q1", "D4", "T1", "O1", "S1", "Q2",
    "D5", "T2", "U4", "Q3", "S2", "D6", "T3", "Q4", "dno", "U5", "T4", "sego", "O2", "D7", "segw", "O3", "U6", "Q5",
    "S3", "dnw", "O4", "dnS", "T5", "Q6", "T6", "O5", "D8", "S4", "segS", "U7", "T7", "S5", "O6", "lout", "Q7", "T8",
    "O7", "gin", "S6", "Q8", "U8", "O8", "T9",
)
SENDS = 116
RECVS = 252


def dp_places():
    dp = lax.axis_index("dp")
    y, x, z = dp // 8, (dp // 2) % 4, dp % 2
    xa, xb = x + 1 - 2 * (x % 2), 3 - x
    ya, yb = y + 1 - 2 * (y % 2), 3 - y
    cube = [
        ((x + x // 2) % 2, y * 8 + xa * 2 + z),
        ((y + y // 2) % 2, ya * 8 + x * 2 + z),
        (x // 2, y * 8 + xb * 2 + z),
        (y // 2, yb * 8 + x * 2 + z),
    ]
    return cube, y * 8 + x * 2 + (1 - z)


def mp_places():
    mp = lax.axis_index("mp")
    zl, core = mp // 2, mp % 2
    return mp, zl, core, zl * 2 + (1 - core), (1 - zl) * 2 + core


class Flight:
    def __init__(self, links, cp, send, recv):
        self.links, self.cp, self.send, self.recv = links, cp, send, recv

    def wait_send(self):
        self.cp.wait_send()
        self.links.spare.append(self.send)

    def wait_recv(self):
        self.cp.wait_recv()

    def wait(self):
        self.wait_send()
        self.wait_recv()


class Links:
    def __init__(self, ssem, rsem):
        self.ssem, self.rsem, self.spare, self.sends, self.recvs = ssem, rsem, [], 0, 0

    def start(self, src, dst, place, like=None):
        if self.spare:
            k = self.spare.pop(0)
        else:
            k, self.sends = self.sends, self.sends + 1
        if like is not None:
            r = like.recv
        else:
            r, self.recvs = self.recvs, self.recvs + 1
        cp = pltpu.make_async_remote_copy(
            src_ref=src, dst_ref=dst, send_sem=self.ssem.at[k], recv_sem=self.rsem.at[r],
            device_id=place, device_id_type=MESH,
        )
        cp.start()
        return Flight(self, cp, k, r)

    def mp(self, src, dst, peer):
        return self.start(src, dst, (lax.axis_index("dp"), peer))

    def dp(self, src, dst, peer, like=None):
        return self.start(src, dst, (peer, lax.axis_index("mp")), like)


def loop(total, step, body, init=None):
    def run(i, carry):
        return body(pl.multiple_of(i * step, step), carry)

    return lax.fori_loop(0, total // step, run, init)


def each(total, step, body):
    def run(r, carry):
        body(r)
        return carry

    loop(total, step, run, 0)


def add_into(dst, dst_at, src, src_at, rows):
    step = 128 if rows % 128 == 0 else 64 if rows % 64 == 0 else 16

    def body(r):
        to, at = dst_at(r, step), src_at(r, step)
        dst[to] = dst[to] + src[at]

    each(rows, step, body)


def quarters(row0, rows, orders):
    return [(row0, rows, 256 * q, 256, order) for q, order in enumerate(orders)]


CUBE_FIRST = ((0, 1, 2, 3, 4), (1, 2, 3, 0, 4), (2, 3, 0, 1, 4), (3, 0, 1, 2, 4))
Z_FIRST = ((4, 0, 1, 2, 3), (4, 1, 2, 3, 0), (4, 2, 3, 0, 1), (4, 3, 0, 1, 2))


class Pieces:
    last = 8

    def __init__(self, links, ref, recv, base, free, pieces):
        self.links, self.ref, self.recv, self.base, self.free, self.pieces = links, ref, recv, base, free, pieces
        cube, zp = dp_places()
        self.dims = cube + [(lax.axis_index("dp") % 2, zp)]
        self.at = [[p[0]] for p in pieces]
        self.flying, self.sent, self.stage, self.out = [None] * len(pieces), [], 0, [[] for _ in pieces]
        self.back = [[[] for _ in range(4)] for _ in pieces]

    def launch(self, i, s):
        row0, n, col0, width, order = self.pieces[i]
        cols = pl.ds(col0, width)
        room = self.base + row0 + n - (n >> s)
        bit, peer = self.dims[order[s]]
        if s < 4:
            half = n >> (s + 1)
            give = pl.multiple_of(self.at[i][s] + (1 - bit) * half, 16)
            self.at[i].append(pl.multiple_of(self.at[i][s] + bit * half, 16))
        else:
            half, give = n >> 4, self.at[i][4]
        cp = self.links.dp(self.ref.at[pl.ds(give, half), cols], self.recv.at[pl.ds(room, half), cols], peer)
        self.out[i].append(cp)
        self.flying[i] = cp

    def give_back(self, i, k, later):
        row0, n, col0, width, order = self.pieces[i]
        start, size, like = self.at[i][min(k + 2, 4)], n >> min(k + 2, 4), self.out[i][k]
        if later:
            start, like = pl.multiple_of(2 * self.at[i][k + 1] + size - start, 16), None
        here = self.ref.at[pl.ds(start, size), pl.ds(col0, width)]
        self.back[i][k].append(self.links.dp(here, here, self.dims[order[k]][1], like))

    def begin(self):
        for i in range(len(self.pieces)):
            self.launch(i, 0)

    def advance(self):
        s = self.stage
        if s == 4:
            pl.semaphore_wait(self.free, 5)
        earlier, self.sent = self.sent, []
        for i, (row0, n, col0, width, _) in enumerate(self.pieces):
            if s > 4:
                k = 8 - s
                for cp in self.back[i][k]:
                    cp.wait_recv()
                self.back[i][k][0].wait_send()
                self.sent.extend(self.back[i][k][1:])
                if k >= 1:
                    self.give_back(i, k - 1, True)
                if k >= 2:
                    self.give_back(i, k - 2, False)
                continue
            cp, cols = self.flying[i], pl.ds(col0, width)
            if s == 4:
                cp.wait_send()
            else:
                self.sent.append(cp)
            cp.wait_recv()
            room, here = self.base + row0 + n - (n >> s), self.at[i][min(s + 1, 4)]
            add_into(
                self.ref, lambda r, m: (pl.ds(here + r, m), cols),
                self.recv, lambda r, m: (pl.ds(room + r, m), cols), n >> min(s + 1, 4),
            )
            if s < 4:
                self.launch(i, s + 1)
            else:
                self.give_back(i, 3, False)
                self.give_back(i, 2, False)
        for cp in earlier:
            cp.wait_send()
        if s == 3:
            for cp in self.sent:
                cp.wait_send()
            self.sent = []
            for _, peer in self.dims:
                pl.semaphore_signal(self.free, inc=1, device_id=(peer, lax.axis_index("mp")), device_id_type=MESH)
        self.stage += 1

    def finish(self):
        for cp in self.sent:
            cp.wait_send()


DOWN_PIECES = quarters(0, 1024, CUBE_FIRST)
UP_PIECES = quarters(0, 1024, CUBE_FIRST)
SQ_PIECES = quarters(0, 512, CUBE_FIRST) + quarters(512, 256, Z_FIRST)


class Strips:
    last = 9

    def __init__(self, links, ref, recv, pack, got, free):
        self.links, self.ref, self.recv, self.pack, self.got, self.free = links, ref, recv, pack, got, free
        self.cube, self.zp = dp_places()
        self.at = [[0] for _ in range(4)]
        self.flying, self.sent, self.stage, self.out = [], [], 0, []
        self.back = [[[] for _ in range(4)] for _ in range(STRIPS)]

    def launch(self, s):
        ref = self.ref
        self.flying = []
        if s < 4:
            for q in range(4):
                bit, _ = self.cube[(q + s) % 4]
                self.at[q].append(pl.multiple_of(self.at[q][s] + bit * (256 >> (s + 1)), 16))
        for j in range(STRIPS):
            q, cols = j % 4, pl.ds(128 * j, 128)
            if s < 4:
                bit, peer = self.cube[(q + s) % 4]
                half = 256 >> (s + 1)
                give = pl.multiple_of(self.at[q][s] + (1 - bit) * half, 16)
                cp = self.links.dp(
                    ref.at[:, pl.ds(give, half), cols], self.recv.at[:, pl.ds(256 - (256 >> s), half), cols], peer
                )
            else:
                cp = self.links.dp(ref.at[:, pl.ds(self.at[q][4], 16), cols], self.recv.at[:, pl.ds(240, 16), cols], self.zp)
            self.flying.append(cp)
        self.out.append(self.flying)

    def give_back(self, j, k, later):
        at = self.at[j % 4]
        start, size, like = at[min(k + 2, 4)], 256 >> min(k + 2, 4), self.out[k][j]
        if later:
            start, like = pl.multiple_of(2 * at[k + 1] + size - start, 16), None
        here = self.ref.at[:, pl.ds(start, size), pl.ds(128 * j, 128)]
        self.back[j][k].append(self.links.dp(here, here, self.cube[(j % 4 + k) % 4][1], like))

    def begin(self):
        self.launch(0)

    def advance(self):
        s = self.stage
        mp, zl, core, part, far = mp_places()
        earlier, self.sent = self.sent, []
        if s > 5:
            k = 9 - s
            for j in range(STRIPS):
                for cp in self.back[j][k]:
                    cp.wait_recv()
                self.back[j][k][0].wait_send()
                self.sent.extend(self.back[j][k][1:])
                if k >= 1:
                    self.give_back(j, k - 1, True)
                if k >= 2:
                    self.give_back(j, k - 2, False)
        elif s == 5:
            for cp in self.flying:
                cp.wait()
            self.got[mp] = self.pack[mp]
            for j in range(STRIPS):
                self.ref[:, pl.ds(self.at[j % 4][4], 16), pl.ds(128 * j, 128)] = self.got[:, j]
            pl.semaphore_wait(self.free, 4)
            for j in range(STRIPS):
                self.give_back(j, 3, False)
                self.give_back(j, 2, False)
        else:
            for j, cp in enumerate(self.flying):
                cols = pl.ds(128 * j, 128)
                if s == 4:
                    cp.wait_send()
                else:
                    self.sent.append(cp)
                cp.wait_recv()
                rows, room, here = 256 >> min(s + 1, 4), 256 - (256 >> s), self.at[j % 4][min(s + 1, 4)]
                add_into(
                    self.ref, lambda r, m: (slice(None), pl.ds(here + r, m), cols),
                    self.recv, lambda r, m: (slice(None), pl.ds(room + r, m), cols), rows,
                )
            if s == 3:
                for cp in self.sent:
                    cp.wait_send()
                self.sent = []
                for _, peer in self.cube:
                    pl.semaphore_signal(self.free, inc=1, device_id=(peer, mp), device_id_type=MESH)
            if s == 4:
                for j in range(STRIPS):
                    self.pack[:, j] = self.ref[:, pl.ds(self.at[j % 4][4], 16), pl.ds(128 * j, 128)]
                self.flying = [self.links.mp(self.pack.at[peer], self.got.at[mp], peer) for peer in (part, far, 3 - mp)]
            else:
                self.launch(s + 1)
        for cp in earlier:
            cp.wait_send()
        self.stage += 1

    def finish(self):
        for cp in self.sent:
            cp.wait_send()


class Smalls:
    last = 6

    def __init__(self, links, ref, recv):
        self.links, self.ref, self.recv, self.stage = links, ref, recv, 0
        cube, zp = dp_places()
        self.peers = [peer for _, peer in cube] + [zp]

    def begin(self):
        s = self.stage
        mp, zl, core, part, far = mp_places()
        self.rows = pl.ds(0, 16 if s < 5 else 8)
        src, dst = self.ref.at[self.rows], self.recv.at[s, self.rows]
        if s < 5:
            self.cp = self.links.dp(src, dst, self.peers[s])
        else:
            self.cp = self.links.mp(src, dst, (part, far)[s - 5])

    def advance(self):
        if self.stage > 6:
            return
        self.cp.wait()
        self.ref[self.rows, :] = self.ref[self.rows, :] + self.recv[self.stage, self.rows, :]
        self.stage += 1
        if self.stage <= 6:
            self.begin()

    def finish(self):
        pass


def dg(a, b, left=1, right=0):
    return lax.dot_general(a, b, (((left,), (right,)), ((), ())), preferred_element_type=F32)


def normalize(rows):
    centre = rows - jnp.mean(rows, axis=-1, keepdims=True)
    inv = lax.rsqrt(jnp.mean(centre * centre, axis=-1, keepdims=True) + EPS)
    return centre * inv, inv


def norm_back(grad, gain, unit, inv):
    g = grad * gain
    return inv * (g - jnp.mean(g, axis=-1, keepdims=True) - unit * jnp.mean(g * unit, axis=-1, keepdims=True))


def iota(shape, dim):
    return lax.broadcasted_iota(jnp.int32, shape, dim)


def fold(x, op):
    out = x[:8]
    for i in range(1, x.shape[0] // 8):
        out = op(out, x[8 * i : 8 * i + 8])
    return out


def layer_body(
    seg_in, mem_in, old_in, gout_in, wq_in, wkv_in, wo_in, wup_in, wdn_in, wsq_in,
    mfill, sfill, slopes, again_in, fgain_in, ubias_in,
    lout_out, sqz_out, gin_out, down_out, up_out, sq_out, out_out, t_out, s_out,
    raw, normed, wkvq, wo, wup, wdn, wsq, kv, query, expo, tmp, tmp2, stat, acc, mixt, mixg, mid, nm, hid, gpre,
    out, got, keep, out2, got2, gb, gmix, gkv, gq, win, sqz, skv, esq, gsq, rec, sbuf, sgot, sqsum, trecv, tpack, tgot, srecv,
    x_down, x_up, x_sq, x_out, t_ref, s_ref, lout, gin, sqz_rows, again, fgain, ubias, lsem, free, ssem, rsem,
):
    links = Links(ssem, rsem)
    mp, zl, core, part, far = mp_places()
    diag = 3 - mp
    cube, zp = dp_places()
    dp = lax.axis_index("dp")
    mine = pl.ds(pl.multiple_of(mp * 256, 256), 256)

    sem = pltpu.get_barrier_semaphore()
    for peer in [peer for _, peer in cube] + [zp]:
        pl.semaphore_signal(sem, inc=1, device_id=(peer, mp), device_id_type=MESH)
    for peer in (part, far, diag):
        pl.semaphore_signal(sem, inc=1, device_id=(dp, peer), device_id_type=MESH)

    ins = {SEG: seg_in, MEM: mem_in, OLD: old_in, GOUT: gout_in}
    own_loads = {}
    nlocal = [0]

    def load(src, dst):
        cp = pltpu.make_async_copy(src, dst, lsem.at[nlocal[0]])
        nlocal[0] += 1
        cp.start()
        return cp

    for a in (SEG, MEM, OLD, GOUT):
        own_loads[a] = load(ins[a], raw.at[a, mp])
    gains = [load(again_in, again), load(fgain_in, fgain), load(ubias_in, ubias)]
    w_loads = [
        load(wkv_in.at[:, mine], wkvq.at[:, pl.ds(0, 256)]),
        load(wkv_in.at[:, pl.ds(pl.multiple_of(D + mp * 256, 256), 256)], wkvq.at[:, pl.ds(256, 256)]),
        load(wq_in.at[:, mine], wkvq.at[:, pl.ds(512, 256)]),
    ]

    pl.semaphore_wait(sem, 8)

    done = []

    far_cp, part_cp, fwd_cp = {}, {}, {}
    sq_load = load(wsq_in, wsq)
    late_loads = [load(wo_in, wo), load(wup_in, wup), load(wdn_in, wdn)]
    mem_limit = M - mfill[0]
    old_limit = C - sfill[0]

    def slope_of(h):
        return slopes[mp * 2 + h]

    def heads(h):
        return pl.ds(h * DH, DH)

    def column(r, rows):
        return iota((rows, 1), 0) + r

    def exponentials(src, dst, dst0, rows, colmask, causal=False):
        step = 64

        def one(r, top):
            s = src[pl.ds(r, step), :] * SCALE + colmask(r, step)
            if causal:
                s = jnp.where(iota((step, 512), 0) + r <= iota((step, 512), 1), s, NEG)
            src[pl.ds(r, step), :] = s
            return jnp.maximum(top, fold(s, jnp.maximum))

        top = loop(rows, step, one, jnp.full((8, 512), NEG, F32))
        top = jnp.max(top, axis=0, keepdims=True)

        def two(r, total):
            e = jnp.exp(src[pl.ds(r, step), :] - top).astype(BF)
            dst[pl.ds(dst0 + r, step), :] = e
            return total + fold(e.astype(F32), jnp.add)

        total = loop(rows, step, two, jnp.zeros((8, 512), F32))
        return top, jnp.sum(total, axis=0, keepdims=True)

    def attend(h, a):
        base = BASE[a]
        rows = pl.ds(base, 512)
        g = base // 512
        tmp[...] = dg(kv[rows, heads(h)], query[:, heads(h)], 1, 1)
        slope = slope_of(h)

        def colmask(r, step):
            j = column(r, step)
            bias = slope * (j + (base - 1536)).astype(F32)
            if a == MEM:
                bias = jnp.where(j >= mem_limit, bias, NEG)
            if a == OLD:
                bias = jnp.where(j >= old_limit, bias, NEG)
            return bias

        top, total = exponentials(tmp, expo.at[h], base, 512, colmask, a == SEG)
        stat[h * 6 + g : h * 6 + g + 1, :] = top
        stat[h * 6 + 3 + g : h * 6 + 4 + g, :] = total
        acc[h * 3 + g] = dg(kv[rows, pl.ds(256 + h * DH, DH)], expo[h, rows, :], 0, 0)

    def first_of(h):
        rows = pl.ds(BASE[MEM], 512)
        tmp[...] = dg(kv[rows, heads(h)], query[:, heads(h)], 1, 1)
        _, total = exponentials(
            tmp, gkv, 0, 512, lambda r, step: jnp.where(column(r, step) >= mem_limit, 0.0, NEG)
        )
        rec[heads(h), :] = dg(kv[rows, pl.ds(256 + h * DH, DH)], gkv[0:512, :], 0, 0) / total

    tasks, ran = {}, set()

    def task(name, *after):
        def keep_it(run):
            tasks[name] = (run, after)
            return run

        return keep_it

    sums = {
        "D": Pieces(links, x_down, wsq, 0, free.at[1], DOWN_PIECES),
        "U": Pieces(links, x_up, wsq, 1024, free.at[2], UP_PIECES),
        "Q": Pieces(links, x_sq, wsq, 2048, free.at[3], SQ_PIECES),
        "O": Pieces(links, x_out, wsq, 2816, free.at[4], quarters(0, 256, [CUBE_FIRST[q] for q in (2, 3, 2, 3)])),
        "T": Strips(links, t_ref, trecv, tpack, tgot, free.at[5]),
        "S": Smalls(links, s_ref, srecv),
    }
    results = {"D": (x_down, down_out), "U": (x_up, up_out), "Q": (x_sq, sq_out), "O": (x_out, out_out), "T": (t_ref, t_out), "S": (s_ref, s_out)}
    flights = {}
    leaving, roomy = [], []
    bias_rows = [jnp.zeros((8, 512), F32)] * 2
    totals = {"gain": jnp.zeros((1, D), F32), "slope": jnp.zeros((1, D), F32), "bias": bias_rows}

    def begin(name):
        if not roomy:
            pl.semaphore_wait(free.at[0], 5)
            roomy.append(True)
        sums[name].begin()

    def half_rows(z):
        return pl.ds(z * 256, 256)

    def block(z, other):
        return pl.ds(pl.multiple_of((2 * z + ((1 - core) if other else core)) * 128, 128), 128)

    waited = set()

    def once(name, copies):
        if name not in waited:
            waited.add(name)
            for cp in copies:
                cp.wait()

    def norm_rows(a, owner):
        once("gains", gains)
        unit, _ = normalize(raw[a, owner].astype(F32))
        normed[pl.ds(pl.multiple_of(BASE[a] + owner * 128, 128), 128), :] = (unit * again[...]).astype(BF)

    def send_rows(a, copies, peer):
        copies[a] = links.mp(ins[a], raw.at[a, mp], peer)
        done.append(copies[a])

    def norm_own(a):
        own_loads[a].wait()
        norm_rows(a, mp)

    def norm_part(a):
        part_cp[a].wait_recv()
        norm_rows(a, part)

    def arrive(a):
        far_cp[a].wait_recv()
        fwd_cp[a] = links.mp(raw.at[a, far], raw.at[a, far], part)
        done.append(fwd_cp[a])

    def norm_diag(a):
        fwd_cp[a].wait_recv()
        norm_rows(a, diag)

    def project(a, chip):
        once("wkvq", w_loads)
        own = pl.ds(pl.multiple_of(chip * 256, 256), 256)
        rows = pl.ds(pl.multiple_of(BASE[a] + chip * 256, 256), 256)
        kv[rows, :] = dg(normed[rows, :], wkvq[:, 0:512]).astype(BF)
        if a == SEG:
            query[own, :] = dg(normed[rows, :], wkvq[:, 512:768]).astype(BF)

    for c, a in (("s", SEG), ("m", MEM), ("o", OLD), ("g", GOUT)):
        task(f"send.{c}")(functools.partial(send_rows, a, far_cp, far))
        task(f"psend.{c}")(functools.partial(send_rows, a, part_cp, part))
        task(f"arr.{c}", f"send.{c}")(functools.partial(arrive, a))
        if a != GOUT:
            task(f"own.{c}")(functools.partial(norm_own, a))
            task(f"par.{c}", f"psend.{c}")(functools.partial(norm_part, a))
            task(f"far.{c}", f"arr.{c}")(functools.partial(norm_rows, a, far))
            task(f"dia.{c}", f"arr.{c}")(functools.partial(norm_diag, a))
            task(f"pjo.{c}", f"own.{c}", f"par.{c}")(functools.partial(project, a, zl))
            task(f"pjf.{c}", f"far.{c}", f"dia.{c}")(functools.partial(project, a, 1 - zl))
            for h in range(2):
                task(f"at.{c}.{h}", f"pjo.{c}", f"pjf.{c}", "pjo.s", "pjf.s")(functools.partial(attend, h, a))

    @task("combine", *(f"at.{c}.{h}" for c in "smo" for h in range(2)))
    def _():
        for h in range(2):
            tops = [stat[h * 6 + g : h * 6 + g + 1, :] for g in range(3)]
            sums = [stat[h * 6 + 3 + g : h * 6 + 4 + g, :] for g in range(3)]
            top = jnp.maximum(jnp.maximum(tops[0], tops[1]), tops[2])
            scales = [jnp.exp(t - top) for t in tops]
            total = scales[0] * sums[0] + scales[1] * sums[1] + scales[2] * sums[2]
            mixed = jnp.zeros((DH, 512), F32)
            for g in range(3):
                inv = scales[g] / total
                stat[12 + h * 3 + g : 13 + h * 3 + g, :] = inv
                mixed = mixed + acc[h * 3 + g] * inv
            mixt[heads(h), :] = mixed
            mixg[mp, :, heads(h)] = mixed.T.astype(BF)
        for z in range(2):
            here = mixg.at[mp, half_rows(z)]
            flights["mix_part", z] = links.mp(here, here, part)
            done.append(flights["mix_part", z])
        send_mix(0)

    def send_mix(z):
        here = mixg.at[mp, half_rows(z)]
        flights["mix_far", z] = links.mp(here, here, far)
        done.append(flights["mix_far", z])

    task("mf1", "combine")(functools.partial(send_mix, 1))

    @task("squeeze", "dia.m")
    def _():
        sq_load.wait()
        rows = raw[MEM].reshape(512, D)
        for tap in range(3):
            pick = (iota((CP, 512), 1) == 3 * iota((CP, 512), 0) + tap).astype(BF)
            win[:, tap * D : (tap + 1) * D] = dg(pick, rows).astype(BF)
        for half in range(2):
            cols = pl.ds(half * 512, 512)
            sqz[:, cols] = dg(win[...], wsq[:, cols])
        for peer in [peer for _, peer in cube] + [zp]:
            pl.semaphore_signal(free.at[0], inc=1, device_id=(peer, mp), device_id_type=MESH)

    @task("r1", "squeeze")
    def _():
        pick = (iota((48, CP), 1) == iota((48, CP), 0) + mp * 43).astype(BF)
        sqz_rows[...] = dg(pick, sqz[...].astype(BF)).astype(BF)
        leaving.append(load(sqz_rows, sqz_out))
        unit, _ = normalize(sqz[...])
        skv[...] = dg((unit * again[...]).astype(BF), wkvq[:, 0:512]).astype(BF)

    for h in range(2):
        task(f"f{h}", "pjo.m", "pjf.m", "pjo.s", "pjf.s")(functools.partial(first_of, h))

    def second_of(h):
        keys, values = skv[:, heads(h)], skv[:, pl.ds(256 + h * DH, DH)]
        tmp[0:CP, :] = dg(keys, query[:, heads(h)], 1, 1)

        def colmask(r, step):
            slot = column(r, step)
            return jnp.where((3 * slot < M) & (3 * slot + 2 >= mem_limit), 0.0, NEG)

        _, total = exponentials(tmp, esq, 0, CP, colmask)
        inv = 1.0 / total
        second = dg(values, esq[...], 0, 0) * inv
        grad = (rec[heads(h), :] - second) * RECON
        inner = inv * jnp.sum(grad * second, axis=0, keepdims=True)
        scaled = (grad * inv).astype(BF)
        gsq[:, pl.ds(256 + h * DH, DH)] = dg(esq[...], scaled, 1, 1).astype(BF)
        gp = dg(values, scaled)
        gs = (esq[...].astype(F32) * (gp - inner)).astype(BF)
        gsq[:, heads(h)] = (dg(gs, query[:, heads(h)]) * SCALE).astype(BF)

    for h in range(2):
        task(f"s{h}", "r1", f"f{h}", "pjo.s", "pjf.s")(functools.partial(second_of, h))

    @task("dsq", "s0", "s1")
    def _():
        unit, inv = normalize(sqz[...])
        sqz[...] = norm_back(dg(gsq[...], wkvq[:, 0:512], 1, 1), again[...], unit, inv)
        sbuf[0] = sqz[pl.ds(pl.multiple_of((1 - core) * 96, 16), 96), :].astype(BF)
        flights["sq_part"] = links.mp(sbuf.at[0], sgot.at[0], part)
        done.append(flights["sq_part"])

    @task("sqS", "dsq")
    def _():
        flights["sq_part"].wait_recv()
        sbuf[1] = (sqz[pl.ds(pl.multiple_of(core * 96, 16), 96), :] + sgot[0].astype(F32)).astype(BF)
        flights["sq_far"] = links.mp(sbuf.at[1], sgot.at[1], far)

    @task("sqT", "sqS")
    def _():
        flights["sq_far"].wait()
        sqsum[core] = (sbuf[1].astype(F32) + sgot[1].astype(F32)).astype(BF)
        flights["sq_back"] = links.mp(sqsum.at[core], sqsum.at[core], part)

    @task("xsq", "sqT")
    def _():
        flights["sq_back"].wait()
        for half in range(2):
            cols = pl.ds(half * 512, 512)
            x_sq[:, cols] = dg(win[:, pl.ds(pl.multiple_of(mp * 768, 256), 768)], sqsum[:, :, cols].reshape(CP, 512), 0, 0).astype(BF)
        begin("Q")

    def mix_into(z, owners, first=False):
        rows = half_rows(z)
        for half in range(2):
            cols = pl.ds(half * 512, 512)
            base = raw[SEG, 2 * z : 2 * z + 2, :, cols].reshape(256, 512).astype(F32) if first else mid[rows, cols]
            for owner in owners:
                base = base + dg(mixg[owner, rows, :], wo[pl.ds(pl.multiple_of(owner * 256, 256), 256), cols])
            mid[rows, cols] = base

    def mix_own(z):
        once("weights", late_loads)
        flights["mix_part", z].wait_recv()
        mix_into(z, (mp, part), True)

    def forward_mix(z):
        flights["mix_far", z].wait_recv()
        here = mixg.at[far, half_rows(z)]
        flights["mix_fwd", z] = links.mp(here, here, part)
        done.append(flights["mix_fwd", z])

    def grad_hidden(z):
        once("weights", late_loads)
        if z == 0:
            own_loads[GOUT].wait()
            part_cp[GOUT].wait_recv()
            fwd_cp[GOUT].wait_recv()
        for half in range(2):
            cols = pl.ds(half * 512, 512)
            keep[z, :, :, cols] = dg(raw[GOUT, 2 * z : 2 * z + 2].reshape(256, D), wdn[cols, :], 1, 1).reshape(2, 128, 512)

    def feed_forward(z):
        flights["mix_fwd", z].wait_recv()
        mix_into(z, (diag,))
        rows = half_rows(z)
        for i in range(2):
            at = pl.ds(z * 256 + i * 128, 128)
            unit, _ = normalize(mid[at, :])
            nm[at, :] = (unit * fgain[...]).astype(BF)
        for half in range(2):
            cols = pl.ds(half * 512, 512)
            tmp[half_rows(half), :] = dg(nm[rows, :], wup[:, cols])
        for half, i in ((0, 0), (0, 1), (1, 0), (1, 1)):
            cols = pl.ds(half * 512, 512)

            def gelu(r, total):
                to = pl.ds(r + z * 256 + i * 128, 64)
                v = tmp[pl.ds(r + half * 256 + i * 128, 64), :] + ubias[:, cols]
                square = v * v
                th = jnp.tanh(0.7978845608028654 * v * (1.0 + 0.044715 * square))
                hid[to, cols] = (0.5 * v * (1.0 + th)).astype(BF)
                slope = 0.5 * (1.0 + th) + (0.5 * 0.7978845608028654) * v * (1.0 - th * th) * (1.0 + 3 * 0.044715 * square)
                g = (slope * keep[z, i, pl.ds(r, 64), cols]).astype(BF)
                gpre[to, cols] = g
                return total + fold(g.astype(F32), jnp.add)

            totals["bias"][half] = loop(128, 64, gelu, totals["bias"][half])
        if z == 1:
            for half in range(2):
                s_ref[8:9, pl.ds(half * 512, 512)] = jnp.sum(totals["bias"][half], axis=0, keepdims=True)

    for z in range(2):
        task(f"mix{z}a", "combine", *(["mix0a"] if z else []))(functools.partial(mix_own, z))
        task(f"fw{z}", "combine", *(["fw0", "mf1"] if z else []))(functools.partial(forward_mix, z))
        task(f"gh{z}", "arr.g", "psend.g", *(["gh0"] if z else []))(functools.partial(grad_hidden, z))
        task(f"mix{z}b", f"mix{z}a", f"fw{z}")(functools.partial(mix_into, z, (far,)))
        task(f"ffn{z}", f"mix{z}b", f"gh{z}", *(["ffn0"] if z else []))(functools.partial(feed_forward, z))

    def tiles(dst, left, right):
        for half in range(2):
            rows = pl.ds(half * 512, 512)
            for quarter in range(2):
                cols = pl.ds(quarter * 512, 512)
                dst[rows, cols] = dg(left(rows), right(cols), 0, 0).astype(BF)

    @task("down", "ffn1", "squeeze")
    def _():
        tiles(x_down, lambda rows: hid[:, rows], lambda cols: raw[GOUT, :, :, cols].reshape(512, 512))
        begin("D")

    @task("up", "ffn1", "squeeze")
    def _():
        tiles(x_up, lambda rows: nm[:, rows], lambda cols: gpre[:, cols])
        begin("U")

    @task("gnmo", "ffn1")
    def _():
        for z in range(2):
            out[0, z] = dg(gpre[block(z, True), :], wup[...], 1, 1).astype(BF)
            flights["gnm_part", z] = links.mp(out.at[0, z], got.at[0, z], part)

    @task("gnmw", "gnmo")
    def _():
        for z in range(2):
            keep[0, z] = dg(gpre[block(z, False), :], wup[...], 1, 1)

    def gnm_sum(z):
        flights["gnm_part", z].wait_recv()
        out2[z] = (keep[0, z] + got[0, z].astype(F32)).astype(BF)
        flights["gnm_far", z] = links.mp(out2.at[z], got2.at[z], far)

    @task("dno", "ffn1")
    def _():
        for z in range(2):
            out[1, z] = dg(hid[block(z, True), :], wdn[...]).astype(BF)
            flights["down_part", z] = links.mp(out.at[1, z], got.at[1, z], part)
            done.append(flights["down_part", z])

    @task("dnw", "ffn1")
    def _():
        for z in range(2):
            keep[1, z] = dg(hid[block(z, False), :], wdn[...])

    @task("dnS", "dno", "dnw")
    def _():
        for z in range(2):
            flights["down_part", z].wait_recv()
        out2[2] = (keep[1, 1 - zl] + got[1, 1 - zl].astype(F32)).astype(BF)
        flights["down_far"] = links.mp(out2.at[2], got2.at[2], far)

    @task("lout", "dnS")
    def _():
        flights["down_far"].wait()
        lout[...] = (
            mid[pl.ds(pl.multiple_of(mp * 128, 128), 128), :]
            + keep[1, zl] + got[1, zl].astype(F32) + got2[2].astype(F32)
        ).astype(BF)
        leaving.append(load(lout, lout_out))

    def norm_mid_back(z):
        flights["gnm_far", z].wait()
        rows = block(z, False)
        unit, inv = normalize(mid[rows, :])
        g = out2[z].astype(F32) + got2[z].astype(F32)
        totals["gain"] = totals["gain"] + jnp.sum(g * unit, axis=0, keepdims=True) * jnp.where(zl == z, 1.0, 0.0)
        gmid = raw[GOUT, 2 * z + core].astype(F32) + norm_back(g, fgain[...], unit, inv)
        keep[0, z] = gmid
        gb[z, core] = gmid.astype(BF)
        flights["gb", z] = links.mp(gb.at[z, core], gb.at[z, core], part)
        if z == 1:
            s_ref[1:2, :] = totals["gain"]

    for z in range(2):
        task(f"gS{z}", "gnmw", *(["gS0"] if z else []))(functools.partial(gnm_sum, z))
        task(f"lnb{z}", f"gS{z}", *(["lnb0"] if z else []))(functools.partial(norm_mid_back, z))

    @task("xout", "lnb1", "squeeze")
    def _():
        for z in range(2):
            flights["gb", z].wait()
        gmix[...] = dg(wo[mine, :], gb[...].reshape(512, D), 1, 1)
        for half in range(2):
            cols = pl.ds(half * 512, 512)
            x_out[:, cols] = dg(mixg[mp], gb[:, :, :, cols].reshape(512, 512), 0, 0).astype(BF)
        begin("O")

    carried = {}

    def attend_back(h, a):
        base = BASE[a]
        rows = pl.ds(base, 512)
        grad = gmix[heads(h), :]
        if a == OLD:
            carried["inner"] = jnp.sum(grad * mixt[heads(h), :], axis=0, keepdims=True)
            carried["slope"] = jnp.zeros((8, 512), F32)
        inv = stat[12 + h * 3 + base // 512 : 13 + h * 3 + base // 512, :]
        scaled = (grad * inv).astype(BF)
        shift = inv * carried["inner"]
        tmp[...] = dg(kv[rows, pl.ds(256 + h * DH, DH)], scaled)
        gkv[rows, pl.ds(256 + h * DH, DH)] = dg(expo[h, rows, :], scaled, 1, 1).astype(BF)

        def score_grads(r, total):
            at = pl.ds(base + r, 64)
            gs = (expo[h, at, :].astype(F32) * (tmp[pl.ds(r, 64), :] - shift)).astype(BF)
            expo[h, at, :] = gs
            dist = (iota((64, 512), 1) - iota((64, 512), 0) + (1024 - base - r)).astype(F32)
            return total + fold(gs.astype(F32) * dist, jnp.add)

        carried["slope"] = loop(512, 64, score_grads, carried["slope"])
        gkv[rows, heads(h)] = (dg(expo[h, rows, :], query[:, heads(h)]) * SCALE).astype(BF)
        if a == SEG:
            gqt = dg(kv[:, heads(h)], expo[h], 0, 0)
            gq[:, heads(h)] = (gqt * SCALE).T.astype(BF)
            value = -jnp.sum(jnp.sum(carried["slope"], axis=0, keepdims=True), axis=1, keepdims=True)
            totals["slope"] = totals["slope"] + jnp.where(iota((1, D), 1) == mp * 2 + h, value, 0.0)

    before = ("xout", "f0", "f1")
    for h in range(2):
        for name, a in ((f"att{h}.0", OLD), (f"att{h}.1", MEM), (f"att{h}", SEG)):
            task(name, *before)(functools.partial(attend_back, h, a))
            before = (name,)

    def projections(b):
        feats = pl.ds(b * 256, 256)
        big = dg(normed[:, feats], gkv[...], 0, 0)
        small = dg(normed[1024:1536, feats], gq[...], 0, 0)
        t_ref[b, :, 0:512] = big.astype(BF)
        t_ref[b, :, 512:768] = small.astype(BF)
        terms = small[:, 0:128] * wkvq[feats, 512:640].astype(F32) + small[:, 128:256] * wkvq[feats, 640:768].astype(F32)
        for j in range(4):
            terms = terms + big[:, j * 128 : (j + 1) * 128] * wkvq[feats, j * 128 : (j + 1) * 128].astype(F32)
        s_ref[0:1, feats] = jnp.sum(terms.T, axis=0, keepdims=True) / again[:, feats]
        if b == 3:
            begin("T")
            s_ref[2:3, :] = totals["slope"]
            s_ref[3:8, :] = jnp.zeros((5, D), F32)
            s_ref[9:16, :] = jnp.zeros((7, D), F32)
            begin("S")

    for b in range(4):
        task(("t.0", "t.1", "t.2", "t")[b], "att1", *([("t.0", "t.1", "t.2")[b - 1]] if b else []))(functools.partial(projections, b))

    def seg_terms(z, other):
        rows = block(z, other)
        at = pl.ds(pl.multiple_of(BASE[SEG] + (2 * z + ((1 - core) if other else core)) * 128, 128), 128)
        return dg(gkv[at, :], wkvq[:, 0:512], 1, 1) + dg(gq[rows, :], wkvq[:, 512:768], 1, 1)

    @task("sego", "att1")
    def _():
        for z in range(2):
            flights["gnm_part", z].wait_send()
            out[0, z] = seg_terms(z, True).astype(BF)
            flights["seg_part", z] = links.mp(out.at[0, z], got.at[0, z], part)
            done.append(flights["seg_part", z])

    @task("segw", "att1")
    def _():
        for z in range(2):
            terms = seg_terms(z, False)
            for half in range(2):
                tmp2[(2 * z + half) * 128 : (2 * z + half + 1) * 128, :] = terms[:, half * 512 : (half + 1) * 512]

    @task("segS", "sego", "segw")
    def _():
        for z in range(2):
            flights["seg_part", z].wait_recv()
        for half in range(2):
            cols = pl.ds(half * 512, 512)
            at = pl.ds(pl.multiple_of((2 * (1 - zl) + half) * 128, 128), 128)
            out2[3, :, cols] = (tmp2[at, :] + got[0, 1 - zl, :, cols].astype(F32)).astype(BF)
        flights["seg_far"] = links.mp(out2.at[3], got2.at[3], far)

    @task("gin", "segS")
    def _():
        flights["seg_far"].wait()
        unit, inv = normalize(raw[SEG, mp].astype(F32))
        own = [tmp2[pl.ds(pl.multiple_of((2 * zl + half) * 128, 128), 128), :] for half in range(2)]
        total = jnp.concatenate(own, axis=1) + got[0, zl].astype(F32) + got2[3].astype(F32)
        gin[...] = keep[0, zl] + norm_back(total, again[...], unit, inv)
        leaving.append(load(gin, gin_out))

    for name in ORDER:
        if name in tasks:
            run, after = tasks[name]
            assert all(other in ran for other in after), name
            run()
        else:
            part_sum = sums[name[0]]
            assert part_sum.stage == int(name[1:]), name
            part_sum.advance()
            if part_sum.stage > part_sum.last:
                leaving.append(load(*results[name[0]]))
        ran.add(name)
    assert len(ran) == len(tasks) + sum(part_sum.last + 1 for part_sum in sums.values())
    for part_sum in sums.values():
        part_sum.finish()
    for cp in leaving:
        cp.wait()
    for cp in done:
        cp.wait_send()
    assert links.sends <= SENDS and links.recvs <= RECVS, (links.sends, links.recvs)


def layer(args):
    def out_shape(shape, dtype):
        return jax.ShapeDtypeStruct(shape, dtype)

    outs = (
        out_shape((128, D), BF), out_shape((48, D), BF), out_shape((128, D), F32), out_shape((1024, D), BF),
        out_shape((1024, D), BF), out_shape((768, D), BF), out_shape((256, D), BF), out_shape((4, 256, 768), BF),
        out_shape((16, D), F32),
    )
    v = pltpu.VMEM
    scratch = [
        v((4, 4, 128, D), BF), v((1536, D), BF), v((D, 768), BF), v((D, D), BF), v((D, D), BF), v((D, D), BF),
        v((3072, D), BF), v((1536, 512), BF), v((512, 256), BF), v((2, 1536, 512), BF), v((512, 512), F32),
        v((512, 512), F32), v((24, 512), F32), v((6, DH, 512), F32), v((256, 512), F32), v((4, 512, 256), BF),
        v((512, D), F32), v((512, D), BF), v((512, D), BF), v((512, D), BF),
        v((2, 2, 128, D), BF), v((2, 2, 128, D), BF), v((2, 2, 128, D), F32), v((4, 128, D), BF), v((4, 128, D), BF),
        v((2, 2, 128, D), BF), v((256, 512), F32), v((1536, 512), BF), v((512, 256), BF),
        v((CP, 3 * D), BF), v((CP, D), F32), v((CP, 512), BF), v((CP, 512), BF), v((CP, 512), BF), v((256, 512), F32),
        v((2, 96, D), BF), v((2, 96, D), BF), v((2, 96, D), BF),
        v((4, 256, 768), BF), v((4, STRIPS, 16, 128), BF), v((4, STRIPS, 16, 128), BF), v((7, 16, D), F32),
        v((D, D), BF), v((D, D), BF), v((768, D), BF), v((256, D), BF), v((4, 256, 768), BF), v((16, D), F32),
        v((128, D), BF), v((128, D), F32), v((48, D), BF), v((1, D), F32), v((1, D), F32), v((1, D), F32),
        pltpu.SemaphoreType.DMA((23,)), pltpu.SemaphoreType.REGULAR((6,)),
        pltpu.SemaphoreType.DMA((SENDS,)), pltpu.SemaphoreType.DMA((RECVS,)),
    ]
    return pl.pallas_call(
        layer_body,
        out_shape=outs,
        in_specs=[ANY] * 10 + [SMEM] * 3 + [ANY] * 3,
        out_specs=(ANY,) * 9,
        scratch_shapes=scratch,
        compiler_params=pltpu.CompilerParams(collective_id=0, has_side_effects=True, vmem_limit_bytes=62 << 20),
    )(*args)


def widen_body(lout, sqz, gin, down, up, sq, outp, t, s, *refs):
    (o_lout, o_sqz, o_gin, o_again, o_q, o_kv, o_out, o_slopes, o_fgain, o_up, o_ubias, o_down, o_sq) = refs[:13]
    tin, lin, kv_wide, q_wide, wide, b_lout, b_gin, b_s, b_sqz, r_again, r_fgain, r_ubias, r_slopes, sem_in, sem_out = refs[13:]
    loads = []

    def load(src, dst):
        cp = pltpu.make_async_copy(src, dst, sem_in.at[len(loads)])
        cp.start()
        loads.append(cp)
        return cp

    s_load = load(s, b_s)
    t_load = load(t, tin)
    pieces = []
    for src, dst, n in ((down, o_down, 4), (up, o_up, 4), (sq, o_sq, 3), (outp, o_out, 1)):
        for i in range(n):
            k = len(pieces)
            pieces.append((load(src.at[pl.ds(256 * i, 256)], lin.at[k]), dst.at[pl.ds(256 * i, 256)]))
    plain = [(load(lout, b_lout), b_lout, o_lout), (load(gin, b_gin), b_gin, o_gin)]
    sqz_load = load(sqz, b_sqz)
    stores = []

    def leave(src, dst):
        stores.append(pltpu.make_async_copy(src, dst, sem_out.at[len(stores)]))
        stores[-1].start()

    s_load.wait()
    for row, to, dst in ((0, r_again, o_again), (1, r_fgain, o_fgain), (8, r_ubias, o_ubias)):
        to[...] = b_s[row : row + 1, :]
        leave(to, dst)
    r_slopes[...] = b_s[2:3, 0:8]
    leave(r_slopes, o_slopes)
    t_load.wait()
    for b in range(4):
        for part in range(2):
            kv_wide[:, pl.ds(part * D + b * 256, 256)] = tin[b, :, part * 256 : part * 256 + 256].astype(F32)
        q_wide[:, pl.ds(b * 256, 256)] = tin[b, :, 512:768].astype(F32)
    leave(kv_wide, o_kv)
    leave(q_wide, o_q)
    for i, (cp, dst) in enumerate(pieces):
        cp.wait()
        wide[i] = lin[i].astype(F32)
        leave(wide.at[i], dst)
    sqz_load.wait()
    o_sqz[...] = b_sqz[0:43, :]
    for cp, src, dst in plain:
        cp.wait()
        leave(src, dst)
    for cp in stores:
        cp.wait()


def widen(args):
    def out_shape(shape, dtype):
        return jax.ShapeDtypeStruct(shape, dtype)

    outs = (
        out_shape((128, D), BF), out_shape((43, D), BF), out_shape((128, D), F32), out_shape((1, D), F32),
        out_shape((256, D), F32), out_shape((256, 2 * D), F32), out_shape((256, D), F32), out_shape((1, 8), F32),
        out_shape((1, D), F32), out_shape((D, D), F32), out_shape((1, D), F32), out_shape((D, D), F32),
        out_shape((768, D), F32),
    )
    v = pltpu.VMEM
    return pl.pallas_call(
        widen_body,
        out_shape=outs,
        in_specs=[ANY] * 9,
        out_specs=tuple(VMEM if i == 1 else ANY for i in range(13)),
        scratch_shapes=[
            v((4, 256, 768), BF), v((12, 256, D), BF), v((256, 2 * D), F32), v((256, D), F32), v((12, 256, D), F32),
            v((128, D), BF), v((128, D), F32), v((16, D), F32), v((48, D), BF),
            v((1, D), F32), v((1, D), F32), v((1, D), F32), v((1, 8), F32),
            pltpu.SemaphoreType.DMA((17,)), pltpu.SemaphoreType.DMA((20,)),
        ],
        compiler_params=pltpu.CompilerParams(vmem_limit_bytes=62 << 20),
    )(*args)


def per_device(
    layer_in, memory, squeezed_mem, memory_fill, squeezed_fill, grad_out, attn_gain, w_query, w_keyval,
    w_output, slopes, ffn_gain, w_up, up_bias, w_down, w_squeeze,
):
    done = layer((
        layer_in[0], memory[0], squeezed_mem[0], grad_out[0], w_query, w_keyval, w_output, w_up, w_down, w_squeeze,
        memory_fill, squeezed_fill, slopes, attn_gain[None], ffn_gain[None], up_bias[None],
    ))
    lout, sqz, gin, again, q, kv, out, slope, fgain, up, ubias, down, sq = widen(done)
    return (
        lout[None], sqz[None], gin[None], again[0], q, kv, out, slope[0], fgain[0], up, ubias[0], down, sq,
    )


def solution(mesh):
    rows = P("dp", "mp", None)
    in_specs = (
        rows, rows, rows, P("dp"), P("dp"), rows, P(), P(), P(), P(), P(), P(), P(None, "mp"), P("mp"), P("mp", None), P(),
    )
    out_specs = (
        rows, rows, rows, P(), P("mp", None), P("mp", None), P("mp", None), P(), P(), P(None, "mp"), P("mp"), P("mp", None), P("mp", None),
    )
    return jax.shard_map(per_device, mesh=mesh, in_specs=in_specs, out_specs=out_specs, check_vma=False)
```
